128 devices in a mesh: rep: 2 (over core), shard: 64 (over y, x, z).
Axes of the slice: x: 4, y: 4, z: 4, core: 2. Of those that a mesh axis runs over, the one named last changes fastest.
Arguments:
- table_rows: float32 [131072, 128], P('shard'), may hold values from -3 to 3
- accum: float32 [131072, 128], P('shard'), may hold values from 0.1 to 1
- hash_keys: int32 [131072], P('shard'), may hold values from 0 to 131071, as said below
- hash_place: int32 [131072], replicated, may hold values from 0 to 131071, as said below
- sample_ids: int32 [32768, 32], P(('rep', 'shard')), may hold values from 0 to 131071, as said below
- sample_grads: bfloat16 [32768, 1024], P(('rep', 'shard')), may hold values from -6 to 6
- req_ids: int32 [16384, 32], P(('rep', 'shard')), may hold values from 0 to 131071, as said below
- w_hidden: bfloat16 [1024, 1024], replicated, may hold values from -0.1875 to 0.1875
- b_hidden: float32 [1024], replicated, may hold values from -3 to 3
- w_score: bfloat16 [1024], replicated, may hold values from -0.1875 to 0.1875
Outputs:
- new_rows: float32 [131072, 128], P('shard')
- new_accum: float32 [131072, 128], P('shard')
- serving_rows: bfloat16 [131072, 128], P('shard')
- scores: float32 [16384], P(('rep', 'shard'))
The draws below stay inside these ranges and needn't reach their ends.
Inputs may be any that keep to these rules, and one draw needn't show every extreme that they name: `hash_keys`: A permutation of the keys; the trainer row p holds a key k with k // 2048 == (p % 2048) // 32. The inverse of hash_keys: hash_keys[hash_place[k]] == k. `sample_ids`: among one device's samples, at most 256 ids have a trainer row in one shard's block of 2048 rows, and this count is reached on every device. `req_ids`: among one device's requests, at most 128 ids lie in one block of 2048 consecutive keys, and this count is reached on every device.
All inputs are finite; a program needn't handle non-finite values.
Results may differ from the reference program's by a relative error of at most 0.0064.
Values may be sent and summed in bfloat16 or wider, within the bound.
No kernel may reach another device: no remote copies, remote signals or barrier semaphores. Data moves between devices by JAX's collectives and lax.ppermute only.
A program may use at most 128 MiB of HBM per device.

```python
import math
import jax
import jax.numpy as jnp
from jax import lax

E = 128
FIELDS = 8
IDS = 4
HID = 1024
ROWS_DEV = 2048
TRAIN_DEV = 256
REQ_DEV = 128
R = 131072
SAMPLES = 32768
REQS = 16384
N_REP = 2
N_SHARD = 64


def hash_tables(key):
    block_rows = ROWS_DEV // N_SHARD
    range_keys = jax.random.split(key, N_SHARD)
    orders = jax.vmap(lambda one_key: jax.random.permutation(one_key, ROWS_DEV))(range_keys)
    held = orders.reshape(N_SHARD, N_SHARD, block_rows) + (jnp.arange(N_SHARD, dtype=jnp.int32) * ROWS_DEV)[:, None, None]
    held = jnp.transpose(held, (1, 0, 2)).reshape(-1).astype(jnp.int32)
    places = jnp.zeros((R,), jnp.int32).at[held].set(jnp.arange(R, dtype=jnp.int32))
    return (held, places)


def owner_slots(key, slot_count, hottest):
    capacity = 2 * slot_count // N_SHARD
    first_key, second_key, third_key = jax.random.split(key, 3)
    own_hot = jax.random.randint(first_key, (), 0, N_SHARD)
    order = jax.random.permutation(second_key, N_SHARD * capacity).astype(jnp.int32)
    positions = jnp.arange(N_SHARD * capacity, dtype=jnp.int32)
    pool_owner = positions // capacity
    filled = (pool_owner == hottest) | (pool_owner == own_hot)
    ranking = jnp.where(filled, positions - N_SHARD * capacity, order)
    chosen = jnp.argsort(ranking, stable=True)[:slot_count]
    owners = pool_owner[chosen]
    shuffle = jax.random.permutation(third_key, slot_count)
    return owners[shuffle]


def draw_hash_keys(key, part):
    held, places = hash_tables(key)
    return held


def draw_hash_place(key, part):
    held, places = hash_tables(key)
    return places


def draw_sample_ids(key, part):
    held, places = hash_tables(key)
    key = jax.random.fold_in(key, 11)
    hottest = jax.random.randint(jax.random.fold_in(key, 1), (), 0, N_SHARD)
    slot_count = TRAIN_DEV * FIELDS * IDS
    device_keys = jax.random.split(jax.random.fold_in(key, 2), N_REP * N_SHARD)

    def one_device(dev_key):
        owner_key, local_key = jax.random.split(dev_key)
        owners = owner_slots(owner_key, slot_count, hottest)
        local_rows = jax.random.randint(local_key, (slot_count,), 0, ROWS_DEV)
        return held[owners * ROWS_DEV + local_rows]
    drawn = jax.vmap(one_device)(device_keys)
    return drawn.reshape(SAMPLES, FIELDS * IDS).astype(jnp.int32)


def draw_req_ids(key, part):
    key = jax.random.fold_in(key, 23)
    hottest = jax.random.randint(jax.random.fold_in(key, 1), (), 0, N_SHARD)
    slot_count = REQ_DEV * FIELDS * IDS
    device_keys = jax.random.split(jax.random.fold_in(key, 2), N_REP * N_SHARD)

    def one_device(dev_key):
        owner_key, local_key = jax.random.split(dev_key)
        owners = owner_slots(owner_key, slot_count, hottest)
        local_rows = jax.random.randint(local_key, (slot_count,), 0, ROWS_DEV)
        return owners * ROWS_DEV + local_rows
    drawn = jax.vmap(one_device)(device_keys)
    return drawn.reshape(REQS, FIELDS * IDS).astype(jnp.int32)


def level_of(rng, dims, cuts, low, largest):
    factor_of, own = 1.0, jax.random.fold_in(rng, 6)
    for axis_at, shards_of in cuts:
        draws = jnp.exp(jax.random.uniform(jax.random.fold_in(own, axis_at), (shards_of,), jnp.float32, low / len(cuts), largest / len(cuts)))
        factor_of = factor_of * jnp.repeat(draws, dims[axis_at] // shards_of).reshape([-1 if axis == axis_at else 1 for axis in range(len(dims))])
    return factor_of


def gaussian(own_key, extent, spread, reach, shards=(), kind=jnp.bfloat16):
    factor_of = level_of(own_key, extent, shards, -0.22, 0.18) if shards else 1.0
    values = jax.random.normal(own_key, extent, jnp.float32) * spread * factor_of
    return jnp.minimum(jnp.maximum(values, -reach), reach).astype(kind)


def setup_inputs(seed: int = 0) -> dict:
    streams_of = jax.random.split(jax.random.key(seed), 11)
    table_rows = gaussian(streams_of[0], (R, E), 0.5, 3.0, ((0, 64),), jnp.float32)
    accum = jnp.clip(jnp.exp(math.log(1.0) - 2.3025851 * jax.random.uniform(streams_of[1], (R, E), jnp.float32) ** level_of(streams_of[1], (R, E), ((0, 64),), -0.2, 0.2)), 0.1, 1.0)
    hash_keys = draw_hash_keys(jax.random.fold_in(streams_of[10], 71), 0)
    hash_place = draw_hash_place(jax.random.fold_in(streams_of[10], 71), 0)
    sample_ids = draw_sample_ids(jax.random.fold_in(streams_of[10], 71), 0)
    sample_grads = gaussian(streams_of[5], (SAMPLES, FIELDS * E), 1.0, 6.0, ((0, 128),))
    req_ids = draw_req_ids(jax.random.fold_in(streams_of[10], 71), 0)
    w_hidden = gaussian(streams_of[7], (FIELDS * E, HID), (FIELDS * E) ** -0.5, 0.1875)
    b_hidden = gaussian(streams_of[8], (HID,), 0.5, 3.0, (), jnp.float32)
    w_score = gaussian(streams_of[9], (HID,), HID ** -0.5, 0.1875)
    return dict(table_rows=table_rows, accum=accum, hash_keys=hash_keys, hash_place=hash_place, sample_ids=sample_ids, sample_grads=sample_grads, req_ids=req_ids, w_hidden=w_hidden, b_hidden=b_hidden, w_score=w_score)


def reference(table_rows, accum, hash_keys, hash_place, sample_ids, sample_grads, req_ids, w_hidden, b_hidden, w_score):
    gradient = jnp.zeros((R, E), jnp.float32)
    for field in range(FIELDS):
        field_grad = sample_grads[:, field * E:(field + 1) * E].astype(jnp.float32)
        for which in range(IDS):
            target = hash_place[sample_ids[:, field * IDS + which]]
            gradient = gradient + jax.ops.segment_sum(field_grad, target, num_segments=R)
    new_accum = accum + gradient * gradient
    new_rows = table_rows - 0.1 * gradient * lax.rsqrt(new_accum)
    serving_rows = jnp.zeros((R, E), jnp.bfloat16).at[hash_keys].set(new_rows.astype(jnp.bfloat16))
    pieces = []
    for field in range(FIELDS):
        summed = jnp.zeros((REQS, E), jnp.float32)
        for which in range(IDS):
            summed = summed + serving_rows[req_ids[:, field * IDS + which]].astype(jnp.float32)
        pieces.append(summed)
    pooled = jnp.concatenate(pieces, axis=1).astype(jnp.bfloat16)
    hidden = jax.nn.relu(jnp.dot(pooled, w_hidden, preferred_element_type=jnp.float32) + b_hidden).astype(jnp.bfloat16)
    scores = jnp.dot(hidden, w_score, preferred_element_type=jnp.float32)
    return (new_rows, new_accum, serving_rows, scores)
```

```python
import functools

import jax
import jax.numpy as jnp
from jax import lax
from jax.experimental import pallas as pl
from jax.experimental.pallas import tpu as pltpu
from jax.sharding import PartitionSpec as P

F32, BF16, I32 = jnp.float32, jnp.bfloat16, jnp.int32
NT = (((1,), (1,)), ((), ()))
VMEM_LIMIT = 56 * 2**20
EXTRA = 16


def params():
    return pltpu.CompilerParams(vmem_limit_bytes=VMEM_LIMIT)


def iota(shape, axis, dtype=I32):
    return lax.broadcasted_iota(I32, shape, axis).astype(dtype)


def dot(a, b):
    return jnp.dot(a, b, preferred_element_type=F32)


def dot_nt(a, b):
    return lax.dot_general(a, b, NT, preferred_element_type=F32)


def ones_where(mask):
    return jnp.where(mask, 1.0, 0.0).astype(BF16)


def rank_chunk(owner, base, shards, tri, ones):
    count = owner.shape[1]
    own = jnp.where(iota((shards, count), 0, F32) == owner, 1.0, 0.0)
    own_b = own.astype(BF16)
    before = dot(own_b, tri) + jnp.concatenate([base] * (count // 128), axis=1)
    return own, jnp.sum(own * before, axis=0, keepdims=True), base + dot(own_b, ones)


def index_kernel(shards, rows_dev, ids_ref, place_ref, req_ref, col_ref, extra_ref, mslot_ref, ex):
    block = rows_dev // shards
    shift = rows_dev.bit_length() - 1
    place = place_ref[...]
    table = jnp.concatenate(
        [(place >> shift).astype(F32).T, (place & (block - 1)).astype(F32).T], axis=0
    ).astype(BF16)
    highs = place_ref.shape[0]
    width = ids_ref.shape[1]
    tri = ones_where(iota((width, width), 0) < iota((width, width), 1))
    ones = jnp.ones((width, 128), BF16)
    lane = iota((1, width), 1)

    def train(c, carry):
        base, col, row = carry
        ids = ids_ref[pl.ds(c, 1), :]
        hot = ones_where(iota((highs, width), 0) == (ids >> 7))
        both = dot(table, hot)
        mask = iota((128, width), 0) == (ids & 127)
        owner = jnp.sum(jnp.where(mask, both[:128], 0.0), axis=0, keepdims=True)
        place_low = jnp.sum(jnp.where(mask, both[128:], 0.0), axis=0, keepdims=True)
        own, rank, base = rank_chunk(owner, base, shards, tri, ones)
        at = ones_where(iota((width, width), 0, F32) == rank)
        field = (c // 4 + 1).astype(F32)
        source = jnp.concatenate([own * lane.astype(F32), own * field], axis=0).astype(BF16)
        target = jnp.concatenate([own * (ids >> shift).astype(F32), own * place_low], axis=0)
        col = col + dot_nt(at, source)
        row = row + dot_nt(target.astype(BF16), at)
        return base, col, row

    base = jnp.zeros((shards, 128), F32)
    unused, col, row = lax.fori_loop(
        0,
        ids_ref.shape[0],
        train,
        (base, jnp.zeros((width, 2 * shards), F32), jnp.zeros((2 * shards, width), F32)),
    )
    col_ref[...] = col

    def serve(c, carry):
        base, row = carry
        ids = req_ref[pl.ds(c, 1), :]
        local = ids & (rows_dev - 1)
        own, rank, base = rank_chunk((ids >> shift).astype(F32), base, shards, tri, ones)
        at = ones_where(iota((128, width), 0, F32) == rank)
        digits = [
            own * (local >> 5).astype(F32),
            own * (local & 31).astype(F32),
            own * (lane & 127).astype(F32),
            own * (c // 2 + 1).astype(F32),
        ]
        row = row + dot_nt(jnp.concatenate(digits, axis=0).astype(BF16), at)
        return base, row

    unused, asked = lax.fori_loop(
        0, req_ref.shape[0], serve, (base, jnp.zeros((4 * shards, 128), F32))
    )
    ex[...] = jnp.zeros_like(ex)
    parts = [
        row[:shards, :128],
        row[:shards, 128:],
        row[shards:, :128],
        row[shards:, 128:],
        asked[:shards],
        asked[shards : 2 * shards],
    ]
    for kind, part in enumerate(parts):
        ex[pl.ds(kind, shards, stride=EXTRA), :] = part
    extra_ref[...] = ex[...].astype(BF16)
    query = asked[2 * shards : 3 * shards] + (asked[3 * shards :] - 1.0) * 128.0
    mslot_ref[...] = query.astype(I32)


def build_kernel(group, shards, col_ref, grads_ref, extra_ref, out_ref):
    slots = col_ref.shape[0]
    samples = grads_ref.shape[0]
    fields = grads_ref.shape[1] // 128

    def one(b, unused):
        owner = pl.program_id(0) * group + b
        turned = pltpu.roll(col_ref[...], lax.rem(2 * shards - owner, 2 * shards), 1)
        source = turned[:, 0:1]
        field = jnp.broadcast_to(turned[:, shards : shards + 1], (slots, 128))
        hot = ones_where(iota((slots, samples), 1, F32) == source)
        rows = dot(hot, grads_ref[...])
        picked = jnp.zeros((slots, 128), F32)
        for f in range(fields):
            picked = jnp.where(field == f + 1.0, rows[:, f * 128 : (f + 1) * 128], picked)
        out_ref[b, 0:slots, :] = picked.astype(BF16)
        out_ref[b, slots : slots + EXTRA, :] = extra_ref[pl.ds(b * EXTRA, EXTRA), :]
        return unused

    lax.fori_loop(0, group, one, 0)


def sum_kernel(group, got_ref, extra_ref, out_ref, scr, hi_scr, lo_scr, total):
    shards = extra_ref.shape[0]
    slots = got_ref.shape[1] - EXTRA
    step = pl.program_id(0)

    @pl.when(step == 0)
    def _():
        scr[...] = extra_ref[...].astype(F32).reshape(scr.shape)
        lows = []
        for half in range(2):
            ranges = scr[pl.ds(half, shards, stride=EXTRA), :].astype(I32)
            within = scr[pl.ds(2 + half, shards, stride=EXTRA), :].astype(I32)
            hi_scr[half] = (ranges & 15) * 32 + within
            lows.append((ranges >> 4).astype(F32))
        lo_scr[...] = jnp.concatenate(lows, axis=0).T
        total[...] = jnp.zeros_like(total)

    highs, values = [], []
    for k in range(group):
        src = step * group + k
        hi = jnp.concatenate([hi_scr[0, pl.ds(src, 1), :], hi_scr[1, pl.ds(src, 1), :]], axis=1)
        highs.append(ones_where(iota((512, slots), 0) == hi))
        turned = pltpu.roll(lo_scr[...], lax.rem(2 * shards - src, 2 * shards), 1)
        low = jnp.concatenate([turned[:, 0:1], turned[:, shards : shards + 1]], axis=0)
        low = jnp.broadcast_to(low, (slots, 128))
        rows = got_ref[k, 0:slots, :]
        values.append(
            jnp.concatenate([rows * ones_where(low == float(q)) for q in range(4)], axis=1)
        )
    total[...] += dot(jnp.concatenate(highs, axis=1), jnp.concatenate(values, axis=0))

    @pl.when(step == pl.num_programs(0) - 1)
    def _():
        for q in range(4):
            out_ref[q * 512 : (q + 1) * 512, :] = total[:, q * 128 : (q + 1) * 128]


def take_rows(low, high, wide):
    count = low.shape[0]
    rows = dot(ones_where(iota((count, 512), 1, F32) == high), wide)
    low = jnp.broadcast_to(low, (count, 128))
    picked = rows[:, 0:128]
    for q in range(1, 4):
        picked = jnp.where(low == float(q), rows[:, q * 128 : (q + 1) * 128], picked)
    return picked.astype(BF16)


def widen(rows):
    return jnp.concatenate([rows[q * 512 : (q + 1) * 512] for q in range(4)], axis=1)


def serve_kernel(group, moved_ref, place_ref, extra_ref, serving_ref, found_ref, scr, wide, low_scr, high_scr):
    shards = extra_ref.shape[0]
    step = pl.program_id(0)

    @pl.when(step == 0)
    def _():
        place = place_ref[...]
        owner = place >> 11
        low = (owner >> 4).astype(F32).T
        high = ((owner & 15) * 32 + (place & 31)).astype(F32).T
        moved = widen(moved_ref[...])
        for b in range(place.shape[0]):
            serving_ref[b * 128 : (b + 1) * 128, :] = take_rows(
                low[:, b : b + 1], high[:, b : b + 1], moved
            )
        wide[...] = widen(serving_ref[...])
        scr[...] = extra_ref[...].astype(F32).reshape(scr.shape)
        first = scr[pl.ds(4, shards, stride=EXTRA), :].astype(I32)
        second = scr[pl.ds(5, shards, stride=EXTRA), :].astype(I32)
        zero = jnp.zeros((128 - shards, 128), F32)
        low_scr[...] = jnp.concatenate([(first >> 4).astype(F32), zero], axis=0).T
        high_scr[...] = jnp.concatenate(
            [((first & 15) * 32 + second).astype(F32), zero], axis=0
        ).T

    turn = lax.rem(128 - step * group, 128)
    low = pltpu.roll(low_scr[...], turn, 1)
    high = pltpu.roll(high_scr[...], turn, 1)
    for b in range(group):
        found_ref[b] = take_rows(low[:, b : b + 1], high[:, b : b + 1], wide[...])


def rank_kernel(group, ret_ref, mslot_ref, w_ref, b_ref, score_ref, out_ref, total):
    step = pl.program_id(0)
    queries = total.shape[0]

    @pl.when(step == 0)
    def _():
        total[...] = jnp.zeros_like(total)

    slots = ret_ref.shape[1]
    hots = [
        ones_where(iota((queries, slots), 0) == mslot_ref[pl.ds(step * group + b, 1), :])
        for b in range(group)
    ]
    total[...] += dot(jnp.concatenate(hots, axis=1), ret_ref[...].reshape(group * slots, 128))

    @pl.when(step == pl.num_programs(0) - 1)
    def _():
        rows = out_ref.shape[1]
        pooled = jnp.concatenate(
            [total[f * rows : (f + 1) * rows, :] for f in range(queries // rows)], axis=1
        ).astype(BF16)
        hidden = jnp.maximum(dot(pooled, w_ref[...]) + b_ref[...], 0.0).astype(BF16)
        out_ref[...] = dot_nt(score_ref[...], hidden)


def adagrad_step(weights, history, gradient):
    updated = history + gradient * gradient
    return (weights - 0.1 * gradient * lax.rsqrt(updated), updated)


def whole(shape):
    return pl.BlockSpec(shape, lambda *step: (0,) * len(shape))


def on_device(
    table_rows,
    accum,
    hash_keys,
    hash_place,
    sample_ids,
    sample_grads,
    req_ids,
    w_hidden,
    b_hidden,
    w_score,
):
    rows_dev, row_width = table_rows.shape
    shards = lax.axis_size("shard")
    samples, id_columns = sample_ids.shape
    requests = req_ids.shape[0]
    slots = 2 * samples * id_columns // shards
    req_slots = 2 * requests * id_columns // shards
    fields = sample_grads.shape[1] // row_width
    hidden_width = w_hidden.shape[1]
    places = hash_place.reshape(-1, 128)
    shape = jax.ShapeDtypeStruct

    col, extra, mslot = pl.pallas_call(
        functools.partial(index_kernel, shards, rows_dev),
        out_shape=(
            shape((slots, 2 * shards), F32),
            shape((shards * EXTRA, 128), BF16),
            shape((shards, req_slots), I32),
        ),
        scratch_shapes=[pltpu.VMEM((shards * EXTRA, 128), F32)],
        compiler_params=params(),
        name="index",
    )(sample_ids.T, places, req_ids.T.reshape(-1, 2 * requests))

    group = 8
    sent = pl.pallas_call(
        functools.partial(build_kernel, group, shards),
        grid=(shards // group,),
        in_specs=[
            whole((slots, 2 * shards)),
            whole(sample_grads.shape),
            pl.BlockSpec((group * EXTRA, 128), lambda g: (g, 0)),
        ],
        out_specs=pl.BlockSpec((group, slots + EXTRA, row_width), lambda g: (g, 0, 0)),
        out_shape=shape((shards, slots + EXTRA, row_width), BF16),
        compiler_params=params(),
        name="build",
    )(col, sample_grads, extra)
    got = lax.all_to_all(sent, "shard", split_axis=0, concat_axis=0, tiled=True)

    group = 4
    extra_spec = pl.BlockSpec((shards, EXTRA, row_width), lambda g: (0, slots // EXTRA, 0))
    partial_sum = pl.pallas_call(
        functools.partial(sum_kernel, group),
        grid=(shards // group,),
        in_specs=[
            pl.BlockSpec((group, slots + EXTRA, row_width), lambda g: (g, 0, 0)),
            extra_spec,
        ],
        out_specs=whole((rows_dev, row_width)),
        out_shape=shape((rows_dev, row_width), F32),
        scratch_shapes=[
            pltpu.VMEM((shards * EXTRA, 128), F32),
            pltpu.VMEM((2, shards, 128), I32),
            pltpu.VMEM((128, 128), F32),
            pltpu.VMEM((512, 512), F32),
        ],
        compiler_params=params(),
        name="gradient_sum",
    )(got, got)
    other = lax.ppermute(partial_sum, "rep", [(0, 1), (1, 0)])
    new_rows, new_accum = adagrad_step(table_rows, accum, partial_sum + other)
    moved = lax.all_to_all(
        new_rows.astype(BF16).reshape(shards, rows_dev // shards, row_width),
        "shard",
        split_axis=0,
        concat_axis=0,
        tiled=True,
    ).reshape(rows_dev, row_width)

    place_rows = rows_dev // 128
    own_places = lax.dynamic_slice_in_dim(
        places, lax.axis_index("shard") * place_rows, place_rows, axis=0
    )
    group = 8
    serving_rows, found = pl.pallas_call(
        functools.partial(serve_kernel, group),
        grid=(shards // group,),
        in_specs=[whole(moved.shape), whole((place_rows, 128)), extra_spec],
        out_specs=(
            whole((rows_dev, row_width)),
            pl.BlockSpec((group, req_slots, row_width), lambda g: (g, 0, 0)),
        ),
        out_shape=(
            shape((rows_dev, row_width), BF16),
            shape((shards, req_slots, row_width), BF16),
        ),
        scratch_shapes=[
            pltpu.VMEM((shards * EXTRA, 128), F32),
            pltpu.VMEM((512, 512), BF16),
            pltpu.VMEM((128, 128), F32),
            pltpu.VMEM((128, 128), F32),
        ],
        compiler_params=params(),
        name="serve",
    )(moved, own_places, got)
    returned = lax.all_to_all(found, "shard", split_axis=0, concat_axis=0, tiled=True)

    scores = pl.pallas_call(
        functools.partial(rank_kernel, group),
        grid=(shards // group,),
        in_specs=[
            pl.BlockSpec((group, req_slots, row_width), lambda g: (g, 0, 0)),
            whole((shards, req_slots)),
            whole(w_hidden.shape),
            whole((1, hidden_width)),
            whole((1, hidden_width)),
        ],
        out_specs=whole((1, requests)),
        out_shape=shape((1, requests), F32),
        scratch_shapes=[pltpu.VMEM((requests * fields, row_width), F32)],
        compiler_params=params(),
        name="pool_rank",
    )(returned, mslot, w_hidden, b_hidden.reshape(1, -1), w_score.reshape(1, -1))
    return (new_rows, new_accum, serving_rows, scores.reshape(requests))


def solution(mesh):
    return jax.shard_map(
        on_device,
        mesh=mesh,
        in_specs=(
            P("shard", None),
            P("shard", None),
            P("shard"),
            P(),
            P(("rep", "shard"), None),
            P(("rep", "shard"), None),
            P(("rep", "shard"), None),
            P(),
            P(),
            P(),
        ),
        out_specs=(P("shard", None), P("shard", None), P("shard", None), P(("rep", "shard"))),
        check_vma=False,
    )
```

```python
import functools

import jax
import jax.numpy as jnp
from jax import lax
from jax.experimental import pallas as pl
from jax.experimental.pallas import tpu as pltpu
from jax.sharding import PartitionSpec as P

F32, BF16, I32 = jnp.float32, jnp.bfloat16, jnp.int32
NT = (((1,), (1,)), ((), ()))
VMEM_LIMIT = 60 * 2**20
EXTRA = 16
LANES = 128


def iota(shape, axis, dtype=I32):
    return lax.broadcasted_iota(I32, shape, axis).astype(dtype)


def dot(a, b):
    return jnp.dot(a, b, preferred_element_type=F32)


def dot_nt(a, b):
    return lax.dot_general(a, b, NT, preferred_element_type=F32)


def ones_where(mask):
    return jnp.where(mask, 1.0, 0.0).astype(BF16)


def lanes_of(ref, first, count):
    return jnp.concatenate([ref[pl.ds(first + k, 1), :] for k in range(count)], axis=1)


def rank_ids(owner, base, shards, tri, ones):
    width = tri.shape[0]
    chunks = owner.shape[1] // width
    own = jnp.where(iota((shards, owner.shape[1]), 0, F32) == owner, 1.0, 0.0)
    stacked = jnp.concatenate(
        [own[:, k * width : (k + 1) * width] for k in range(chunks)], axis=0
    ).astype(BF16)
    before = dot(stacked, tri)
    totals = dot(stacked, ones)
    ranks = []
    for k in range(chunks):
        rows = slice(k * shards, (k + 1) * shards)
        at = before[rows] + jnp.concatenate([base] * (width // LANES), axis=1)
        ranks.append(jnp.sum(own[:, k * width : (k + 1) * width] * at, axis=0, keepdims=True))
        base = base + totals[rows]
    return own, jnp.concatenate(ranks, axis=1), base


def strict_upper(width):
    return ones_where(iota((width, width), 0) < iota((width, width), 1))


def pack_places(place, shift, block):
    last = place & (block - 1)
    scale = (1 << (last & 15)).astype(F32) * jnp.where(last >= 16, 65536.0, 1.0)
    packed = ((place >> shift) + 64).astype(F32) * scale
    half = place.shape[0] // 2
    return jnp.concatenate([packed[:half].T, packed[half:].T], axis=0).astype(BF16)


def look_up(table, ids):
    count = ids.shape[1]
    lows, lines = table.shape
    line = ids >> 7
    hot = ones_where(iota((lines, count), 0) == (line & (lines - 1)))
    low = (ids & 127) + jnp.where(line >= lines, LANES, 0)
    found = jnp.where(iota((lows, count), 0) == low, dot(table, hot), 0.0)
    value = jnp.sum(found, axis=0, keepdims=True)
    last = jnp.zeros_like(value)
    for bits in (16, 8, 4, 2, 1):
        big = value >= 64.0 * 2.0**bits
        value = jnp.where(big, value * 2.0**-bits, value)
        last = last + jnp.where(big, float(bits), 0.0)
    return value - 64.0, last


def index_kernel(
    shards, rows_dev, per_field, groups,
    ids_ref, place_ref, col_ref, off_ref, extra_ref, table, ex, own_scr, rank_scr, mark, off_scr,
):
    shift = rows_dev.bit_length() - 1
    width = ids_ref.shape[1]
    count = per_field * width
    fields = ids_ref.shape[0] // per_field
    span = fields // groups
    table[...] = pack_places(place_ref[...], shift, rows_dev // shards)
    tri = strict_upper(width)
    ones = jnp.ones((width, LANES), BF16)

    def field_step(field, carry):
        base, row = carry
        ids = lanes_of(ids_ref, field * per_field, per_field)
        owner, last = look_up(table[...], ids)
        mark[pl.ds(field * shards, shards), :] = base
        own, rank, base = rank_ids(owner, base, shards, tri, ones)
        own_scr[pl.ds(field, 1), :] = owner
        rank_scr[pl.ds(field, 1), :] = rank
        at = ones_where(iota((width, count), 0, F32) == rank)
        target = jnp.concatenate([own * (ids >> shift).astype(F32), own * last], axis=0)
        row = row + dot_nt(target.astype(BF16), at)
        return base, row

    base, row = lax.fori_loop(
        0,
        fields,
        field_step,
        (jnp.zeros((shards, LANES), F32), jnp.zeros((2 * shards, width), F32)),
    )
    mark[fields * shards :, :] = base
    ex[...] = jnp.zeros_like(ex)
    for kind in range(2):
        for half in range(2):
            ex[pl.ds(2 * kind + half, shards, stride=EXTRA), :] = row[
                kind * shards : (kind + 1) * shards, half * LANES : (half + 1) * LANES
            ]
    extra_ref[...] = ex[...].astype(BF16)

    earlier = ones_where(iota((shards, shards), 1) < iota((shards, shards), 0))
    lane = iota((shards, LANES), 1)
    table_off = jnp.zeros((shards, LANES), F32)
    for g in range(groups):
        first = mark[g * span * shards : (g * span + 1) * shards, :]
        after = mark[(g + 1) * span * shards : ((g + 1) * span + 1) * shards, :]
        off = dot(earlier, (after - first).astype(BF16)) - first
        off_scr[g * shards : (g + 1) * shards, :] = off
        table_off = jnp.where(lane == g, off, table_off)
        table_off = jnp.where(lane == groups + g, after, table_off)
    off_ref[...] = table_off.astype(I32)

    total = span * count
    blocks = total // LANES
    at = iota((1, total), 1)
    sample = (at & (width - 1)).astype(F32)
    field = (at // count).astype(F32)

    def group_step(g, unused):
        owner = lanes_of(own_scr, g * span, span)
        off = off_scr[pl.ds(g * shards, shards), :]
        shifts = jnp.where(
            iota((shards, total), 0, F32) == owner,
            jnp.concatenate([off] * blocks, axis=1),
            0.0,
        )
        pos = lanes_of(rank_scr, g * span, span) + jnp.sum(shifts, axis=0, keepdims=True)
        pos = pos.astype(I32)
        block = iota((blocks, total), 0) == (pos >> 7)
        source = jnp.concatenate(
            [jnp.where(block, sample, 0.0), jnp.where(block, field, 0.0)], axis=0
        ).astype(BF16)
        col_ref[g] = dot_nt(ones_where(iota((LANES, total), 0) == (pos & 127)), source)
        return unused

    lax.fori_loop(0, groups, group_step, 0)


def request_kernel(shards, rows_dev, req_ref, place_ref, out_ref, mrow_ref, mcol_ref, table, ex):
    shift = rows_dev.bit_length() - 1
    width = req_ref.shape[1]
    rows = req_ref.shape[0]
    batch = 4
    count = batch * width
    table[...] = pack_places(place_ref[...], shift, rows_dev // shards)
    tri = strict_upper(width)
    ones = jnp.ones((width, LANES), BF16)
    lane = iota((1, count), 1)

    def step(c, carry):
        base, row, col = carry
        ids = lanes_of(req_ref, c * batch, batch)
        owner, last = look_up(table[...], ids)
        own, rank, base = rank_ids((ids >> shift).astype(F32), base, shards, tri, ones)
        at = ones_where(iota((LANES, count), 0, F32) == rank)
        field = c * (batch // 2) + lane // (2 * width)
        query = (own * (lane & (LANES - 1)).astype(F32)).astype(BF16)
        number = (own * (field + 1).astype(F32)).astype(BF16)
        high = (own * owner).astype(BF16)
        low = (own * last).astype(BF16)
        row = row + dot_nt(jnp.concatenate([high, low, query, number], axis=0), at)
        col = col + dot_nt(at, jnp.concatenate([number, number], axis=0))
        return base, row, col

    unused, row, col = lax.fori_loop(
        0,
        rows // batch,
        step,
        (
            jnp.zeros((shards, LANES), F32),
            jnp.zeros((4 * shards, LANES), F32),
            jnp.zeros((LANES, 2 * shards), F32),
        ),
    )
    ex[...] = jnp.zeros_like(ex)
    for kind in range(2):
        ex[pl.ds(kind, shards, stride=EXTRA), :] = row[kind * shards : (kind + 1) * shards]
    out_ref[...] = ex[...].astype(BF16)
    field = row[3 * shards :].astype(I32) - 1
    mrow_ref[...] = jnp.where(
        field < 0, -1, (field & 3) * LANES + row[2 * shards : 3 * shards].astype(I32)
    )
    mcol_ref[...] = jnp.where(col > 4.0, 1.0, 0.0)


def build_kernel(group, shards, off_ref, col_ref, grads_ref, extra_ref, out_ref, rows_scr):
    slots = out_ref.shape[1] - EXTRA
    samples = grads_ref.shape[0]
    groups = col_ref.shape[0]
    blocks = col_ref.shape[2] // 2
    total = blocks * LANES
    span = grads_ref.shape[1] // groups
    step = pl.program_id(0)

    @pl.when(step == 0)
    def _():
        def sort_group(g, unused):
            col = col_ref[g]
            hots = [
                ones_where(iota((LANES, samples), 1, F32) == col[:, b : b + 1])
                for b in range(blocks)
            ]
            part = grads_ref[:, pl.ds(pl.multiple_of(g * span, span), span)]
            rows = dot(jnp.concatenate(hots, axis=0), part)
            field = jnp.concatenate(
                [
                    jnp.broadcast_to(col[:, blocks + b : blocks + b + 1], (LANES, LANES))
                    for b in range(blocks)
                ],
                axis=0,
            )
            picked = rows[:, :LANES]
            for q in range(1, span // LANES):
                picked = jnp.where(field == float(q), rows[:, q * LANES : (q + 1) * LANES], picked)
            rows_scr[g, slots : slots + total, :] = picked
            return unused

        lax.fori_loop(0, groups, sort_group, 0)

    at = iota((slots, LANES), 0)

    def one(b, unused):
        owner = step * group + b
        picked = rows_scr[0, pl.ds(slots + off_ref[owner, 0], slots), :]
        for g in range(1, groups):
            start = off_ref[owner, groups + g - 1]
            rows = rows_scr[g, pl.ds(slots + off_ref[owner, g], slots), :]
            picked = jnp.where(at >= start, rows, picked)
        picked = jnp.where(at >= off_ref[owner, 2 * groups - 1], 0.0, picked)
        out_ref[b, 0:slots, :] = picked.astype(BF16)
        out_ref[b, slots : slots + EXTRA, :] = extra_ref[pl.ds(b * EXTRA, EXTRA), :]
        return unused

    lax.fori_loop(0, group, one, 0, unroll=4)


def sum_kernel(group, got_ref, extra_ref, unused_ref, out_ref, scr, hi_scr, lo_scr, total):
    shards = extra_ref.shape[0]
    slots = got_ref.shape[1] - EXTRA
    step = pl.program_id(0)

    @pl.when(step == 0)
    def _():
        scr[...] = extra_ref[...].astype(F32).reshape(scr.shape)
        lows = []
        for half in range(2):
            ranges = scr[pl.ds(half, shards, stride=EXTRA), :].astype(I32)
            within = scr[pl.ds(2 + half, shards, stride=EXTRA), :].astype(I32)
            hi_scr[half] = (ranges & 15) * 32 + within
            lows.append((ranges >> 4).astype(F32))
        lo_scr[...] = jnp.concatenate(lows, axis=0).T
        total[...] = jnp.zeros_like(total)

    turned = pltpu.roll(lo_scr[...], lax.rem(2 * shards - step * group, 2 * shards), 1)
    highs, values = [], []
    for k in range(group):
        for half in range(2):
            hi = hi_scr[half, pl.ds(step * group + k, 1), :]
            highs.append(ones_where(iota((512, LANES), 0) == hi))
            low = jnp.broadcast_to(
                turned[:, half * shards + k : half * shards + k + 1], (LANES, LANES)
            )
            rows = got_ref[k, half * LANES : (half + 1) * LANES, :]
            values.append(
                jnp.concatenate([rows * ones_where(low == float(q)) for q in range(4)], axis=1)
            )
    total[...] += dot(jnp.concatenate(highs, axis=1), jnp.concatenate(values, axis=0))

    @pl.when(step == pl.num_programs(0) - 1)
    def _():
        for q in range(4):
            out_ref[q * 512 : (q + 1) * 512, :] = total[:, q * LANES : (q + 1) * LANES]


def adagrad_kernel(table_ref, accum_ref, one_ref, two_ref, extra_ref, rows_ref, new_accum_ref, sent_ref):
    gradient = one_ref[...] + two_ref[...]
    updated = accum_ref[...] + gradient * gradient
    rows = table_ref[...] - 0.1 * gradient * lax.rsqrt(updated)
    new_accum_ref[...] = updated
    rows_ref[...] = rows
    block = sent_ref.shape[1] - EXTRA
    group = sent_ref.shape[0]
    sent_ref[:, :block, :] = rows.astype(BF16).reshape(group, block, LANES)
    sent_ref[:, block:, :] = extra_ref[...].reshape(group, EXTRA, LANES)


def widen(moved_ref):
    block = moved_ref.shape[1] - EXTRA
    quarter = moved_ref.shape[0] // 4
    return jnp.concatenate(
        [
            moved_ref[q * quarter : (q + 1) * quarter, :block, :].reshape(quarter * block, LANES)
            for q in range(4)
        ],
        axis=1,
    )


def pick_rows(count, high, low, wide):
    hots = [ones_where(iota((LANES, 512), 1, F32) == high[:, b : b + 1]) for b in range(count)]
    rows = dot(jnp.concatenate(hots, axis=0), wide)
    lows = jnp.concatenate(
        [jnp.broadcast_to(low[:, b : b + 1], (LANES, LANES)) for b in range(count)], axis=0
    )
    picked = rows[:, :LANES]
    for q in range(1, 4):
        picked = jnp.where(lows == float(q), rows[:, q * LANES : (q + 1) * LANES], picked)
    return picked.astype(BF16)


def columns_of(owner, last):
    high = ((owner & 15) * 32 + last).astype(F32)
    return jnp.concatenate([high, (owner >> 4).astype(F32)], axis=0).T


def found_kernel(group, moved_ref, out_ref, wide, cols, scr):
    shards = moved_ref.shape[0]
    step = pl.program_id(0)

    @pl.when(step == 0)
    def _():
        wide[...] = widen(moved_ref)
        block = moved_ref.shape[1] - EXTRA
        scr[...] = moved_ref[:, block:, :].astype(F32).reshape(scr.shape)
        owner = scr[pl.ds(0, shards, stride=EXTRA), :].astype(I32)
        cols[...] = columns_of(owner, scr[pl.ds(1, shards, stride=EXTRA), :].astype(I32))

    turned = pltpu.roll(cols[...], lax.rem(LANES - step * group, LANES), 1)
    picked = pick_rows(group, turned, turned[:, shards:], wide[...])
    out_ref[...] = picked.reshape(out_ref.shape)


def serving_kernel(place_ref, moved_ref, out_ref):
    place = place_ref[...]
    blocks = place.shape[0]
    zero = jnp.zeros((LANES // 2 - blocks, LANES), I32)
    cols = columns_of(
        jnp.concatenate([place >> 11, zero], axis=0), jnp.concatenate([place & 31, zero], axis=0)
    )
    out_ref[...] = pick_rows(blocks, cols, cols[:, LANES // 2 :], widen(moved_ref))


def rank_kernel(group, ret_ref, mrow_ref, mcol_ref, w_ref, b_ref, score_ref, out_ref, total):
    step = pl.program_id(0)

    @pl.when(step == 0)
    def _():
        total[...] = jnp.zeros_like(total)

    slots = ret_ref.shape[1]
    turned = pltpu.roll(mcol_ref[...], lax.rem(LANES - step * group, LANES), 1)
    hots, values = [], []
    for b in range(group):
        hots.append(
            ones_where(iota((512, slots), 0) == mrow_ref[pl.ds(step * group + b, 1), :])
        )
        low = jnp.broadcast_to(turned[:, b : b + 1], (slots, LANES))
        rows = ret_ref[b]
        values.append(
            jnp.concatenate([rows * (1.0 - low).astype(BF16), rows * low.astype(BF16)], axis=1)
        )
    total[...] += dot(jnp.concatenate(hots, axis=1), jnp.concatenate(values, axis=0))

    @pl.when(step == pl.num_programs(0) - 1)
    def _():
        pooled = jnp.concatenate(
            [
                total[(f & 3) * LANES : (f & 3) * LANES + LANES, (f >> 2) * LANES : (f >> 2) * LANES + LANES]
                for f in range(8)
            ],
            axis=1,
        ).astype(BF16)
        hidden = jnp.maximum(dot(pooled, w_ref[...]) + b_ref[...], 0.0).astype(BF16)
        out_ref[...] = dot_nt(score_ref[...], hidden)


def whole(shape):
    return pl.BlockSpec(shape, lambda *step: (0,) * len(shape))


def call(kernel, name, flops, moved, **kwargs):
    return pl.pallas_call(
        kernel,
        name=name,
        compiler_params=pltpu.CompilerParams(vmem_limit_bytes=VMEM_LIMIT),
        cost_estimate=pl.CostEstimate(flops=flops, bytes_accessed=moved, transcendentals=0),
        **kwargs,
    )


def exchange(rows):
    return lax.all_to_all(rows, "shard", split_axis=0, concat_axis=0, tiled=True)


def on_device(
    table_rows,
    accum,
    hash_keys,
    hash_place,
    sample_ids,
    sample_grads,
    req_ids,
    w_hidden,
    b_hidden,
    w_score,
):
    rows_dev, width = table_rows.shape
    shards = lax.axis_size("shard")
    samples, id_columns = sample_ids.shape
    requests = req_ids.shape[0]
    slots = 2 * samples * id_columns // shards
    req_slots = 2 * requests * id_columns // shards
    hidden_width = w_hidden.shape[1]
    per_field = id_columns * width // sample_grads.shape[1]
    block = rows_dev // shards
    groups = 4
    sorted_rows = samples * id_columns // groups
    places = hash_place.reshape(-1, LANES)
    shape = jax.ShapeDtypeStruct
    extras = shape((shards * EXTRA, LANES), BF16)
    columns = shape((LANES, 2 * shards), F32)
    table = pltpu.VMEM((2 * LANES, places.shape[0] // 2), BF16)
    ex = pltpu.VMEM(extras.shape, F32)

    col, off, extra = call(
        functools.partial(index_kernel, shards, rows_dev, per_field, groups),
        "index",
        2**33,
        2**21,
        out_shape=(
            shape((groups, LANES, 2 * sorted_rows // LANES), F32),
            shape((shards, LANES), I32),
            extras,
        ),
        scratch_shapes=[
            table,
            ex,
            pltpu.VMEM((id_columns // per_field, per_field * samples), F32),
            pltpu.VMEM((id_columns // per_field, per_field * samples), F32),
            pltpu.VMEM(((id_columns // per_field + 1) * shards, LANES), F32),
            pltpu.VMEM((groups * shards, LANES), F32),
        ],
    )(sample_ids.T, places)

    group = 16
    sent = call(
        functools.partial(build_kernel, group, shards),
        "build",
        2**33,
        2**22,
        grid=(shards // group,),
        in_specs=[
            pl.BlockSpec(memory_space=pltpu.SMEM),
            whole(col.shape),
            whole(sample_grads.shape),
            pl.BlockSpec((group * EXTRA, LANES), lambda g: (g, 0)),
        ],
        out_specs=pl.BlockSpec((group, slots + EXTRA, width), lambda g: (g, 0, 0)),
        out_shape=shape((shards, slots + EXTRA, width), BF16),
        scratch_shapes=[pltpu.VMEM((groups, sorted_rows + 2 * slots, width), F32)],
    )(off, col, sample_grads, extra)
    got = exchange(sent)

    asked, mrow, mcol = call(
        functools.partial(request_kernel, shards, rows_dev),
        "request_index",
        2**31,
        2**19,
        out_shape=(extras, shape((shards, req_slots), I32), columns),
        scratch_shapes=[table, ex],
    )(req_ids.T.reshape(-1, 2 * requests), places)

    group = 8
    partial_sum = call(
        functools.partial(sum_kernel, group),
        "gradient_sum",
        2**33,
        2**22,
        grid=(shards // group,),
        in_specs=[
            pl.BlockSpec((group, slots + EXTRA, width), lambda g: (g, 0, 0)),
            pl.BlockSpec((shards, EXTRA, width), lambda g: (0, slots // EXTRA, 0)),
            pl.BlockSpec(memory_space=pl.ANY),
        ],
        out_specs=whole((rows_dev, width)),
        out_shape=shape((rows_dev, width), F32),
        scratch_shapes=[
            ex,
            pltpu.VMEM((2, shards, LANES), I32),
            pltpu.VMEM((LANES, LANES), F32),
            pltpu.VMEM((512, 512), F32),
        ],
    )(got, got, mrow)
    other = lax.ppermute(partial_sum, "rep", [(0, 1), (1, 0)])

    steps = 4
    rows_spec = pl.BlockSpec((rows_dev // steps, width), lambda g: (g, 0))
    new_rows, new_accum, moved = call(
        adagrad_kernel,
        "adagrad",
        2**21,
        2**23,
        grid=(steps,),
        in_specs=[rows_spec] * 4
        + [pl.BlockSpec((shards * EXTRA // steps, LANES), lambda g: (g, 0))],
        out_specs=(
            rows_spec,
            rows_spec,
            pl.BlockSpec((shards // steps, block + EXTRA, width), lambda g: (g, 0, 0)),
        ),
        out_shape=(
            shape((rows_dev, width), F32),
            shape((rows_dev, width), F32),
            shape((shards, block + EXTRA, width), BF16),
        ),
    )(table_rows, accum, partial_sum, other, asked)
    moved = exchange(moved)

    group = 16
    found = call(
        functools.partial(found_kernel, group),
        "found",
        2**32,
        2**22,
        grid=(shards // group,),
        in_specs=[whole(moved.shape)],
        out_specs=pl.BlockSpec((group, req_slots, width), lambda g: (g, 0, 0)),
        out_shape=shape((shards, req_slots, width), BF16),
        scratch_shapes=[
            pltpu.VMEM((512, 512), BF16),
            pltpu.VMEM((LANES, LANES), F32),
            ex,
        ],
    )(moved)
    returned = exchange(found)

    place_rows = rows_dev // LANES
    own_places = lax.dynamic_slice_in_dim(
        places, lax.axis_index("shard") * place_rows, place_rows, axis=0
    )
    serving_rows = call(
        serving_kernel,
        "serving",
        2**30,
        2**20,
        out_shape=shape((rows_dev, width), BF16),
    )(own_places, moved)

    scores = call(
        functools.partial(rank_kernel, group),
        "pool_rank",
        2**32,
        2**22,
        grid=(shards // group,),
        in_specs=[
            pl.BlockSpec((group, req_slots, width), lambda g: (g, 0, 0)),
            whole((shards, req_slots)),
            whole(columns.shape),
            whole(w_hidden.shape),
            whole((1, hidden_width)),
            whole((1, hidden_width)),
        ],
        out_specs=whole((1, requests)),
        out_shape=shape((1, requests), F32),
        scratch_shapes=[pltpu.VMEM((512, 256), F32)],
    )(returned, mrow, mcol, w_hidden, b_hidden.reshape(1, -1), w_score.reshape(1, -1))
    return (new_rows, new_accum, serving_rows, scores.reshape(requests))


def solution(mesh):
    return jax.shard_map(
        on_device,
        mesh=mesh,
        in_specs=(
            P("shard", None),
            P("shard", None),
            P("shard"),
            P(),
            P(("rep", "shard"), None),
            P(("rep", "shard"), None),
            P(("rep", "shard"), None),
            P(),
            P(),
            P(),
        ),
        out_specs=(P("shard", None), P("shard", None), P("shard", None), P(("rep", "shard"))),
        check_vma=False,
    )
```

```python
import functools

import jax
import jax.numpy as jnp
from jax import lax
from jax.experimental import pallas as pl
from jax.experimental.pallas import tpu as pltpu
from jax.sharding import PartitionSpec as P

F32, BF16, I32 = jnp.float32, jnp.bfloat16, jnp.int32
NT = (((1,), (1,)), ((), ()))
SMALL, LARGE = 32 * 2**20, 60 * 2**20
EXTRA = 16
LANES = 128
REQ_SLOTS = 112


def iota(shape, axis, dtype=I32):
    return lax.broadcasted_iota(I32, shape, axis).astype(dtype)


def dot(a, b):
    return jnp.dot(a, b, preferred_element_type=F32)


def dot_nt(a, b):
    return lax.dot_general(a, b, NT, preferred_element_type=F32)


def ones_where(mask):
    return jnp.where(mask, 1.0, 0.0).astype(BF16)


def lanes_of(ref, first, count):
    return jnp.concatenate([ref[pl.ds(first + k, 1), :] for k in range(count)], axis=1)


def rank_ids(owner, base, shards, tri, ones):
    width = tri.shape[0]
    chunks = owner.shape[1] // width
    own = jnp.where(iota((shards, owner.shape[1]), 0, F32) == owner, 1.0, 0.0)
    stacked = jnp.concatenate(
        [own[:, k * width : (k + 1) * width] for k in range(chunks)], axis=0
    ).astype(BF16)
    before = dot(stacked, tri)
    totals = dot(stacked, ones)
    ranks = []
    for k in range(chunks):
        rows = slice(k * shards, (k + 1) * shards)
        at = before[rows] + jnp.concatenate([base] * (width // LANES), axis=1)
        ranks.append(jnp.sum(own[:, k * width : (k + 1) * width] * at, axis=0, keepdims=True))
        base = base + totals[rows]
    return own, jnp.concatenate(ranks, axis=1), base


def strict_upper(width):
    return ones_where(iota((width, width), 0) < iota((width, width), 1))


def pack_places(place, shift, block):
    last = place & (block - 1)
    scale = (1 << (last & 15)).astype(F32) * jnp.where(last >= 16, 65536.0, 1.0)
    packed = ((place >> shift) + 64).astype(F32) * scale
    half = place.shape[0] // 2
    return jnp.concatenate([packed[:half].T, packed[half:].T], axis=0).astype(BF16)


def look_up(table, ids):
    count = ids.shape[1]
    lows, lines = table.shape
    line = ids >> 7
    hot = ones_where(iota((lines, count), 0) == (line & (lines - 1)))
    low = (ids & 127) + jnp.where(line >= lines, LANES, 0)
    found = jnp.where(iota((lows, count), 0) == low, dot(table, hot), 0.0)
    value = jnp.sum(found, axis=0, keepdims=True)
    last = jnp.zeros_like(value)
    for bits in (16, 8, 4, 2, 1):
        big = value >= 64.0 * 2.0**bits
        value = jnp.where(big, value * 2.0**-bits, value)
        last = last + jnp.where(big, float(bits), 0.0)
    return value - 64.0, last


def index_kernel(
    shards, rows_dev, per_field, groups,
    ids_ref, place_ref, req_ref, col_ref, off_ref, extra_ref, mrow_ref, mcol_ref,
    table, ex, own_scr, rank_scr, mark, off_scr,
):
    shift = rows_dev.bit_length() - 1
    width = ids_ref.shape[1]
    count = per_field * width
    fields = ids_ref.shape[0] // per_field
    span = fields // groups
    table[...] = pack_places(place_ref[...], shift, rows_dev // shards)
    tri = strict_upper(width)
    ones = jnp.ones((width, LANES), BF16)

    def field_step(field, carry):
        base, row = carry
        ids = lanes_of(ids_ref, field * per_field, per_field)
        owner, last = look_up(table[...], ids)
        mark[pl.ds(field * shards, shards), :] = base
        own, rank, base = rank_ids(owner, base, shards, tri, ones)
        own_scr[pl.ds(field, 1), :] = owner
        rank_scr[pl.ds(field, 1), :] = rank
        at = ones_where(iota((width, count), 0, F32) == rank)
        target = jnp.concatenate([own * (ids >> shift).astype(F32), own * last], axis=0)
        row = row + dot_nt(target.astype(BF16), at)
        return base, row

    base, row = lax.fori_loop(
        0,
        fields,
        field_step,
        (jnp.zeros((shards, LANES), F32), jnp.zeros((2 * shards, width), F32)),
    )
    mark[fields * shards :, :] = base
    ex[...] = jnp.zeros_like(ex)
    for kind in range(2):
        for half in range(2):
            ex[pl.ds(2 * kind + half, shards, stride=EXTRA), :] = row[
                kind * shards : (kind + 1) * shards, half * LANES : (half + 1) * LANES
            ]
    index_requests(shards, shift, req_ref, table, ex, mrow_ref, mcol_ref)
    extra_ref[...] = ex[...].astype(BF16)

    earlier = ones_where(iota((shards, shards), 1) < iota((shards, shards), 0))
    lane = iota((shards, LANES), 1)
    table_off = jnp.zeros((shards, LANES), F32)
    for g in range(groups):
        first = mark[g * span * shards : (g * span + 1) * shards, :]
        after = mark[(g + 1) * span * shards : ((g + 1) * span + 1) * shards, :]
        off = dot(earlier, (after - first).astype(BF16)) - first
        off_scr[g * shards : (g + 1) * shards, :] = off
        table_off = jnp.where(lane == g, off, table_off)
        table_off = jnp.where(lane == groups + g, after, table_off)
    off_ref[...] = table_off.astype(I32)

    total = span * count
    blocks = total // LANES
    at = iota((1, total), 1)
    sample = (at & (width - 1)).astype(F32)
    field = (at // count).astype(F32)

    def group_step(g, unused):
        owner = lanes_of(own_scr, g * span, span)
        off = off_scr[pl.ds(g * shards, shards), :]
        shifts = jnp.where(
            iota((shards, total), 0, F32) == owner,
            jnp.concatenate([off] * blocks, axis=1),
            0.0,
        )
        pos = lanes_of(rank_scr, g * span, span) + jnp.sum(shifts, axis=0, keepdims=True)
        pos = pos.astype(I32)
        block = iota((blocks, total), 0) == (pos >> 7)
        source = jnp.concatenate(
            [jnp.where(block, sample, 0.0), jnp.where(block, field, 0.0)], axis=0
        ).astype(BF16)
        col_ref[g] = dot_nt(ones_where(iota((LANES, total), 0) == (pos & 127)), source)
        return unused

    lax.fori_loop(0, groups, group_step, 0)


def index_requests(shards, shift, req_ref, table, ex, mrow_ref, mcol_ref):
    width = req_ref.shape[1]
    batch = 4
    count = batch * width
    tri = strict_upper(width)
    ones = jnp.ones((width, LANES), BF16)
    lane = iota((1, count), 1)

    def step(c, carry):
        base, row, col = carry
        ids = lanes_of(req_ref, c * batch, batch)
        owner, last = look_up(table[...], ids)
        own, rank, base = rank_ids(owner, base, shards, tri, ones)
        at = ones_where(iota((LANES, count), 0, F32) == jnp.where(rank < REQ_SLOTS, rank, -1.0))
        field = c * (batch // 2) + lane // (2 * width)
        query = (own * (lane & (LANES - 1)).astype(F32)).astype(BF16)
        number = (own * (field + 1).astype(F32)).astype(BF16)
        high = (own * (ids >> shift).astype(F32)).astype(BF16)
        low = (own * last).astype(BF16)
        row = row + dot_nt(jnp.concatenate([high, low, query, number], axis=0), at)
        col = col + dot_nt(at, jnp.concatenate([number, number], axis=0))
        return base, row, col

    base, row, col = lax.fori_loop(
        0,
        req_ref.shape[0] // batch,
        step,
        (
            jnp.zeros((shards, LANES), F32),
            jnp.zeros((4 * shards, LANES), F32),
            jnp.zeros((LANES, 2 * shards), F32),
        ),
    )
    most = jnp.broadcast_to(jnp.max(base, axis=0, keepdims=True), (shards, LANES)).astype(I32)
    parts = [row[:shards], row[shards : 2 * shards], (most >> 5).astype(F32), (most & 31).astype(F32)]
    for kind, part in enumerate(parts):
        ex[pl.ds(4 + kind, shards, stride=EXTRA), :] = part
    field = row[3 * shards :].astype(I32) - 1
    mrow_ref[...] = jnp.where(
        field < 0, -1, (field & 3) * LANES + row[2 * shards : 3 * shards].astype(I32)
    )
    mcol_ref[...] = jnp.where(col > 4.0, 1.0, 0.0)


def build_kernel(group, shards, off_ref, col_ref, grads_ref, extra_ref, out_ref, rows_scr):
    slots = out_ref.shape[1] - EXTRA
    samples = grads_ref.shape[0]
    groups = col_ref.shape[0]
    blocks = col_ref.shape[2] // 2
    total = blocks * LANES
    span = grads_ref.shape[1] // groups
    step = pl.program_id(0)

    @pl.when(step == 0)
    def _():
        def sort_group(g, unused):
            col = col_ref[g]
            hots = [
                ones_where(iota((LANES, samples), 1, F32) == col[:, b : b + 1])
                for b in range(blocks)
            ]
            part = grads_ref[:, pl.ds(pl.multiple_of(g * span, span), span)]
            rows = dot(jnp.concatenate(hots, axis=0), part)
            field = jnp.concatenate(
                [
                    jnp.broadcast_to(col[:, blocks + b : blocks + b + 1], (LANES, LANES))
                    for b in range(blocks)
                ],
                axis=0,
            )
            picked = rows[:, :LANES]
            for q in range(1, span // LANES):
                picked = jnp.where(field == float(q), rows[:, q * LANES : (q + 1) * LANES], picked)
            rows_scr[g, slots : slots + total, :] = picked
            return unused

        lax.fori_loop(0, groups, sort_group, 0)

    at = iota((slots, LANES), 0)

    def one(b, unused):
        owner = step * group + b
        picked = rows_scr[0, pl.ds(slots + off_ref[owner, 0], slots), :]
        for g in range(1, groups):
            start = off_ref[owner, groups + g - 1]
            rows = rows_scr[g, pl.ds(slots + off_ref[owner, g], slots), :]
            picked = jnp.where(at >= start, rows, picked)
        picked = jnp.where(at >= off_ref[owner, 2 * groups - 1], 0.0, picked)
        out_ref[b, 0:slots, :] = picked.astype(BF16)
        out_ref[b, slots : slots + EXTRA, :] = extra_ref[pl.ds(b * EXTRA, EXTRA), :]
        return unused

    lax.fori_loop(0, group, one, 0, unroll=4)


def sum_kernel(group, got_ref, extra_ref, out_ref, picks_ref, scr, hi_scr, lo_scr, total):
    shards = extra_ref.shape[0]
    slots = got_ref.shape[1] - EXTRA
    step = pl.program_id(0)

    @pl.when(step == 0)
    def _():
        scr[...] = extra_ref[...].astype(F32).reshape(scr.shape)
        lows = []
        for half in range(2):
            ranges = scr[pl.ds(half, shards, stride=EXTRA), :].astype(I32)
            within = scr[pl.ds(2 + half, shards, stride=EXTRA), :].astype(I32)
            hi_scr[half] = (ranges & 15) * 32 + within
            lows.append((ranges >> 4).astype(F32))
        lo_scr[...] = jnp.concatenate(lows, axis=0).T
        total[...] = jnp.zeros_like(total)
        kinds = [scr[pl.ds(kind, shards, stride=EXTRA), :].astype(I32) for kind in range(4, 8)]
        high = (kinds[0] & 15) * 32 + kinds[1]
        picks_ref[...] = jnp.concatenate([high, kinds[0] >> 4], axis=0).astype(F32).T
        most = jnp.max((kinds[2] * 32 + kinds[3]).astype(F32), axis=0, keepdims=True)
        out_ref[4 * 512 :, :] = jnp.broadcast_to(most, (8, LANES))

    turned = pltpu.roll(lo_scr[...], lax.rem(2 * shards - step * group, 2 * shards), 1)
    highs, values = [], []
    for k in range(group):
        for half in range(2):
            hi = hi_scr[half, pl.ds(step * group + k, 1), :]
            highs.append(ones_where(iota((512, LANES), 0) == hi))
            low = jnp.broadcast_to(
                turned[:, half * shards + k : half * shards + k + 1], (LANES, LANES)
            )
            rows = got_ref[k, half * LANES : (half + 1) * LANES, :]
            values.append(
                jnp.concatenate([rows * ones_where(low == float(q)) for q in range(4)], axis=1)
            )
    total[...] += dot(jnp.concatenate(highs, axis=1), jnp.concatenate(values, axis=0))

    @pl.when(step == pl.num_programs(0) - 1)
    def _():
        for q in range(4):
            out_ref[q * 512 : (q + 1) * 512, :] = total[:, q * LANES : (q + 1) * LANES]


def pick_rows(count, height, high, low, wide):
    hots = [
        ones_where(iota((height, 512), 1, F32) == high[:height, b : b + 1]) for b in range(count)
    ]
    rows = dot(jnp.concatenate(hots, axis=0), wide)
    lows = jnp.concatenate(
        [jnp.broadcast_to(low[:height, b : b + 1], (height, LANES)) for b in range(count)], axis=0
    )
    picked = rows[:, :LANES]
    for q in range(1, 4):
        picked = jnp.where(lows == float(q), rows[:, q * LANES : (q + 1) * LANES], picked)
    return picked.astype(BF16)


def update_kernel(
    group, table_ref, accum_ref, one_ref, two_ref, picks_ref, rows_ref, accum_out_ref, sent_ref,
    most_ref, rows, updated, moved, wide, sems,
):
    step = pl.program_id(0)
    count = rows.shape[0]
    copies = (
        pltpu.make_async_copy(rows, rows_ref, sems.at[0]),
        pltpu.make_async_copy(updated, accum_out_ref, sems.at[1]),
    )

    @pl.when(step == 0)
    def _():
        most_ref[...] = jnp.maximum(one_ref[count:, :], two_ref[count:, :])
        gradient = one_ref[:count, :] + two_ref[:count, :]
        history = accum_ref[...] + gradient * gradient
        updated[...] = history
        rows[...] = table_ref[...] - 0.1 * gradient * lax.rsqrt(history)
        for copy in copies:
            copy.start()
        moved[...] = rows[...].astype(BF16)
        wide[...] = jnp.concatenate(
            [moved[q * 512 : (q + 1) * 512, :] for q in range(4)], axis=1
        )

    turned = pltpu.roll(picks_ref[...], lax.rem(LANES - step * group, LANES), 1)
    picked = pick_rows(group, REQ_SLOTS, turned, turned[:, LANES // 2 :], wide[...])
    sent_ref[:, :REQ_SLOTS, :] = picked.reshape(group, REQ_SLOTS, LANES)
    block = sent_ref.shape[1] - REQ_SLOTS
    start = pl.multiple_of(step * (group * block), group * block)
    sent_ref[:, REQ_SLOTS:, :] = moved[pl.ds(start, group * block), :].reshape(group, block, LANES)

    @pl.when(step == pl.num_programs(0) - 1)
    def _():
        for copy in copies:
            copy.wait()


def rank_kernel(
    group, ret_ref, mrow_ref, mcol_ref, place_ref, w_ref, b_ref, score_ref, out_ref, serving_ref,
    total, wide,
):
    step = pl.program_id(0)

    @pl.when(step == 0)
    def _():
        total[...] = jnp.zeros_like(total)

    turned = pltpu.roll(mcol_ref[...], lax.rem(LANES - step * group, LANES), 1)
    hots, values = [], []
    for b in range(group):
        hots.append(
            ones_where(iota((512, LANES), 0) == mrow_ref[pl.ds(step * group + b, 1), :])
        )
        low = jnp.broadcast_to(turned[:, b : b + 1], (LANES, LANES))
        rows = ret_ref[b, :LANES, :]
        values.append(
            jnp.concatenate([rows * (1.0 - low).astype(BF16), rows * low.astype(BF16)], axis=1)
        )
    total[...] += dot(jnp.concatenate(hots, axis=1), jnp.concatenate(values, axis=0))
    wide[step] = ret_ref[:, REQ_SLOTS:, :].reshape(wide.shape[1:])

    @pl.when(step == pl.num_programs(0) - 1)
    def _():
        pooled = jnp.concatenate(
            [
                total[(f & 3) * LANES : (f & 3) * LANES + LANES, (f >> 2) * LANES : (f >> 2) * LANES + LANES]
                for f in range(8)
            ],
            axis=1,
        ).astype(BF16)
        hidden = jnp.maximum(dot(pooled, w_ref[...]) + b_ref[...], 0.0).astype(BF16)
        out_ref[...] = dot_nt(score_ref[...], hidden)
        place = place_ref[...]
        owner, last = place >> 11, place & 31
        high = ((owner & 15) * 32 + last).astype(F32)
        zero = jnp.zeros((LANES // 2 - place.shape[0], LANES), F32)
        cols = jnp.concatenate([high, zero, (owner >> 4).astype(F32), zero], axis=0).T
        moved = jnp.concatenate([wide[q] for q in range(4)], axis=1)
        serving_ref[...] = pick_rows(
            place.shape[0], LANES, cols, cols[:, LANES // 2 :], moved
        )


def bucket_slots(targets, target_count, capacity):
    one_hot = (targets[:, None] == jnp.arange(target_count, dtype=I32)[None, :]).astype(I32)
    ranking = jnp.sum(jnp.cumsum(one_hot, axis=0) * one_hot, axis=1) - 1
    return targets * capacity + ranking


def range_scores(serving_rows, req_ids, w_hidden, b_hidden, w_score, shards, fields):
    rows_dev, width = serving_rows.shape
    requests, id_columns = req_ids.shape
    capacity = 2 * requests * id_columns // shards
    flat = req_ids.reshape(-1)
    slot = bucket_slots(flat // rows_dev, shards, capacity)
    keys = jnp.zeros((shards * capacity,), I32).at[slot].set(flat % rows_dev)
    asked = exchange(keys.reshape(shards, capacity))
    found = jnp.take(serving_rows, asked.reshape(-1), axis=0, mode="clip")
    returned = exchange(found.reshape(shards, capacity, width)).reshape(-1, width)
    rows = jnp.take(returned, slot, axis=0, mode="clip").astype(F32)
    pooled = jnp.sum(rows.reshape(requests * fields, id_columns // fields, width), axis=1)
    pooled = pooled.astype(BF16).reshape(requests, fields * width)
    hidden = jnp.dot(pooled, w_hidden, preferred_element_type=F32) + b_hidden
    return jnp.dot(jax.nn.relu(hidden).astype(BF16), w_score, preferred_element_type=F32)


def whole(shape):
    return pl.BlockSpec(shape, lambda *step: (0,) * len(shape))


def call(kernel, name, flops, moved, limit=SMALL, **kwargs):
    return pl.pallas_call(
        kernel,
        name=name,
        compiler_params=pltpu.CompilerParams(vmem_limit_bytes=limit),
        cost_estimate=pl.CostEstimate(flops=flops, bytes_accessed=moved, transcendentals=0),
        **kwargs,
    )


def exchange(rows):
    return lax.all_to_all(rows, "shard", split_axis=0, concat_axis=0, tiled=True)


def on_device(
    table_rows,
    accum,
    hash_keys,
    hash_place,
    sample_ids,
    sample_grads,
    req_ids,
    w_hidden,
    b_hidden,
    w_score,
):
    rows_dev, width = table_rows.shape
    shards = lax.axis_size("shard")
    samples, id_columns = sample_ids.shape
    requests = req_ids.shape[0]
    slots = 2 * samples * id_columns // shards
    hidden_width = w_hidden.shape[1]
    per_field = id_columns * width // sample_grads.shape[1]
    block = rows_dev // shards
    groups = 4
    sorted_rows = samples * id_columns // groups
    places = hash_place.reshape(-1, LANES)
    shape = jax.ShapeDtypeStruct
    extras = shape((shards * EXTRA, LANES), BF16)
    columns = shape((LANES, 2 * shards), F32)
    table = pltpu.VMEM((2 * LANES, places.shape[0] // 2), BF16)
    ex = pltpu.VMEM(extras.shape, F32)

    col, off, extra, mrow, mcol = call(
        functools.partial(index_kernel, shards, rows_dev, per_field, groups),
        "index",
        2**33,
        2**21,
        LARGE,
        out_shape=(
            shape((groups, LANES, 2 * sorted_rows // LANES), F32),
            shape((shards, LANES), I32),
            extras,
            shape((shards, LANES), I32),
            columns,
        ),
        scratch_shapes=[
            table,
            ex,
            pltpu.VMEM((id_columns // per_field, per_field * samples), F32),
            pltpu.VMEM((id_columns // per_field, per_field * samples), F32),
            pltpu.VMEM(((id_columns // per_field + 1) * shards, LANES), F32),
            pltpu.VMEM((groups * shards, LANES), F32),
        ],
    )(sample_ids.T, places, req_ids.T.reshape(-1, 2 * requests))

    group = 16
    sent = call(
        functools.partial(build_kernel, group, shards),
        "build",
        2**33,
        2**22,
        LARGE,
        grid=(shards // group,),
        in_specs=[
            pl.BlockSpec(memory_space=pltpu.SMEM),
            whole(col.shape),
            whole(sample_grads.shape),
            pl.BlockSpec((group * EXTRA, LANES), lambda g: (g, 0)),
        ],
        out_specs=pl.BlockSpec((group, slots + EXTRA, width), lambda g: (g, 0, 0)),
        out_shape=shape((shards, slots + EXTRA, width), BF16),
        scratch_shapes=[pltpu.VMEM((groups, sorted_rows + 2 * slots, width), F32)],
    )(off, col, sample_grads, extra)
    got = exchange(sent)

    group = 8
    partial_sum, picks = call(
        functools.partial(sum_kernel, group),
        "gradient_sum",
        2**33,
        2**22,
        grid=(shards // group,),
        in_specs=[
            pl.BlockSpec((group, slots + EXTRA, width), lambda g: (g, 0, 0)),
            pl.BlockSpec((shards, EXTRA, width), lambda g: (0, slots // EXTRA, 0)),
        ],
        out_specs=(whole((rows_dev + 8, width)), whole(columns.shape)),
        out_shape=(shape((rows_dev + 8, width), F32), columns),
        scratch_shapes=[
            ex,
            pltpu.VMEM((2, shards, LANES), I32),
            pltpu.VMEM((LANES, LANES), F32),
            pltpu.VMEM((512, 512), F32),
        ],
    )(got, got)
    other = lax.ppermute(partial_sum, "rep", [(0, 1), (1, 0)])

    group = 16
    rows_type = shape((rows_dev, width), F32)
    any_space = pl.BlockSpec(memory_space=pl.ANY)
    new_rows, new_accum, sent, most = call(
        functools.partial(update_kernel, group),
        "update",
        2**32,
        2**23,
        grid=(shards // group,),
        in_specs=[
            whole(table_rows.shape),
            whole(accum.shape),
            whole(partial_sum.shape),
            whole(partial_sum.shape),
            whole(columns.shape),
        ],
        out_specs=(
            any_space,
            any_space,
            pl.BlockSpec((group, REQ_SLOTS + block, width), lambda g: (g, 0, 0)),
            whole((8, LANES)),
        ),
        out_shape=(
            rows_type,
            rows_type,
            pltpu.HBM((shards, REQ_SLOTS + block, width), BF16),
            shape((8, LANES), F32),
        ),
        scratch_shapes=[
            pltpu.VMEM(table_rows.shape, F32),
            pltpu.VMEM(table_rows.shape, F32),
            pltpu.VMEM(table_rows.shape, BF16),
            pltpu.VMEM((512, 512), BF16),
            pltpu.SemaphoreType.DMA((2,)),
        ],
    )(table_rows, accum, partial_sum, other, picks)
    returned = exchange(sent)

    place_rows = rows_dev // LANES
    own_places = lax.dynamic_slice_in_dim(
        places, lax.axis_index("shard") * place_rows, place_rows, axis=0
    )
    scores, serving_rows = call(
        functools.partial(rank_kernel, group),
        "pool_rank",
        2**32,
        2**22,
        grid=(shards // group,),
        in_specs=[
            pl.BlockSpec((group, REQ_SLOTS + block, width), lambda g: (g, 0, 0)),
            whole((shards, LANES)),
            whole(columns.shape),
            whole(own_places.shape),
            whole(w_hidden.shape),
            whole((1, hidden_width)),
            whole((1, hidden_width)),
        ],
        out_specs=(whole((1, requests)), whole((rows_dev, width))),
        out_shape=(shape((1, requests), F32), shape((rows_dev, width), BF16)),
        scratch_shapes=[pltpu.VMEM((512, 256), F32), pltpu.VMEM((4, 512, LANES), BF16)],
    )(returned, mrow, mcol, own_places, w_hidden, b_hidden.reshape(1, -1), w_score.reshape(1, -1))
    scores = lax.cond(
        most[0, 0] <= REQ_SLOTS,
        lambda: scores.reshape(requests),
        lambda: range_scores(
            serving_rows, req_ids, w_hidden, b_hidden, w_score, shards, id_columns // per_field
        ),
    )
    return (new_rows, new_accum, serving_rows, scores)


def solution(mesh):
    return jax.shard_map(
        on_device,
        mesh=mesh,
        in_specs=(
            P("shard", None),
            P("shard", None),
            P("shard"),
            P(),
            P(("rep", "shard"), None),
            P(("rep", "shard"), None),
            P(("rep", "shard"), None),
            P(),
            P(),
            P(),
        ),
        out_specs=(P("shard", None), P("shard", None), P("shard", None), P(("rep", "shard"))),
        check_vma=False,
    )
```

```python
import functools

import jax
import jax.numpy as jnp
from jax import lax
from jax.experimental import pallas as pl
from jax.experimental.pallas import tpu as pltpu
from jax.sharding import PartitionSpec as P

F32, BF16, I32 = jnp.float32, jnp.bfloat16, jnp.int32
NT = (((1,), (1,)), ((), ()))
VMEM_LIMIT = 32 * 2**20
EXTRA = 16
LANES = 128
REQ_SLOTS = 112


def iota(shape, axis, dtype=I32):
    return lax.broadcasted_iota(I32, shape, axis).astype(dtype)


def dot(a, b):
    return jnp.dot(a, b, preferred_element_type=F32)


def dot_nt(a, b):
    return lax.dot_general(a, b, NT, preferred_element_type=F32)


def ones_where(mask):
    return jnp.where(mask, 1.0, 0.0).astype(BF16)


def lanes_of(ref, first, count):
    return jnp.concatenate([ref[pl.ds(first + k, 1), :] for k in range(count)], axis=1)


def rank_ids(owner, base, shards, tri, ones):
    width = tri.shape[0]
    chunks = owner.shape[1] // width
    own = jnp.where(iota((shards, owner.shape[1]), 0, F32) == owner, 1.0, 0.0)
    stacked = jnp.concatenate(
        [own[:, k * width : (k + 1) * width] for k in range(chunks)], axis=0
    ).astype(BF16)
    before = dot(stacked, tri)
    totals = dot(stacked, ones)
    ranks = []
    for k in range(chunks):
        rows = slice(k * shards, (k + 1) * shards)
        at = before[rows] + jnp.concatenate([base] * (width // LANES), axis=1)
        ranks.append(jnp.sum(own[:, k * width : (k + 1) * width] * at, axis=0, keepdims=True))
        base = base + totals[rows]
    return own, jnp.concatenate(ranks, axis=1), base


def strict_upper(width):
    return ones_where(iota((width, width), 0) < iota((width, width), 1))


def pack_places(place, shift, block):
    last = place & (block - 1)
    scale = (1 << (last & 15)).astype(F32) * jnp.where(last >= 16, 65536.0, 1.0)
    packed = ((place >> shift) + 64).astype(F32) * scale
    half = place.shape[0] // 2
    return jnp.concatenate([packed[:half].T, packed[half:].T], axis=0).astype(BF16)


def look_up(table, ids):
    count = ids.shape[1]
    lows, lines = table.shape
    line = ids >> 7
    hot = ones_where(iota((lines, count), 0) == (line & (lines - 1)))
    low = (ids & 127) + jnp.where(line >= lines, LANES, 0)
    found = jnp.where(iota((lows, count), 0) == low, dot(table, hot), 0.0)
    return jnp.sum(found, axis=0, keepdims=True)


def unpack(value):
    last, scale = jnp.zeros_like(value), jnp.ones_like(value)
    for bits in (16, 8, 4, 2, 1):
        big = value >= 64.0 * 2.0**bits
        value = jnp.where(big, value * 2.0**-bits, value)
        last = last + jnp.where(big, float(bits), 0.0)
        scale = jnp.where(big, scale * 2.0**bits, scale)
    return value - 64.0, last, scale


def send_kernel(
    shards, rows_dev, per_field, groups, group,
    ids_ref, place_ref, req_ref, grads_ref, out_ref, mrow_ref, mcol_ref,
    ids, places, requests, grads, col, off_vmem, off, extra, rows_scr, sems, *scratch,
):
    step = pl.program_id(0)

    @pl.when(step == 0)
    def _():
        loads = [
            pltpu.make_async_copy(source, target, sems.at[at])
            for at, (source, target) in enumerate(
                ((place_ref, places), (ids_ref, ids), (req_ref, requests), (grads_ref, grads))
            )
        ]
        for load in loads:
            load.start()
        for load in loads[:3]:
            load.wait()
        index_ids(
            shards, rows_dev, per_field, groups,
            ids, places, requests, col, off_vmem, extra, mrow_ref, mcol_ref, *scratch,
        )
        copy = pltpu.make_async_copy(off_vmem, off, sems.at[4])
        copy.start()
        loads[3].wait()
        sort_rows(col, grads, rows_scr)
        copy.wait()

    fill_slots(step, group, groups, off, extra, rows_scr, out_ref)


def index_ids(
    shards, rows_dev, per_field, groups,
    ids_ref, place_ref, req_ref, col_ref, off_ref, extra_ref, mrow_ref, mcol_ref,
    table, ex, values, owners, scales, rank_scr, mark, off_scr,
):
    shift = rows_dev.bit_length() - 1
    width = ids_ref.shape[1]
    count = per_field * width
    fields = ids_ref.shape[0] // per_field
    span = fields // groups
    batch = count // req_ref.shape[1]
    batches = req_ref.shape[0] // batch
    table[...] = pack_places(place_ref[...], shift, rows_dev // shards)
    tri = strict_upper(width)
    ones = jnp.ones((width, LANES), BF16)

    def train_look_up(c, unused):
        ids = lanes_of(ids_ref, c * per_field, per_field)
        values[pl.ds(c, 1), :] = look_up(table[...], ids)
        return unused

    def request_look_up(c, unused):
        ids = lanes_of(req_ref, c * batch, batch)
        values[pl.ds(fields + c, 1), :] = look_up(table[...], ids)
        return unused

    values[...] = jnp.zeros_like(values)
    lax.fori_loop(0, fields, train_look_up, 0, unroll=4)
    lax.fori_loop(0, batches, request_look_up, 0, unroll=4)
    owner, unused, scale = unpack(values[...])
    owners[...] = owner
    scales[...] = scale

    def packed(ids, at):
        return ((ids >> shift) + 64).astype(F32) * scales[pl.ds(at, 1), :]

    def field_step(field, carry):
        base, row = carry
        ids = lanes_of(ids_ref, field * per_field, per_field)
        mark[pl.ds(field * shards, shards), :] = base
        own, rank, base = rank_ids(owners[pl.ds(field, 1), :], base, shards, tri, ones)
        rank_scr[pl.ds(field, 1), :] = rank
        at = ones_where(iota((width, count), 0, F32) == rank)
        return base, row + dot_nt((own * packed(ids, field)).astype(BF16), at)

    base, row = lax.fori_loop(
        0,
        fields,
        field_step,
        (jnp.zeros((shards, LANES), F32), jnp.zeros((shards, width), F32)),
        unroll=4,
    )
    mark[fields * shards :, :] = base

    lane = iota((1, count), 1)

    def request_step(c, carry):
        base, row = carry
        ids = lanes_of(req_ref, c * batch, batch)
        own, rank, base = rank_ids(owners[pl.ds(fields + c, 1), :], base, shards, tri, ones)
        at = ones_where(iota((LANES, count), 0, F32) == jnp.where(rank < REQ_SLOTS, rank, -1.0))
        field = c * (batch // per_field) + lane // (per_field * LANES)
        digits = [
            own * packed(ids, fields + c),
            own * (lane & (LANES - 1)).astype(F32),
            own * (field + 1).astype(F32),
        ]
        return base, row + dot_nt(jnp.concatenate(digits, axis=0).astype(BF16), at)

    most, asked = lax.fori_loop(
        0,
        batches,
        request_step,
        (jnp.zeros((shards, LANES), F32), jnp.zeros((3 * shards, LANES), F32)),
        unroll=4,
    )
    most = jnp.minimum(jnp.max(most, axis=0, keepdims=True), 255.0)
    parts = [
        row[:, :LANES], row[:, LANES:], asked[:shards], jnp.broadcast_to(most, (shards, LANES))
    ]
    ex[...] = jnp.zeros_like(ex)
    for kind, part in enumerate(parts):
        ex[pl.ds(kind, shards, stride=EXTRA), :] = part
    extra_ref[...] = ex[...].astype(BF16)
    number = asked[2 * shards :]
    field = number.astype(I32) - 1
    mrow_ref[...] = jnp.where(
        field < 0, -1, (field & 3) * LANES + asked[shards : 2 * shards].astype(I32)
    )
    mcol_ref[...] = jnp.where(jnp.concatenate([number, number], axis=0).T > 4.0, 1.0, 0.0)

    earlier = ones_where(iota((shards, shards), 1) < iota((shards, shards), 0))
    lane = iota((shards, LANES), 1)
    table_off = jnp.zeros((shards, LANES), F32)
    for g in range(groups):
        first = mark[g * span * shards : (g * span + 1) * shards, :]
        after = mark[(g + 1) * span * shards : ((g + 1) * span + 1) * shards, :]
        off = dot(earlier, (after - first).astype(BF16)) - first
        off_scr[g * shards : (g + 1) * shards, :] = off
        table_off = jnp.where(lane == g, off, table_off)
        table_off = jnp.where(lane == groups + g, after, table_off)
    off_ref[...] = table_off.astype(I32)

    total = span * count
    blocks = total // LANES
    at = iota((1, total), 1)
    sample = (at & (width - 1)).astype(F32)
    field = (at // count).astype(F32)

    def group_step(g, unused):
        owner = lanes_of(owners, g * span, span)
        off = off_scr[pl.ds(g * shards, shards), :]
        shifts = jnp.where(
            iota((shards, total), 0, F32) == owner,
            jnp.concatenate([off] * blocks, axis=1),
            0.0,
        )
        pos = lanes_of(rank_scr, g * span, span) + jnp.sum(shifts, axis=0, keepdims=True)
        pos = pos.astype(I32)
        block = iota((blocks, total), 0) == (pos >> 7)
        source = jnp.concatenate(
            [jnp.where(block, sample, 0.0), jnp.where(block, field, 0.0)], axis=0
        ).astype(BF16)
        col_ref[g] = dot_nt(ones_where(iota((LANES, total), 0) == (pos & 127)), source)
        return unused

    lax.fori_loop(0, groups, group_step, 0, unroll=4)


def index_scratch(samples, id_columns, per_field, groups, shards, lines):
    fields = id_columns // per_field
    count = per_field * samples
    return [
        pltpu.VMEM((2 * LANES, lines // 2), BF16),
        pltpu.VMEM((shards * EXTRA, LANES), F32),
        pltpu.VMEM((2 * fields, count), F32),
        pltpu.VMEM((2 * fields, count), F32),
        pltpu.VMEM((2 * fields, count), F32),
        pltpu.VMEM((fields, count), F32),
        pltpu.VMEM(((fields + 1) * shards, LANES), F32),
        pltpu.VMEM((groups * shards, LANES), F32),
    ]


def sort_rows(col_ref, grads_ref, rows_scr):
    samples = grads_ref.shape[0]
    groups = col_ref.shape[0]
    blocks = col_ref.shape[2] // 2
    total = blocks * LANES
    pad = (rows_scr.shape[1] - total) // 2
    span = grads_ref.shape[1] // groups

    def sort_group(g, unused):
        col = col_ref[g]
        hots = [
            ones_where(iota((LANES, samples), 1, F32) == col[:, b : b + 1]) for b in range(blocks)
        ]
        part = grads_ref[:, pl.ds(pl.multiple_of(g * span, span), span)]
        rows = dot(jnp.concatenate(hots, axis=0), part)
        field = jnp.concatenate(
            [
                jnp.broadcast_to(col[:, blocks + b : blocks + b + 1], (LANES, LANES))
                for b in range(blocks)
            ],
            axis=0,
        )
        picked = rows[:, :LANES]
        for q in range(1, span // LANES):
            picked = jnp.where(field == float(q), rows[:, q * LANES : (q + 1) * LANES], picked)
        rows_scr[g, pad : pad + total, :] = picked
        return unused

    lax.fori_loop(0, groups, sort_group, 0)


def fill_slots(step, group, groups, off_ref, extra_ref, rows_scr, out_ref):
    slots = out_ref.shape[1] - EXTRA
    at = iota((slots, LANES), 0)

    def one(b, unused):
        owner = step * group + b
        picked = rows_scr[0, pl.ds(slots + off_ref[owner, 0], slots), :]
        for g in range(1, groups):
            start = off_ref[owner, groups + g - 1]
            rows = rows_scr[g, pl.ds(slots + off_ref[owner, g], slots), :]
            picked = jnp.where(at >= start, rows, picked)
        picked = jnp.where(at >= off_ref[owner, 2 * groups - 1], 0.0, picked)
        out_ref[b, 0:slots, :] = picked.astype(BF16)
        out_ref[b, slots : slots + EXTRA, :] = extra_ref[
            pl.ds(pl.multiple_of(owner * EXTRA, EXTRA), EXTRA), :
        ]
        return unused

    lax.fori_loop(0, group, one, 0, unroll=4)


def sum_kernel(group, got_ref, extra_ref, out_ref, picks_ref, scr, hi_scr, lo_scr, total):
    shards = extra_ref.shape[0]
    slots = got_ref.shape[1] - EXTRA
    step = pl.program_id(0)

    @pl.when(step == 0)
    def _():
        scr[...] = extra_ref[...].astype(F32).reshape(scr.shape)
        kinds = [scr[pl.ds(kind, shards, stride=EXTRA), :] for kind in range(4)]
        first, last, unused = unpack(jnp.concatenate(kinds[:3], axis=0))
        first = jnp.maximum(first, 0.0).astype(I32)
        high = (first & 15) * 32 + last.astype(I32)
        low = (first >> 4).astype(F32)
        for half in range(2):
            hi_scr[half] = high[half * shards : (half + 1) * shards]
        lo_scr[...] = low[: 2 * shards].T
        total[...] = jnp.zeros_like(total)
        picks_ref[...] = jnp.concatenate(
            [high[2 * shards :].astype(F32), low[2 * shards :]], axis=0
        ).T
        most = jnp.max(kinds[3], axis=0, keepdims=True)
        out_ref[4 * 512 :, :] = jnp.broadcast_to(most, (8, LANES))

    turned = pltpu.roll(lo_scr[...], lax.rem(2 * shards - step * group, 2 * shards), 1)
    highs, values = [], []
    for k in range(group):
        for half in range(2):
            hi = hi_scr[half, pl.ds(step * group + k, 1), :]
            highs.append(ones_where(iota((512, LANES), 0) == hi))
            low = jnp.broadcast_to(
                turned[:, half * shards + k : half * shards + k + 1], (LANES, LANES)
            )
            rows = got_ref[k, half * LANES : (half + 1) * LANES, :]
            values.append(
                jnp.concatenate([rows * ones_where(low == float(q)) for q in range(4)], axis=1)
            )
    total[...] += dot(jnp.concatenate(highs, axis=1), jnp.concatenate(values, axis=0))

    @pl.when(step == pl.num_programs(0) - 1)
    def _():
        for q in range(4):
            out_ref[q * 512 : (q + 1) * 512, :] = total[:, q * LANES : (q + 1) * LANES]


def pick_rows(count, height, high, low, wide):
    hots = [
        ones_where(iota((height, 512), 1, F32) == high[:height, b : b + 1]) for b in range(count)
    ]
    rows = dot(jnp.concatenate(hots, axis=0), wide)
    lows = jnp.concatenate(
        [jnp.broadcast_to(low[:height, b : b + 1], (height, LANES)) for b in range(count)], axis=0
    )
    picked = rows[:, :LANES]
    for q in range(1, 4):
        picked = jnp.where(lows == float(q), rows[:, q * LANES : (q + 1) * LANES], picked)
    return picked.astype(BF16)


def update_kernel(
    group, table_ref, accum_ref, one_ref, two_ref, picks_ref, rows_ref, accum_out_ref, sent_ref,
    most_ref, rows, updated, moved, wide, sems,
):
    step = pl.program_id(0)
    count = rows.shape[0]
    copies = (
        pltpu.make_async_copy(rows, rows_ref, sems.at[0]),
        pltpu.make_async_copy(updated, accum_out_ref, sems.at[1]),
    )

    @pl.when(step == 0)
    def _():
        most_ref[...] = jnp.maximum(one_ref[count:, :], two_ref[count:, :])
        gradient = one_ref[:count, :] + two_ref[:count, :]
        history = accum_ref[...] + gradient * gradient
        updated[...] = history
        rows[...] = table_ref[...] - 0.1 * gradient * lax.rsqrt(history)
        for copy in copies:
            copy.start()
        moved[...] = rows[...].astype(BF16)
        wide[...] = jnp.concatenate(
            [moved[q * 512 : (q + 1) * 512, :] for q in range(4)], axis=1
        )

    turned = pltpu.roll(picks_ref[...], lax.rem(LANES - step * group, LANES), 1)
    picked = pick_rows(group, REQ_SLOTS, turned, turned[:, LANES // 2 :], wide[...])
    sent_ref[:, :REQ_SLOTS, :] = picked.reshape(group, REQ_SLOTS, LANES)
    block = sent_ref.shape[1] - REQ_SLOTS
    start = pl.multiple_of(step * (group * block), group * block)
    sent_ref[:, REQ_SLOTS:, :] = moved[pl.ds(start, group * block), :].reshape(group, block, LANES)

    @pl.when(step == pl.num_programs(0) - 1)
    def _():
        for copy in copies:
            copy.wait()


def rank_kernel(
    group, ret_ref, mrow_ref, mcol_ref, place_ref, w_ref, b_ref, score_ref, out_ref, serving_ref,
    total, wide, weights, sem,
):
    step = pl.program_id(0)
    load = pltpu.make_async_copy(w_ref, weights, sem)

    @pl.when(step == 0)
    def _():
        load.start()
        total[...] = jnp.zeros_like(total)

    turned = pltpu.roll(mcol_ref[...], lax.rem(LANES - step * group, LANES), 1)
    hots, values = [], []
    for b in range(group):
        hots.append(
            ones_where(iota((512, LANES), 0) == mrow_ref[pl.ds(step * group + b, 1), :])
        )
        low = jnp.broadcast_to(turned[:, b : b + 1], (LANES, LANES))
        rows = ret_ref[b, :LANES, :]
        values.append(
            jnp.concatenate([rows * (1.0 - low).astype(BF16), rows * low.astype(BF16)], axis=1)
        )
    total[...] += dot(jnp.concatenate(hots, axis=1), jnp.concatenate(values, axis=0))
    wide[step] = ret_ref[:, REQ_SLOTS:, :].reshape(wide.shape[1:])

    @pl.when(step == pl.num_programs(0) - 1)
    def _():
        pooled = jnp.concatenate(
            [
                total[(f & 3) * LANES : (f & 3) * LANES + LANES, (f >> 2) * LANES : (f >> 2) * LANES + LANES]
                for f in range(8)
            ],
            axis=1,
        ).astype(BF16)
        load.wait()
        hidden = jnp.maximum(dot(pooled, weights[...]) + b_ref[...], 0.0).astype(BF16)
        out_ref[...] = dot_nt(score_ref[...], hidden)
        place = place_ref[...]
        owner, last = place >> 11, place & 31
        high = ((owner & 15) * 32 + last).astype(F32)
        zero = jnp.zeros((LANES // 2 - place.shape[0], LANES), F32)
        cols = jnp.concatenate([high, zero, (owner >> 4).astype(F32), zero], axis=0).T
        moved = jnp.concatenate([wide[q] for q in range(4)], axis=1)
        serving_ref[...] = pick_rows(
            place.shape[0], LANES, cols, cols[:, LANES // 2 :], moved
        )


def bucket_slots(targets, target_count, capacity):
    one_hot = (targets[:, None] == jnp.arange(target_count, dtype=I32)[None, :]).astype(I32)
    ranking = jnp.sum(jnp.cumsum(one_hot, axis=0) * one_hot, axis=1) - 1
    return targets * capacity + ranking


def range_scores(serving_rows, req_ids, w_hidden, b_hidden, w_score, shards, fields):
    rows_dev, width = serving_rows.shape
    requests, id_columns = req_ids.shape
    capacity = 2 * requests * id_columns // shards
    flat = req_ids.reshape(-1)
    slot = bucket_slots(flat // rows_dev, shards, capacity)
    keys = jnp.zeros((shards * capacity,), I32).at[slot].set(flat % rows_dev)
    asked = exchange(keys.reshape(shards, capacity))
    found = jnp.take(serving_rows, asked.reshape(-1), axis=0, mode="clip")
    returned = exchange(found.reshape(shards, capacity, width)).reshape(-1, width)
    rows = jnp.take(returned, slot, axis=0, mode="clip").astype(F32)
    pooled = jnp.sum(rows.reshape(requests * fields, id_columns // fields, width), axis=1)
    pooled = pooled.astype(BF16).reshape(requests, fields * width)
    hidden = jnp.dot(pooled, w_hidden, preferred_element_type=F32) + b_hidden
    return jnp.dot(jax.nn.relu(hidden).astype(BF16), w_score, preferred_element_type=F32)


def whole(shape):
    return pl.BlockSpec(shape, lambda *step: (0,) * len(shape))


def call(kernel, name, flops, moved, **kwargs):
    return pl.pallas_call(
        kernel,
        name=name,
        compiler_params=pltpu.CompilerParams(vmem_limit_bytes=VMEM_LIMIT),
        cost_estimate=pl.CostEstimate(flops=flops, bytes_accessed=moved, transcendentals=0),
        **kwargs,
    )


def in_hbm(array):
    return pltpu.with_memory_space_constraint(array, pltpu.HBM)


def exchange(rows):
    return lax.all_to_all(rows, "shard", split_axis=0, concat_axis=0, tiled=True)


def on_device(
    table_rows,
    accum,
    hash_keys,
    hash_place,
    sample_ids,
    sample_grads,
    req_ids,
    w_hidden,
    b_hidden,
    w_score,
):
    rows_dev, width = table_rows.shape
    shards = lax.axis_size("shard")
    samples, id_columns = sample_ids.shape
    requests = req_ids.shape[0]
    slots = 2 * samples * id_columns // shards
    hidden_width = w_hidden.shape[1]
    per_field = id_columns * width // sample_grads.shape[1]
    block = rows_dev // shards
    groups = 2
    sorted_rows = samples * id_columns // groups
    places = hash_place.reshape(-1, LANES)
    shape = jax.ShapeDtypeStruct
    extras = shape((shards * EXTRA, LANES), BF16)
    columns = shape((LANES, 2 * shards), F32)
    ex = pltpu.VMEM(extras.shape, F32)

    group = 16
    sent, mrow, mcol = call(
        functools.partial(send_kernel, shards, rows_dev, per_field, groups, group),
        "send",
        2**34,
        2**23,
        grid=(shards // group,),
        in_specs=[pl.BlockSpec(memory_space=pl.ANY)] * 4,
        out_specs=(
            pl.BlockSpec((group, slots + EXTRA, width), lambda g: (g, 0, 0)),
            whole((shards, LANES)),
            whole(columns.shape),
        ),
        out_shape=(
            shape((shards, slots + EXTRA, width), BF16),
            shape((shards, LANES), I32),
            columns,
        ),
        scratch_shapes=[
            pltpu.VMEM((id_columns, samples), I32),
            pltpu.VMEM(places.shape, I32),
            pltpu.VMEM((id_columns, requests), I32),
            pltpu.VMEM(sample_grads.shape, BF16),
            pltpu.VMEM((groups, LANES, 2 * sorted_rows // LANES), F32),
            pltpu.VMEM((shards, LANES), I32),
            pltpu.SMEM((shards, LANES), I32),
            pltpu.VMEM(extras.shape, BF16),
            pltpu.VMEM((groups, sorted_rows + 2 * slots, width), F32),
            pltpu.SemaphoreType.DMA((5,)),
        ]
        + index_scratch(samples, id_columns, per_field, groups, shards, places.shape[0]),
    )(*[in_hbm(array) for array in (sample_ids.T, places, req_ids.T, sample_grads)])
    got = exchange(sent)

    group = 16
    partial_sum, picks = call(
        functools.partial(sum_kernel, group),
        "gradient_sum",
        2**33,
        2**22,
        grid=(shards // group,),
        in_specs=[
            pl.BlockSpec((group, slots + EXTRA, width), lambda g: (g, 0, 0)),
            pl.BlockSpec((shards, EXTRA, width), lambda g: (0, slots // EXTRA, 0)),
        ],
        out_specs=(whole((rows_dev + 8, width)), whole(columns.shape)),
        out_shape=(shape((rows_dev + 8, width), F32), columns),
        scratch_shapes=[
            ex,
            pltpu.VMEM((2, shards, LANES), I32),
            pltpu.VMEM((LANES, LANES), F32),
            pltpu.VMEM((512, 512), F32),
        ],
    )(got, got)
    other = lax.ppermute(partial_sum, "rep", [(0, 1), (1, 0)])

    group = 32
    rows_type = shape((rows_dev, width), F32)
    any_space = pl.BlockSpec(memory_space=pl.ANY)
    new_rows, new_accum, sent, most = call(
        functools.partial(update_kernel, group),
        "update",
        2**32,
        2**23,
        grid=(shards // group,),
        in_specs=[
            whole(table_rows.shape),
            whole(accum.shape),
            whole(partial_sum.shape),
            whole(partial_sum.shape),
            whole(columns.shape),
        ],
        out_specs=(
            any_space,
            any_space,
            pl.BlockSpec((group, REQ_SLOTS + block, width), lambda g: (g, 0, 0)),
            whole((8, LANES)),
        ),
        out_shape=(
            rows_type,
            rows_type,
            pltpu.HBM((shards, REQ_SLOTS + block, width), BF16),
            shape((8, LANES), F32),
        ),
        scratch_shapes=[
            pltpu.VMEM(table_rows.shape, F32),
            pltpu.VMEM(table_rows.shape, F32),
            pltpu.VMEM(table_rows.shape, BF16),
            pltpu.VMEM((512, 512), BF16),
            pltpu.SemaphoreType.DMA((2,)),
        ],
    )(table_rows, accum, partial_sum, other, picks)
    returned = exchange(sent)

    place_rows = rows_dev // LANES
    own_places = lax.dynamic_slice_in_dim(
        places, lax.axis_index("shard") * place_rows, place_rows, axis=0
    )
    group = 16
    scores, serving_rows = call(
        functools.partial(rank_kernel, group),
        "pool_rank",
        2**32,
        2**22,
        grid=(shards // group,),
        in_specs=[
            pl.BlockSpec((group, REQ_SLOTS + block, width), lambda g: (g, 0, 0)),
            whole((shards, LANES)),
            whole(columns.shape),
            whole(own_places.shape),
            pl.BlockSpec(memory_space=pl.ANY),
            whole((1, hidden_width)),
            whole((1, hidden_width)),
        ],
        out_specs=(whole((1, requests)), whole((rows_dev, width))),
        out_shape=(pltpu.HBM((1, requests), F32), shape((rows_dev, width), BF16)),
        scratch_shapes=[
            pltpu.VMEM((512, 256), F32),
            pltpu.VMEM((4, 512, LANES), BF16),
            pltpu.VMEM(w_hidden.shape, BF16),
            pltpu.SemaphoreType.DMA,
        ],
    )(
        returned, mrow, mcol, own_places, in_hbm(w_hidden),
        b_hidden.reshape(1, -1), w_score.reshape(1, -1),
    )
    scores = lax.cond(
        most[0, 0] <= REQ_SLOTS,
        lambda: scores.reshape(requests),
        lambda: range_scores(
            serving_rows, req_ids, w_hidden, b_hidden, w_score, shards, id_columns // per_field
        ),
    )
    return (new_rows, new_accum, serving_rows, scores)


def solution(mesh):
    return jax.shard_map(
        on_device,
        mesh=mesh,
        in_specs=(
            P("shard", None),
            P("shard", None),
            P("shard"),
            P(),
            P(("rep", "shard"), None),
            P(("rep", "shard"), None),
            P(("rep", "shard"), None),
            P(),
            P(),
            P(),
        ),
        out_specs=(P("shard", None), P("shard", None), P("shard", None), P(("rep", "shard"))),
        check_vma=False,
    )
```

```python
import functools

import jax
import jax.numpy as jnp
from jax import lax
from jax.experimental import pallas as pl
from jax.experimental.pallas import tpu as pltpu
from jax.sharding import PartitionSpec as P

F32, BF16, I32 = jnp.float32, jnp.bfloat16, jnp.int32
NT = (((1,), (1,)), ((), ()))
VMEM_LIMIT = 32 * 2**20
EXTRA = 16
LANES = 128
REQ_SLOTS = 112


def iota(shape, axis, dtype=I32):
    return lax.broadcasted_iota(I32, shape, axis).astype(dtype)


def dot(a, b):
    return jnp.dot(a, b, preferred_element_type=F32)


def dot_nt(a, b):
    return lax.dot_general(a, b, NT, preferred_element_type=F32)


def ones_where(mask):
    return jnp.where(mask, 1.0, 0.0).astype(BF16)


def hot_rows(rows, index):
    short = jnp.broadcast_to(index, (16, index.shape[1])).astype(jnp.int16)
    at = lax.broadcasted_iota(jnp.int16, (rows, index.shape[1]), 0)
    match = at == jnp.concatenate([short] * (rows // 16), axis=0)
    return jnp.where(match, jnp.ones((), BF16), jnp.zeros((), BF16))


def hot_columns(column, width):
    rows = column.shape[0]
    short = jnp.broadcast_to(column, (rows, LANES)).astype(I32).astype(jnp.int16)
    at = lax.broadcasted_iota(jnp.int16, (rows, width), 1)
    match = at == jnp.concatenate([short] * (width // LANES), axis=1)
    return jnp.where(match, jnp.ones((), BF16), jnp.zeros((), BF16))


def lanes_of(ref, first, count):
    return jnp.concatenate([ref[pl.ds(first + k, 1), :] for k in range(count)], axis=1)


def rank_ids(owner, base, shards, tri, ones):
    width = tri.shape[0]
    chunks = owner.shape[1] // width
    own = jnp.where(iota((shards, owner.shape[1]), 0, F32) == owner, 1.0, 0.0)
    stacked = jnp.concatenate(
        [own[:, k * width : (k + 1) * width] for k in range(chunks)], axis=0
    ).astype(BF16)
    before = dot(stacked, tri)
    totals = dot(stacked, ones)
    ranks = []
    for k in range(chunks):
        rows = slice(k * shards, (k + 1) * shards)
        at = before[rows] + jnp.concatenate([base] * (width // LANES), axis=1)
        ranks.append(jnp.sum(own[:, k * width : (k + 1) * width] * at, axis=0, keepdims=True))
        base = base + totals[rows]
    return own, jnp.concatenate(ranks, axis=1), base


def strict_upper(width):
    return ones_where(iota((width, width), 0) < iota((width, width), 1))


def pack_places(place, shift, block):
    last = place & (block - 1)
    scale = (1 << (last & 15)).astype(F32) * jnp.where(last >= 16, 65536.0, 1.0)
    packed = ((place >> shift) + 64).astype(F32) * scale
    half = place.shape[0] // 2
    return jnp.concatenate([packed[:half].T, packed[half:].T], axis=0).astype(BF16)


def look_up(table, ids):
    count = ids.shape[1]
    lows, lines = table.shape
    line = ids >> 7
    hot = hot_rows(lines, line & (lines - 1))
    low = (ids & 127) + jnp.where(line >= lines, LANES, 0)
    found = jnp.where(iota((lows, count), 0) == low, dot(table, hot), 0.0)
    return jnp.sum(found, axis=0, keepdims=True)


def unpack(value):
    last, scale = jnp.zeros_like(value), jnp.ones_like(value)
    for bits in (16, 8, 4, 2, 1):
        big = value >= 64.0 * 2.0**bits
        value = jnp.where(big, value * 2.0**-bits, value)
        last = last + jnp.where(big, float(bits), 0.0)
        scale = jnp.where(big, scale * 2.0**bits, scale)
    return value - 64.0, last, scale


def send_kernel(
    shards, rows_dev, per_field, groups, group,
    ids_ref, place_ref, req_ref, grads_ref, out_ref, mrow_ref, mcol_ref,
    ids, places, requests, grads, col, off_vmem, off, extra, rows_scr, sems, *scratch,
):
    step = pl.program_id(0)

    @pl.when(step == 0)
    def _():
        loads = [
            pltpu.make_async_copy(source, target, sems.at[at])
            for at, (source, target) in enumerate(
                ((place_ref, places), (ids_ref, ids), (req_ref, requests), (grads_ref, grads))
            )
        ]
        for load in loads:
            load.start()
        for load in loads[:3]:
            load.wait()
        index_ids(
            shards, rows_dev, per_field, groups,
            ids, places, requests, col, off_vmem, extra, mrow_ref, mcol_ref, *scratch,
        )
        copy = pltpu.make_async_copy(off_vmem, off, sems.at[4])
        copy.start()
        loads[3].wait()
        sort_rows(col, grads, rows_scr)
        copy.wait()

    fill_slots(step, group, groups, off, extra, rows_scr, out_ref)


def index_ids(
    shards, rows_dev, per_field, groups,
    ids_ref, place_ref, req_ref, col_ref, off_ref, extra_ref, mrow_ref, mcol_ref,
    table, ex, values, owners, scales, rank_scr, mark, off_scr,
):
    shift = rows_dev.bit_length() - 1
    width = ids_ref.shape[1]
    count = per_field * width
    fields = ids_ref.shape[0] // per_field
    span = fields // groups
    batch = count // req_ref.shape[1]
    batches = req_ref.shape[0] // batch
    table[...] = pack_places(place_ref[...], shift, rows_dev // shards)
    tri = strict_upper(width)
    ones = jnp.ones((width, LANES), BF16)

    def train_look_up(c, unused):
        ids = lanes_of(ids_ref, c * per_field, per_field)
        values[pl.ds(c, 1), :] = look_up(table[...], ids)
        return unused

    def request_look_up(c, unused):
        ids = lanes_of(req_ref, c * batch, batch)
        values[pl.ds(fields + c, 1), :] = look_up(table[...], ids)
        return unused

    values[...] = jnp.zeros_like(values)
    lax.fori_loop(0, fields, train_look_up, 0, unroll=4)
    lax.fori_loop(0, batches, request_look_up, 0, unroll=4)
    owner, unused, scale = unpack(values[...])
    owners[...] = owner
    scales[...] = scale

    def packed(ids, at):
        return ((ids >> shift) + 64).astype(F32) * scales[pl.ds(at, 1), :]

    def field_step(field, carry):
        base, row = carry
        ids = lanes_of(ids_ref, field * per_field, per_field)
        mark[pl.ds(field * shards, shards), :] = base
        own, rank, base = rank_ids(owners[pl.ds(field, 1), :], base, shards, tri, ones)
        rank_scr[pl.ds(field, 1), :] = rank
        at = hot_rows(width, rank.astype(I32))
        return base, row + dot_nt((own * packed(ids, field)).astype(BF16), at)

    base, row = lax.fori_loop(
        0,
        fields,
        field_step,
        (jnp.zeros((shards, LANES), F32), jnp.zeros((shards, width), F32)),
        unroll=4,
    )
    mark[fields * shards :, :] = base

    lane = iota((1, count), 1)

    def request_step(c, carry):
        base, row = carry
        ids = lanes_of(req_ref, c * batch, batch)
        own, rank, base = rank_ids(owners[pl.ds(fields + c, 1), :], base, shards, tri, ones)
        at = hot_rows(LANES, jnp.where(rank < REQ_SLOTS, rank, -1.0).astype(I32))
        field = c * (batch // per_field) + lane // (per_field * LANES)
        digits = [
            own * packed(ids, fields + c),
            own * (lane & (LANES - 1)).astype(F32),
            own * (field + 1).astype(F32),
        ]
        return base, row + dot_nt(jnp.concatenate(digits, axis=0).astype(BF16), at)

    most, asked = lax.fori_loop(
        0,
        batches,
        request_step,
        (jnp.zeros((shards, LANES), F32), jnp.zeros((3 * shards, LANES), F32)),
        unroll=4,
    )
    most = jnp.minimum(jnp.max(most, axis=0, keepdims=True), 255.0)
    parts = [
        row[:, :LANES], row[:, LANES:], asked[:shards], jnp.broadcast_to(most, (shards, LANES))
    ]
    ex[...] = jnp.zeros_like(ex)
    for kind, part in enumerate(parts):
        ex[pl.ds(kind, shards, stride=EXTRA), :] = part
    extra_ref[...] = ex[: shards * EXTRA, :].astype(BF16)
    number = asked[2 * shards :]
    field = number.astype(I32) - 1
    mrow_ref[...] = jnp.where(
        field < 0, -1, (field & 3) * LANES + asked[shards : 2 * shards].astype(I32)
    )
    mcol_ref[...] = jnp.where(jnp.concatenate([number, number], axis=0).T > 4.0, 1.0, 0.0)

    earlier = ones_where(iota((shards, shards), 1) < iota((shards, shards), 0))
    lane = iota((shards, LANES), 1)
    table_off = jnp.zeros((shards, LANES), F32)
    for g in range(groups):
        first = mark[g * span * shards : (g * span + 1) * shards, :]
        after = mark[(g + 1) * span * shards : ((g + 1) * span + 1) * shards, :]
        off = dot(earlier, (after - first).astype(BF16)) - first
        off_scr[g * shards : (g + 1) * shards, :] = off
        table_off = jnp.where(lane == g, off, table_off)
        table_off = jnp.where(lane == groups + g, after, table_off)
    off_ref[...] = table_off.astype(I32)

    total = span * count
    blocks = total // LANES
    at = iota((1, total), 1)
    sample = (at & (width - 1)).astype(F32)
    field = (at // count).astype(F32)

    def group_step(g, unused):
        owner = lanes_of(owners, g * span, span)
        off = off_scr[pl.ds(g * shards, shards), :]
        shifts = jnp.where(
            iota((shards, total), 0, F32) == owner,
            jnp.concatenate([off] * blocks, axis=1),
            0.0,
        )
        pos = lanes_of(rank_scr, g * span, span) + jnp.sum(shifts, axis=0, keepdims=True)
        pos = pos.astype(I32)
        block = iota((blocks, total), 0) == (pos >> 7)
        source = jnp.concatenate(
            [jnp.where(block, sample, 0.0), jnp.where(block, field, 0.0)], axis=0
        ).astype(BF16)
        col_ref[g] = dot_nt(hot_rows(LANES, pos & 127), source)
        return unused

    lax.fori_loop(0, groups, group_step, 0, unroll=4)


def index_scratch(samples, id_columns, per_field, groups, shards, lines):
    fields = id_columns // per_field
    count = per_field * samples
    return [
        pltpu.VMEM((2 * LANES, lines // 2), BF16),
        pltpu.VMEM(((shards + 1) * EXTRA, LANES), F32),
        pltpu.VMEM((2 * fields, count), F32),
        pltpu.VMEM((2 * fields, count), F32),
        pltpu.VMEM((2 * fields, count), F32),
        pltpu.VMEM((fields, count), F32),
        pltpu.VMEM(((fields + 1) * shards, LANES), F32),
        pltpu.VMEM((groups * shards, LANES), F32),
    ]


def sort_rows(col_ref, grads_ref, rows_scr):
    samples = grads_ref.shape[0]
    groups = col_ref.shape[0]
    blocks = col_ref.shape[2] // 2
    total = blocks * LANES
    pad = (rows_scr.shape[1] - total) // 2
    span = grads_ref.shape[1] // groups

    def sort_group(g, unused):
        col = col_ref[g]
        hots = [
            hot_columns(col[:, b : b + 1], samples) for b in range(blocks)
        ]
        part = grads_ref[:, pl.ds(pl.multiple_of(g * span, span), span)]
        rows = dot(jnp.concatenate(hots, axis=0), part)
        field = jnp.concatenate(
            [
                jnp.broadcast_to(col[:, blocks + b : blocks + b + 1], (LANES, LANES))
                for b in range(blocks)
            ],
            axis=0,
        )
        picked = rows[:, :LANES]
        for q in range(1, span // LANES):
            picked = jnp.where(field == float(q), rows[:, q * LANES : (q + 1) * LANES], picked)
        rows_scr[g, pad : pad + total, :] = picked
        return unused

    lax.fori_loop(0, groups, sort_group, 0)


def fill_slots(step, group, groups, off_ref, extra_ref, rows_scr, out_ref):
    slots = out_ref.shape[1] - EXTRA
    at = iota((slots, LANES), 0)

    def one(b, unused):
        owner = step * group + b
        picked = rows_scr[0, pl.ds(slots + off_ref[owner, 0], slots), :]
        for g in range(1, groups):
            start = off_ref[owner, groups + g - 1]
            rows = rows_scr[g, pl.ds(slots + off_ref[owner, g], slots), :]
            picked = jnp.where(at >= start, rows, picked)
        picked = jnp.where(at >= off_ref[owner, 2 * groups - 1], 0.0, picked)
        out_ref[b, 0:slots, :] = picked.astype(BF16)
        out_ref[b, slots : slots + EXTRA, :] = extra_ref[
            pl.ds(pl.multiple_of(owner * EXTRA, EXTRA), EXTRA), :
        ]
        return unused

    lax.fori_loop(0, group, one, 0, unroll=4)


def sum_kernel(group, got_ref, extra_ref, out_ref, picks_ref, scr, hi_scr, lo_scr, total):
    shards = extra_ref.shape[0]
    slots = got_ref.shape[1] - EXTRA
    step = pl.program_id(0)

    @pl.when(step == 0)
    def _():
        scr[: shards * EXTRA, :] = extra_ref[...].astype(F32).reshape(shards * EXTRA, LANES)
        kinds = [scr[pl.ds(kind, shards, stride=EXTRA), :] for kind in range(4)]
        first, last, unused = unpack(jnp.concatenate(kinds[:3], axis=0))
        first = jnp.maximum(first, 0.0).astype(I32)
        high = (first & 15) * 32 + last.astype(I32)
        low = (first >> 4).astype(F32)
        for half in range(2):
            hi_scr[half] = high[half * shards : (half + 1) * shards]
        lo_scr[...] = low[: 2 * shards].T
        total[...] = jnp.zeros_like(total)
        picks_ref[...] = jnp.concatenate(
            [high[2 * shards :].astype(F32), low[2 * shards :]], axis=0
        ).T
        most = jnp.max(kinds[3], axis=0, keepdims=True)
        out_ref[4 * 512 :, :] = jnp.broadcast_to(most, (8, LANES))

    turned = pltpu.roll(lo_scr[...], lax.rem(2 * shards - step * group, 2 * shards), 1)
    highs, values = [], []
    for k in range(group):
        for half in range(2):
            hi = hi_scr[half, pl.ds(step * group + k, 1), :]
            highs.append(hot_rows(512, hi))
            low = turned[:, half * shards + k : half * shards + k + 1]
            low = jnp.broadcast_to(low, (LANES, LANES)).astype(I32).astype(jnp.int16)
            rows = got_ref[k, half * LANES : (half + 1) * LANES, :]
            zero = jnp.zeros((), BF16)
            values.append(
                jnp.concatenate(
                    [jnp.where(low == jnp.int16(q), rows, zero) for q in range(4)], axis=1
                )
            )
    total[...] += dot(jnp.concatenate(highs, axis=1), jnp.concatenate(values, axis=0))

    @pl.when(step == pl.num_programs(0) - 1)
    def _():
        for q in range(4):
            out_ref[q * 512 : (q + 1) * 512, :] = total[:, q * LANES : (q + 1) * LANES]


def pick_rows(count, height, high, low, wide):
    hots = [
        hot_columns(high[:height, b : b + 1], 512) for b in range(count)
    ]
    rows = dot(jnp.concatenate(hots, axis=0), wide)
    lows = jnp.concatenate(
        [jnp.broadcast_to(low[:height, b : b + 1], (height, LANES)) for b in range(count)], axis=0
    )
    picked = rows[:, :LANES]
    for q in range(1, 4):
        picked = jnp.where(lows == float(q), rows[:, q * LANES : (q + 1) * LANES], picked)
    return picked.astype(BF16)


def update_kernel(
    group, table_ref, accum_ref, one_ref, two_ref, picks_ref, rows_ref, accum_out_ref, sent_ref,
    most_ref, rows, updated, moved, wide, sems,
):
    step = pl.program_id(0)
    count = rows.shape[0]
    copies = (
        pltpu.make_async_copy(rows, rows_ref, sems.at[0]),
        pltpu.make_async_copy(updated, accum_out_ref, sems.at[1]),
    )

    @pl.when(step == 0)
    def _():
        most_ref[...] = jnp.maximum(one_ref[count:, :], two_ref[count:, :])
        gradient = one_ref[:count, :] + two_ref[:count, :]
        history = accum_ref[...] + gradient * gradient
        updated[...] = history
        rows[...] = table_ref[...] - 0.1 * gradient * lax.rsqrt(history)
        for copy in copies:
            copy.start()
        moved[...] = rows[...].astype(BF16)
        wide[...] = jnp.concatenate(
            [moved[q * 512 : (q + 1) * 512, :] for q in range(4)], axis=1
        )

    turned = pltpu.roll(picks_ref[...], lax.rem(LANES - step * group, LANES), 1)
    picked = pick_rows(group, REQ_SLOTS, turned, turned[:, LANES // 2 :], wide[...])
    sent_ref[:, :REQ_SLOTS, :] = picked.reshape(group, REQ_SLOTS, LANES)
    block = sent_ref.shape[1] - REQ_SLOTS
    start = pl.multiple_of(step * (group * block), group * block)
    sent_ref[:, REQ_SLOTS:, :] = moved[pl.ds(start, group * block), :].reshape(group, block, LANES)

    @pl.when(step == pl.num_programs(0) - 1)
    def _():
        for copy in copies:
            copy.wait()


def rank_kernel(
    group, ret_ref, mrow_ref, mcol_ref, place_ref, w_ref, b_ref, score_ref, out_ref, serving_ref,
    total, wide, weights, sem,
):
    step = pl.program_id(0)
    load = pltpu.make_async_copy(w_ref, weights, sem)

    @pl.when(step == 0)
    def _():
        load.start()
        total[...] = jnp.zeros_like(total)

    turned = pltpu.roll(mcol_ref[...], lax.rem(LANES - step * group, LANES), 1)
    hots, values = [], []
    for b in range(group):
        hots.append(
            hot_rows(512, mrow_ref[pl.ds(step * group + b, 1), :])
        )
        low = jnp.broadcast_to(turned[:, b : b + 1], (LANES, LANES)).astype(I32).astype(jnp.int16)
        rows = ret_ref[b, :LANES, :]
        zero = jnp.zeros((), BF16)
        values.append(
            jnp.concatenate([jnp.where(low == jnp.int16(q), rows, zero) for q in range(2)], axis=1)
        )
    total[...] += dot(jnp.concatenate(hots, axis=1), jnp.concatenate(values, axis=0))
    wide[step] = ret_ref[:, REQ_SLOTS:, :].reshape(wide.shape[1:])

    @pl.when(step == pl.num_programs(0) - 1)
    def _():
        pooled = jnp.concatenate(
            [
                total[(f & 3) * LANES : (f & 3) * LANES + LANES, (f >> 2) * LANES : (f >> 2) * LANES + LANES]
                for f in range(8)
            ],
            axis=1,
        ).astype(BF16)
        load.wait()
        hidden = jnp.maximum(dot(pooled, weights[...]) + b_ref[...], 0.0).astype(BF16)
        out_ref[...] = dot_nt(score_ref[...], hidden)
        place = place_ref[...]
        owner, last = place >> 11, place & 31
        high = ((owner & 15) * 32 + last).astype(F32)
        zero = jnp.zeros((LANES // 2 - place.shape[0], LANES), F32)
        cols = jnp.concatenate([high, zero, (owner >> 4).astype(F32), zero], axis=0).T
        moved = jnp.concatenate([wide[q // 2, (q % 2) * 512 : (q % 2) * 512 + 512] for q in range(4)], axis=1)
        serving_ref[...] = pick_rows(
            place.shape[0], LANES, cols, cols[:, LANES // 2 :], moved
        )


def bucket_slots(targets, target_count, capacity):
    one_hot = (targets[:, None] == jnp.arange(target_count, dtype=I32)[None, :]).astype(I32)
    ranking = jnp.sum(jnp.cumsum(one_hot, axis=0) * one_hot, axis=1) - 1
    return targets * capacity + ranking


def range_scores(serving_rows, req_ids, w_hidden, b_hidden, w_score, shards, fields):
    rows_dev, width = serving_rows.shape
    requests, id_columns = req_ids.shape
    capacity = 2 * requests * id_columns // shards
    flat = req_ids.reshape(-1)
    slot = bucket_slots(flat // rows_dev, shards, capacity)
    keys = jnp.zeros((shards * capacity,), I32).at[slot].set(flat % rows_dev)
    asked = exchange(keys.reshape(shards, capacity))
    found = jnp.take(serving_rows, asked.reshape(-1), axis=0, mode="clip")
    returned = exchange(found.reshape(shards, capacity, width)).reshape(-1, width)
    rows = jnp.take(returned, slot, axis=0, mode="clip").astype(F32)
    pooled = jnp.sum(rows.reshape(requests * fields, id_columns // fields, width), axis=1)
    pooled = pooled.astype(BF16).reshape(requests, fields * width)
    hidden = jnp.dot(pooled, w_hidden, preferred_element_type=F32) + b_hidden
    return jnp.dot(jax.nn.relu(hidden).astype(BF16), w_score, preferred_element_type=F32)


def whole(shape):
    return pl.BlockSpec(shape, lambda *step: (0,) * len(shape))


def call(kernel, name, flops, moved, **kwargs):
    return pl.pallas_call(
        kernel,
        name=name,
        compiler_params=pltpu.CompilerParams(vmem_limit_bytes=VMEM_LIMIT),
        cost_estimate=pl.CostEstimate(flops=flops, bytes_accessed=moved, transcendentals=0),
        **kwargs,
    )


def in_hbm(array):
    return pltpu.with_memory_space_constraint(array, pltpu.HBM)


def exchange(rows):
    return lax.all_to_all(rows, "shard", split_axis=0, concat_axis=0, tiled=True)


def on_device(
    table_rows,
    accum,
    hash_keys,
    hash_place,
    sample_ids,
    sample_grads,
    req_ids,
    w_hidden,
    b_hidden,
    w_score,
):
    rows_dev, width = table_rows.shape
    shards = lax.axis_size("shard")
    samples, id_columns = sample_ids.shape
    requests = req_ids.shape[0]
    slots = 2 * samples * id_columns // shards
    hidden_width = w_hidden.shape[1]
    per_field = id_columns * width // sample_grads.shape[1]
    block = rows_dev // shards
    groups = 2
    sorted_rows = samples * id_columns // groups
    places = hash_place.reshape(-1, LANES)
    shape = jax.ShapeDtypeStruct
    extras = shape((shards * EXTRA, LANES), BF16)
    columns = shape((LANES, 2 * shards), F32)
    ex = pltpu.VMEM(((shards + 1) * EXTRA, LANES), F32)

    group = 16
    sent, mrow, mcol = call(
        functools.partial(send_kernel, shards, rows_dev, per_field, groups, group),
        "send",
        2**34,
        2**23,
        grid=(shards // group,),
        in_specs=[pl.BlockSpec(memory_space=pl.ANY)] * 4,
        out_specs=(
            pl.BlockSpec((group, slots + EXTRA, width), lambda g: (g, 0, 0)),
            whole((shards, LANES)),
            whole(columns.shape),
        ),
        out_shape=(
            shape((shards, slots + EXTRA, width), BF16),
            shape((shards, LANES), I32),
            columns,
        ),
        scratch_shapes=[
            pltpu.VMEM((id_columns, samples), I32),
            pltpu.VMEM(places.shape, I32),
            pltpu.VMEM((id_columns, requests), I32),
            pltpu.VMEM(sample_grads.shape, BF16),
            pltpu.VMEM((groups, LANES, 2 * sorted_rows // LANES), F32),
            pltpu.VMEM((shards, LANES), I32),
            pltpu.SMEM((shards, LANES), I32),
            pltpu.VMEM(extras.shape, BF16),
            pltpu.VMEM((groups, sorted_rows + 2 * slots, width), F32),
            pltpu.SemaphoreType.DMA((5,)),
        ]
        + index_scratch(samples, id_columns, per_field, groups, shards, places.shape[0]),
    )(*[in_hbm(array) for array in (sample_ids.T, places, req_ids.T, sample_grads)])
    got = exchange(sent)

    group = 32
    partial_sum, picks = call(
        functools.partial(sum_kernel, group),
        "gradient_sum",
        2**33,
        2**22,
        grid=(shards // group,),
        in_specs=[
            pl.BlockSpec((group, slots + EXTRA, width), lambda g: (g, 0, 0)),
            pl.BlockSpec((shards, EXTRA, width), lambda g: (0, slots // EXTRA, 0)),
        ],
        out_specs=(whole((rows_dev + 8, width)), whole(columns.shape)),
        out_shape=(shape((rows_dev + 8, width), F32), columns),
        scratch_shapes=[
            ex,
            pltpu.VMEM((2, shards, LANES), I32),
            pltpu.VMEM((LANES, LANES), F32),
            pltpu.VMEM((512, 512), F32),
        ],
    )(got, got)
    other = lax.ppermute(partial_sum, "rep", [(0, 1), (1, 0)])

    group = 64
    rows_type = shape((rows_dev, width), F32)
    any_space = pl.BlockSpec(memory_space=pl.ANY)
    new_rows, new_accum, sent, most = call(
        functools.partial(update_kernel, group),
        "update",
        2**32,
        2**23,
        grid=(shards // group,),
        in_specs=[
            whole(table_rows.shape),
            whole(accum.shape),
            whole(partial_sum.shape),
            whole(partial_sum.shape),
            whole(columns.shape),
        ],
        out_specs=(
            any_space,
            any_space,
            pl.BlockSpec((group, REQ_SLOTS + block, width), lambda g: (g, 0, 0)),
            whole((8, LANES)),
        ),
        out_shape=(
            rows_type,
            rows_type,
            pltpu.HBM((shards, REQ_SLOTS + block, width), BF16),
            shape((8, LANES), F32),
        ),
        scratch_shapes=[
            pltpu.VMEM(table_rows.shape, F32),
            pltpu.VMEM(table_rows.shape, F32),
            pltpu.VMEM(table_rows.shape, BF16),
            pltpu.VMEM((512, 512), BF16),
            pltpu.SemaphoreType.DMA((2,)),
        ],
    )(table_rows, accum, partial_sum, other, picks)
    returned = exchange(sent)

    place_rows = rows_dev // LANES
    own_places = lax.dynamic_slice_in_dim(
        places, lax.axis_index("shard") * place_rows, place_rows, axis=0
    )
    group = 32
    scores, serving_rows = call(
        functools.partial(rank_kernel, group),
        "pool_rank",
        2**32,
        2**22,
        grid=(shards // group,),
        in_specs=[
            pl.BlockSpec((group, REQ_SLOTS + block, width), lambda g: (g, 0, 0)),
            whole((shards, LANES)),
            whole(columns.shape),
            whole(own_places.shape),
            pl.BlockSpec(memory_space=pl.ANY),
            whole((1, hidden_width)),
            whole((1, hidden_width)),
        ],
        out_specs=(whole((1, requests)), whole((rows_dev, width))),
        out_shape=(pltpu.HBM((1, requests), F32), shape((rows_dev, width), BF16)),
        scratch_shapes=[
            pltpu.VMEM((512, 256), F32),
            pltpu.VMEM((2, 1024, LANES), BF16),
            pltpu.VMEM(w_hidden.shape, BF16),
            pltpu.SemaphoreType.DMA,
        ],
    )(
        returned, mrow, mcol, own_places, in_hbm(w_hidden),
        b_hidden.reshape(1, -1), w_score.reshape(1, -1),
    )
    scores = lax.cond(
        most[0, 0] <= REQ_SLOTS,
        lambda: scores.reshape(requests),
        lambda: range_scores(
            serving_rows, req_ids, w_hidden, b_hidden, w_score, shards, id_columns // per_field
        ),
    )
    return (new_rows, new_accum, serving_rows, scores)


def solution(mesh):
    return jax.shard_map(
        on_device,
        mesh=mesh,
        in_specs=(
            P("shard", None),
            P("shard", None),
            P("shard"),
            P(),
            P(("rep", "shard"), None),
            P(("rep", "shard"), None),
            P(("rep", "shard"), None),
            P(),
            P(),
            P(),
        ),
        out_specs=(P("shard", None), P("shard", None), P("shard", None), P(("rep", "shard"))),
        check_vma=False,
    )
```

```python
import functools

import jax
import jax.numpy as jnp
from jax import lax
from jax.experimental import pallas as pl
from jax.experimental.pallas import tpu as pltpu
from jax.sharding import PartitionSpec as P

F32, BF16, I32 = jnp.float32, jnp.bfloat16, jnp.int32
NT = (((1,), (1,)), ((), ()))
VMEM_LIMIT = 32 * 2**20
EXTRA = 16
LANES = 128
REQ_SLOTS = 112


def iota(shape, axis, dtype=I32):
    return lax.broadcasted_iota(I32, shape, axis).astype(dtype)


def dot(a, b):
    return jnp.dot(a, b, preferred_element_type=F32)


def dot_nt(a, b):
    return lax.dot_general(a, b, NT, preferred_element_type=F32)


def ones_where(mask):
    return jnp.where(mask, 1.0, 0.0).astype(BF16)


def hot_rows(rows, index):
    short = jnp.broadcast_to(index, (16, index.shape[1])).astype(jnp.int16)
    at = lax.broadcasted_iota(jnp.int16, (rows, index.shape[1]), 0)
    match = at == jnp.concatenate([short] * (rows // 16), axis=0)
    return jnp.where(match, jnp.ones((), BF16), jnp.zeros((), BF16))


def hot_columns(column, width):
    rows = column.shape[0]
    short = jnp.broadcast_to(column, (rows, LANES)).astype(I32).astype(jnp.int16)
    at = lax.broadcasted_iota(jnp.int16, (rows, width), 1)
    match = at == jnp.concatenate([short] * (width // LANES), axis=1)
    return jnp.where(match, jnp.ones((), BF16), jnp.zeros((), BF16))


def lanes_of(ref, first, count):
    return jnp.concatenate([ref[pl.ds(first + k, 1), :] for k in range(count)], axis=1)


def rank_ids(owner, base, shards, tri, ones):
    width = tri.shape[0]
    chunks = owner.shape[1] // width
    own = jnp.where(iota((shards, owner.shape[1]), 0, F32) == owner, 1.0, 0.0)
    stacked = jnp.concatenate(
        [own[:, k * width : (k + 1) * width] for k in range(chunks)], axis=0
    ).astype(BF16)
    before = dot(stacked, tri)
    totals = dot(stacked, ones)
    ranks = []
    for k in range(chunks):
        rows = slice(k * shards, (k + 1) * shards)
        at = before[rows] + jnp.concatenate([base] * (width // LANES), axis=1)
        ranks.append(jnp.sum(own[:, k * width : (k + 1) * width] * at, axis=0, keepdims=True))
        base = base + totals[rows]
    return own, jnp.concatenate(ranks, axis=1), base


def strict_upper(width):
    return ones_where(iota((width, width), 0) < iota((width, width), 1))


def pack_places(place, shift, block):
    last = place & (block - 1)
    scale = (1 << (last & 15)).astype(F32) * jnp.where(last >= 16, 65536.0, 1.0)
    packed = ((place >> shift) + 64).astype(F32) * scale
    half = place.shape[0] // 2
    return jnp.concatenate([packed[:half].T, packed[half:].T], axis=0).astype(BF16)


def look_up(table, ids):
    count = ids.shape[1]
    lows, lines = table.shape
    line = ids >> 7
    hot = hot_rows(lines, line & (lines - 1))
    low = (ids & 127) + jnp.where(line >= lines, LANES, 0)
    found = jnp.where(iota((lows, count), 0) == low, dot(table, hot), 0.0)
    return jnp.sum(found, axis=0, keepdims=True)


def unpack(value):
    last, scale = jnp.zeros_like(value), jnp.ones_like(value)
    for bits in (16, 8, 4, 2, 1):
        big = value >= 64.0 * 2.0**bits
        value = jnp.where(big, value * 2.0**-bits, value)
        last = last + jnp.where(big, float(bits), 0.0)
        scale = jnp.where(big, scale * 2.0**bits, scale)
    return value - 64.0, last, scale


def send_kernel(
    shards, rows_dev, per_field, groups, group,
    ids_ref, place_ref, req_ref, grads_ref, out_ref, mrow_ref, mcol_ref,
    ids, places, requests, grads, col, off_vmem, off, extra, rows_scr, sems, *scratch,
):
    step = pl.program_id(0)

    @pl.when(step == 0)
    def _():
        loads = [
            pltpu.make_async_copy(source, target, sems.at[at])
            for at, (source, target) in enumerate(
                ((place_ref, places), (ids_ref, ids), (req_ref, requests), (grads_ref, grads))
            )
        ]
        for load in loads:
            load.start()
        for load in loads[:3]:
            load.wait()
        index_ids(
            shards, rows_dev, per_field, groups,
            ids, places, requests, col, off_vmem, extra, mrow_ref, mcol_ref, *scratch,
        )
        copy = pltpu.make_async_copy(off_vmem, off, sems.at[4])
        copy.start()
        loads[3].wait()
        sort_rows(col, grads, rows_scr)
        copy.wait()

    fill_slots(step, group, groups, off, extra, rows_scr, out_ref)


def index_ids(
    shards, rows_dev, per_field, groups,
    ids_ref, place_ref, req_ref, col_ref, off_ref, extra_ref, mrow_ref, mcol_ref,
    table, ex, values, owners, scales, rank_scr, mark, off_scr,
):
    shift = rows_dev.bit_length() - 1
    width = ids_ref.shape[1]
    count = per_field * width
    fields = ids_ref.shape[0] // per_field
    span = fields // groups
    batch = count // req_ref.shape[1]
    batches = req_ref.shape[0] // batch
    table[...] = pack_places(place_ref[...], shift, rows_dev // shards)
    tri = strict_upper(width)
    ones = jnp.ones((width, LANES), BF16)

    def train_look_up(c, unused):
        ids = lanes_of(ids_ref, c * per_field, per_field)
        values[pl.ds(c, 1), :] = look_up(table[...], ids)
        return unused

    def request_look_up(c, unused):
        ids = lanes_of(req_ref, c * batch, batch)
        values[pl.ds(fields + c, 1), :] = look_up(table[...], ids)
        return unused

    values[...] = jnp.zeros_like(values)
    lax.fori_loop(0, fields, train_look_up, 0, unroll=8)
    lax.fori_loop(0, batches, request_look_up, 0, unroll=4)
    owner, unused, scale = unpack(values[...])
    owners[...] = owner
    scales[...] = scale

    def packed(ids, at):
        return ((ids >> shift) + 64).astype(F32) * scales[pl.ds(at, 1), :]

    def field_step(field, carry):
        base, row = carry
        ids = lanes_of(ids_ref, field * per_field, per_field)
        mark[pl.ds(field * shards, shards), :] = base
        own, rank, base = rank_ids(owners[pl.ds(field, 1), :], base, shards, tri, ones)
        rank_scr[pl.ds(field, 1), :] = rank
        at = hot_rows(width, rank.astype(I32))
        digits = (own * packed(ids, field)).astype(BF16)
        return base, row + dot_nt(at, jnp.concatenate([digits, digits], axis=0))

    base, row = lax.fori_loop(
        0,
        fields,
        field_step,
        (jnp.zeros((shards, LANES), F32), jnp.zeros((width, 2 * shards), F32)),
        unroll=8,
    )
    mark[fields * shards :, :] = base
    row = row.T[:shards]

    lane = iota((1, count), 1)

    def request_step(c, carry):
        base, row = carry
        ids = lanes_of(req_ref, c * batch, batch)
        own, rank, base = rank_ids(owners[pl.ds(fields + c, 1), :], base, shards, tri, ones)
        at = hot_rows(LANES, jnp.where(rank < REQ_SLOTS, rank, -1.0).astype(I32))
        field = c * (batch // per_field) + lane // (per_field * LANES)
        digits = [
            own * packed(ids, fields + c),
            own * (lane & (LANES - 1)).astype(F32),
            own * (field + 1).astype(F32),
        ]
        return base, row + dot_nt(jnp.concatenate(digits, axis=0).astype(BF16), at)

    most, asked = lax.fori_loop(
        0,
        batches,
        request_step,
        (jnp.zeros((shards, LANES), F32), jnp.zeros((3 * shards, LANES), F32)),
        unroll=4,
    )
    most = jnp.minimum(jnp.max(most, axis=0, keepdims=True), 255.0)
    parts = [
        row[:, :LANES], row[:, LANES:], asked[:shards], jnp.broadcast_to(most, (shards, LANES))
    ]
    ex[...] = jnp.zeros_like(ex)
    for kind, part in enumerate(parts):
        ex[pl.ds(kind, shards, stride=EXTRA), :] = part
    extra_ref[...] = ex[: shards * EXTRA, :].astype(BF16)
    number = asked[2 * shards :]
    field = number.astype(I32) - 1
    mrow_ref[...] = jnp.where(
        field < 0, -1, (field & 3) * LANES + asked[shards : 2 * shards].astype(I32)
    )
    mcol_ref[...] = jnp.where(jnp.concatenate([number, number], axis=0).T > 4.0, 1.0, 0.0)

    earlier = ones_where(iota((shards, shards), 1) < iota((shards, shards), 0))
    lane = iota((shards, LANES), 1)
    table_off = jnp.zeros((shards, LANES), F32)
    for g in range(groups):
        first = mark[g * span * shards : (g * span + 1) * shards, :]
        after = mark[(g + 1) * span * shards : ((g + 1) * span + 1) * shards, :]
        off = dot(earlier, (after - first).astype(BF16)) - first
        off_scr[g * shards : (g + 1) * shards, :] = off
        table_off = jnp.where(lane == g, off, table_off)
        table_off = jnp.where(lane == groups + g, after, table_off)
    off_ref[...] = table_off.astype(I32)

    total = span * count
    blocks = total // LANES
    at = iota((1, total), 1)
    sample = (at & (width - 1)).astype(F32)
    field = (at // count).astype(F32)

    def group_step(g, unused):
        owner = lanes_of(owners, g * span, span)
        off = off_scr[pl.ds(g * shards, shards), :]
        shifts = jnp.where(
            iota((shards, total), 0, F32) == owner,
            jnp.concatenate([off] * blocks, axis=1),
            0.0,
        )
        pos = lanes_of(rank_scr, g * span, span) + jnp.sum(shifts, axis=0, keepdims=True)
        pos = pos.astype(I32)
        block = iota((blocks, total), 0) == (pos >> 7)
        source = jnp.concatenate(
            [jnp.where(block, sample, 0.0), jnp.where(block, field, 0.0)], axis=0
        ).astype(BF16)
        col_ref[g] = dot_nt(hot_rows(LANES, pos & 127), source)
        return unused

    lax.fori_loop(0, groups, group_step, 0, unroll=4)


def index_scratch(samples, id_columns, per_field, groups, shards, lines):
    fields = id_columns // per_field
    count = per_field * samples
    return [
        pltpu.VMEM((2 * LANES, lines // 2), BF16),
        pltpu.VMEM(((shards + 1) * EXTRA, LANES), F32),
        pltpu.VMEM((2 * fields, count), F32),
        pltpu.VMEM((2 * fields, count), F32),
        pltpu.VMEM((2 * fields, count), F32),
        pltpu.VMEM((fields, count), F32),
        pltpu.VMEM(((fields + 1) * shards, LANES), F32),
        pltpu.VMEM((groups * shards, LANES), F32),
    ]


def sort_rows(col_ref, grads_ref, rows_scr):
    samples = grads_ref.shape[0]
    groups = col_ref.shape[0]
    blocks = col_ref.shape[2] // 2
    total = blocks * LANES
    pad = (rows_scr.shape[1] - total) // 2
    span = grads_ref.shape[1] // groups

    def sort_group(g, unused):
        col = col_ref[g]
        hots = [
            hot_columns(col[:, b : b + 1], samples) for b in range(blocks)
        ]
        part = grads_ref[:, pl.ds(pl.multiple_of(g * span, span), span)]
        rows = dot(jnp.concatenate(hots, axis=0), part)
        field = jnp.concatenate(
            [
                jnp.broadcast_to(col[:, blocks + b : blocks + b + 1], (LANES, LANES))
                for b in range(blocks)
            ],
            axis=0,
        )
        picked = rows[:, :LANES]
        for q in range(1, span // LANES):
            picked = jnp.where(field == float(q), rows[:, q * LANES : (q + 1) * LANES], picked)
        rows_scr[g, pad : pad + total, :] = picked
        return unused

    lax.fori_loop(0, groups, sort_group, 0, unroll=2)


def fill_slots(step, group, groups, off_ref, extra_ref, rows_scr, out_ref):
    slots = out_ref.shape[1] - EXTRA
    at = iota((slots, LANES), 0)

    def one(b, unused):
        owner = step * group + b
        picked = rows_scr[0, pl.ds(slots + off_ref[owner, 0], slots), :]
        for g in range(1, groups):
            start = off_ref[owner, groups + g - 1]
            rows = rows_scr[g, pl.ds(slots + off_ref[owner, g], slots), :]
            picked = jnp.where(at >= start, rows, picked)
        picked = jnp.where(at >= off_ref[owner, 2 * groups - 1], 0.0, picked)
        out_ref[b, 0:slots, :] = picked.astype(BF16)
        out_ref[b, slots : slots + EXTRA, :] = extra_ref[
            pl.ds(pl.multiple_of(owner * EXTRA, EXTRA), EXTRA), :
        ]
        return unused

    lax.fori_loop(0, group, one, 0, unroll=4)


def sum_kernel(group, got_ref, extra_ref, out_ref, picks_ref, scr, hi_scr, lo_scr, total):
    shards = extra_ref.shape[0]
    slots = got_ref.shape[1] - EXTRA
    step = pl.program_id(0)

    @pl.when(step == 0)
    def _():
        scr[: shards * EXTRA, :] = extra_ref[...].astype(F32).reshape(shards * EXTRA, LANES)
        kinds = [scr[pl.ds(kind, shards, stride=EXTRA), :] for kind in range(4)]
        first, last, unused = unpack(jnp.concatenate(kinds[:3], axis=0))
        first = jnp.maximum(first, 0.0).astype(I32)
        high = (first & 15) * 32 + last.astype(I32)
        low = (first >> 4).astype(F32)
        for half in range(2):
            hi_scr[half] = high[half * shards : (half + 1) * shards]
        lo_scr[...] = low[: 2 * shards].T
        total[...] = jnp.zeros_like(total)
        picks_ref[...] = jnp.concatenate(
            [high[2 * shards :].astype(F32), low[2 * shards :]], axis=0
        ).T
        most = jnp.max(kinds[3], axis=0, keepdims=True)
        out_ref[4 * 512 :, :] = jnp.broadcast_to(most, (8, LANES))

    turned = pltpu.roll(lo_scr[...], lax.rem(2 * shards - step * group, 2 * shards), 1)
    highs, values = [], []
    for k in range(group):
        for half in range(2):
            hi = hi_scr[half, pl.ds(step * group + k, 1), :]
            highs.append(hot_rows(512, hi))
            low = turned[:, half * shards + k : half * shards + k + 1]
            low = jnp.broadcast_to(low, (LANES, LANES)).astype(I32).astype(jnp.int16)
            rows = got_ref[k, half * LANES : (half + 1) * LANES, :]
            zero = jnp.zeros((), BF16)
            values.append(
                jnp.concatenate(
                    [jnp.where(low == jnp.int16(q), rows, zero) for q in range(4)], axis=1
                )
            )
    total[...] += dot(jnp.concatenate(highs, axis=1), jnp.concatenate(values, axis=0))

    @pl.when(step == pl.num_programs(0) - 1)
    def _():
        for q in range(4):
            out_ref[q * 512 : (q + 1) * 512, :] = total[:, q * LANES : (q + 1) * LANES]


def pick_rows(count, height, high, low, wide):
    hots = [
        hot_columns(high[:height, b : b + 1], 512) for b in range(count)
    ]
    rows = dot(jnp.concatenate(hots, axis=0), wide)
    lows = jnp.concatenate(
        [jnp.broadcast_to(low[:height, b : b + 1], (height, LANES)) for b in range(count)], axis=0
    )
    picked = rows[:, :LANES]
    for q in range(1, 4):
        picked = jnp.where(lows == float(q), rows[:, q * LANES : (q + 1) * LANES], picked)
    return picked.astype(BF16)


def update_kernel(
    group, table_ref, accum_ref, one_ref, two_ref, picks_ref, rows_ref, accum_out_ref, sent_ref,
    most_ref, rows, updated, moved, wide, sems,
):
    step = pl.program_id(0)
    count = rows.shape[0]
    copies = (
        pltpu.make_async_copy(rows, rows_ref, sems.at[0]),
        pltpu.make_async_copy(updated, accum_out_ref, sems.at[1]),
    )

    @pl.when(step == 0)
    def _():
        most_ref[...] = jnp.maximum(one_ref[count:, :], two_ref[count:, :])
        gradient = one_ref[:count, :] + two_ref[:count, :]
        history = accum_ref[...] + gradient * gradient
        updated[...] = history
        rows[...] = table_ref[...] - 0.1 * gradient * lax.rsqrt(history)
        for copy in copies:
            copy.start()
        moved[...] = rows[...].astype(BF16)
        wide[...] = jnp.concatenate(
            [moved[q * 512 : (q + 1) * 512, :] for q in range(4)], axis=1
        )

    turned = pltpu.roll(picks_ref[...], lax.rem(LANES - step * group, LANES), 1)
    picked = pick_rows(group, REQ_SLOTS, turned, turned[:, LANES // 2 :], wide[...])
    sent_ref[:, :REQ_SLOTS, :] = picked.reshape(group, REQ_SLOTS, LANES)
    block = sent_ref.shape[1] - REQ_SLOTS
    start = pl.multiple_of(step * (group * block), group * block)
    sent_ref[:, REQ_SLOTS:, :] = moved[pl.ds(start, group * block), :].reshape(group, block, LANES)

    @pl.when(step == pl.num_programs(0) - 1)
    def _():
        for copy in copies:
            copy.wait()


def rank_kernel(
    group, ret_ref, mrow_ref, mcol_ref, place_ref, w_ref, b_ref, score_ref, out_ref, serving_ref,
    total, wide, weights, sem,
):
    step = pl.program_id(0)
    load = pltpu.make_async_copy(w_ref, weights, sem)

    @pl.when(step == 0)
    def _():
        load.start()
        total[...] = jnp.zeros_like(total)

    turned = pltpu.roll(mcol_ref[...], lax.rem(LANES - step * group, LANES), 1)
    hots, values = [], []
    for b in range(group):
        hots.append(
            hot_rows(512, mrow_ref[pl.ds(step * group + b, 1), :])
        )
        low = jnp.broadcast_to(turned[:, b : b + 1], (LANES, LANES)).astype(I32).astype(jnp.int16)
        rows = ret_ref[b, :LANES, :]
        zero = jnp.zeros((), BF16)
        values.append(
            jnp.concatenate([jnp.where(low == jnp.int16(q), rows, zero) for q in range(2)], axis=1)
        )
    total[...] += dot(jnp.concatenate(hots, axis=1), jnp.concatenate(values, axis=0))
    wide[step] = ret_ref[:, REQ_SLOTS:, :].reshape(wide.shape[1:])

    @pl.when(step == pl.num_programs(0) - 1)
    def _():
        pooled = jnp.concatenate(
            [
                total[(f & 3) * LANES : (f & 3) * LANES + LANES, (f >> 2) * LANES : (f >> 2) * LANES + LANES]
                for f in range(8)
            ],
            axis=1,
        ).astype(BF16)
        load.wait()
        hidden = jnp.maximum(dot(pooled, weights[...]) + b_ref[...], 0.0).astype(BF16)
        out_ref[...] = dot_nt(score_ref[...], hidden)
        place = place_ref[...]
        owner, last = place >> 11, place & 31
        high = ((owner & 15) * 32 + last).astype(F32)
        zero = jnp.zeros((LANES // 2 - place.shape[0], LANES), F32)
        cols = jnp.concatenate([high, zero, (owner >> 4).astype(F32), zero], axis=0).T
        moved = jnp.concatenate([wide[q // 2, (q % 2) * 512 : (q % 2) * 512 + 512] for q in range(4)], axis=1)
        serving_ref[...] = pick_rows(
            place.shape[0], LANES, cols, cols[:, LANES // 2 :], moved
        )


def bucket_slots(targets, target_count, capacity):
    one_hot = (targets[:, None] == jnp.arange(target_count, dtype=I32)[None, :]).astype(I32)
    ranking = jnp.sum(jnp.cumsum(one_hot, axis=0) * one_hot, axis=1) - 1
    return targets * capacity + ranking


def range_scores(serving_rows, req_ids, w_hidden, b_hidden, w_score, shards, fields):
    rows_dev, width = serving_rows.shape
    requests, id_columns = req_ids.shape
    capacity = 2 * requests * id_columns // shards
    flat = req_ids.reshape(-1)
    slot = bucket_slots(flat // rows_dev, shards, capacity)
    keys = jnp.zeros((shards * capacity,), I32).at[slot].set(flat % rows_dev)
    asked = exchange(keys.reshape(shards, capacity))
    found = jnp.take(serving_rows, asked.reshape(-1), axis=0, mode="clip")
    returned = exchange(found.reshape(shards, capacity, width)).reshape(-1, width)
    rows = jnp.take(returned, slot, axis=0, mode="clip").astype(F32)
    pooled = jnp.sum(rows.reshape(requests * fields, id_columns // fields, width), axis=1)
    pooled = pooled.astype(BF16).reshape(requests, fields * width)
    hidden = jnp.dot(pooled, w_hidden, preferred_element_type=F32) + b_hidden
    return jnp.dot(jax.nn.relu(hidden).astype(BF16), w_score, preferred_element_type=F32)


def whole(shape):
    return pl.BlockSpec(shape, lambda *step: (0,) * len(shape))


def call(kernel, name, flops, moved, **kwargs):
    return pl.pallas_call(
        kernel,
        name=name,
        compiler_params=pltpu.CompilerParams(vmem_limit_bytes=VMEM_LIMIT),
        cost_estimate=pl.CostEstimate(flops=flops, bytes_accessed=moved, transcendentals=0),
        **kwargs,
    )


def in_hbm(array):
    return pltpu.with_memory_space_constraint(array, pltpu.HBM)


def exchange(rows):
    return lax.all_to_all(rows, "shard", split_axis=0, concat_axis=0, tiled=True)


def on_device(
    table_rows,
    accum,
    hash_keys,
    hash_place,
    sample_ids,
    sample_grads,
    req_ids,
    w_hidden,
    b_hidden,
    w_score,
):
    rows_dev, width = table_rows.shape
    shards = lax.axis_size("shard")
    samples, id_columns = sample_ids.shape
    requests = req_ids.shape[0]
    slots = 2 * samples * id_columns // shards
    hidden_width = w_hidden.shape[1]
    per_field = id_columns * width // sample_grads.shape[1]
    block = rows_dev // shards
    groups = 2
    sorted_rows = samples * id_columns // groups
    places = hash_place.reshape(-1, LANES)
    shape = jax.ShapeDtypeStruct
    extras = shape((shards * EXTRA, LANES), BF16)
    columns = shape((LANES, 2 * shards), F32)
    ex = pltpu.VMEM(((shards + 1) * EXTRA, LANES), F32)

    group = 16
    sent, mrow, mcol = call(
        functools.partial(send_kernel, shards, rows_dev, per_field, groups, group),
        "send",
        2**34,
        2**23,
        grid=(shards // group,),
        in_specs=[pl.BlockSpec(memory_space=pl.ANY)] * 4,
        out_specs=(
            pl.BlockSpec((group, slots + EXTRA, width), lambda g: (g, 0, 0)),
            whole((shards, LANES)),
            whole(columns.shape),
        ),
        out_shape=(
            shape((shards, slots + EXTRA, width), BF16),
            shape((shards, LANES), I32),
            columns,
        ),
        scratch_shapes=[
            pltpu.VMEM((id_columns, samples), I32),
            pltpu.VMEM(places.shape, I32),
            pltpu.VMEM((id_columns, requests), I32),
            pltpu.VMEM(sample_grads.shape, BF16),
            pltpu.VMEM((groups, LANES, 2 * sorted_rows // LANES), F32),
            pltpu.VMEM((shards, LANES), I32),
            pltpu.SMEM((shards, LANES), I32),
            pltpu.VMEM(extras.shape, BF16),
            pltpu.VMEM((groups, sorted_rows + 2 * slots, width), F32),
            pltpu.SemaphoreType.DMA((5,)),
        ]
        + index_scratch(samples, id_columns, per_field, groups, shards, places.shape[0]),
    )(*[in_hbm(array) for array in (sample_ids.T, places, req_ids.T, sample_grads)])
    got = exchange(sent)

    group = 32
    partial_sum, picks = call(
        functools.partial(sum_kernel, group),
        "gradient_sum",
        2**33,
        2**22,
        grid=(shards // group,),
        in_specs=[
            pl.BlockSpec((group, slots + EXTRA, width), lambda g: (g, 0, 0)),
            pl.BlockSpec((shards, EXTRA, width), lambda g: (0, slots // EXTRA, 0)),
        ],
        out_specs=(whole((rows_dev + 8, width)), whole(columns.shape)),
        out_shape=(shape((rows_dev + 8, width), F32), columns),
        scratch_shapes=[
            ex,
            pltpu.VMEM((2, shards, LANES), I32),
            pltpu.VMEM((LANES, LANES), F32),
            pltpu.VMEM((512, 512), F32),
        ],
    )(got, got)
    other = lax.ppermute(partial_sum, "rep", [(0, 1), (1, 0)])

    group = 64
    rows_type = shape((rows_dev, width), F32)
    any_space = pl.BlockSpec(memory_space=pl.ANY)
    new_rows, new_accum, sent, most = call(
        functools.partial(update_kernel, group),
        "update",
        2**32,
        2**23,
        grid=(shards // group,),
        in_specs=[
            whole(table_rows.shape),
            whole(accum.shape),
            whole(partial_sum.shape),
            whole(partial_sum.shape),
            whole(columns.shape),
        ],
        out_specs=(
            any_space,
            any_space,
            pl.BlockSpec((group, REQ_SLOTS + block, width), lambda g: (g, 0, 0)),
            whole((8, LANES)),
        ),
        out_shape=(
            rows_type,
            rows_type,
            pltpu.HBM((shards, REQ_SLOTS + block, width), BF16),
            shape((8, LANES), F32),
        ),
        scratch_shapes=[
            pltpu.VMEM(table_rows.shape, F32),
            pltpu.VMEM(table_rows.shape, F32),
            pltpu.VMEM(table_rows.shape, BF16),
            pltpu.VMEM((512, 512), BF16),
            pltpu.SemaphoreType.DMA((2,)),
        ],
    )(table_rows, accum, partial_sum, other, picks)
    returned = exchange(sent)

    place_rows = rows_dev // LANES
    own_places = lax.dynamic_slice_in_dim(
        places, lax.axis_index("shard") * place_rows, place_rows, axis=0
    )
    group = 32
    scores, serving_rows = call(
        functools.partial(rank_kernel, group),
        "pool_rank",
        2**32,
        2**22,
        grid=(shards // group,),
        in_specs=[
            pl.BlockSpec((group, REQ_SLOTS + block, width), lambda g: (g, 0, 0)),
            whole((shards, LANES)),
            whole(columns.shape),
            whole(own_places.shape),
            pl.BlockSpec(memory_space=pl.ANY),
            whole((1, hidden_width)),
            whole((1, hidden_width)),
        ],
        out_specs=(whole((1, requests)), whole((rows_dev, width))),
        out_shape=(pltpu.HBM((1, requests), F32), shape((rows_dev, width), BF16)),
        scratch_shapes=[
            pltpu.VMEM((512, 256), F32),
            pltpu.VMEM((2, 1024, LANES), BF16),
            pltpu.VMEM(w_hidden.shape, BF16),
            pltpu.SemaphoreType.DMA,
        ],
    )(
        returned, mrow, mcol, own_places, in_hbm(w_hidden),
        b_hidden.reshape(1, -1), w_score.reshape(1, -1),
    )
    scores = lax.cond(
        most[0, 0] <= REQ_SLOTS,
        lambda: scores.reshape(requests),
        lambda: range_scores(
            serving_rows, req_ids, w_hidden, b_hidden, w_score, shards, id_columns // per_field
        ),
    )
    return (new_rows, new_accum, serving_rows, scores)


def solution(mesh):
    return jax.shard_map(
        on_device,
        mesh=mesh,
        in_specs=(
            P("shard", None),
            P("shard", None),
            P("shard"),
            P(),
            P(("rep", "shard"), None),
            P(("rep", "shard"), None),
            P(("rep", "shard"), None),
            P(),
            P(),
            P(),
        ),
        out_specs=(P("shard", None), P("shard", None), P("shard", None), P(("rep", "shard"))),
        check_vma=False,
    )
```

```python
import functools

import jax
import jax.numpy as jnp
from jax import lax
from jax.experimental import pallas as pl
from jax.experimental.pallas import tpu as pltpu
from jax.sharding import PartitionSpec as P

F32, BF16, I32 = jnp.float32, jnp.bfloat16, jnp.int32
NT = (((1,), (1,)), ((), ()))
VMEM_LIMIT = 32 * 2**20
EXTRA = 16
LANES = 128
REQ_SLOTS = 112


def iota(shape, axis, dtype=I32):
    return lax.broadcasted_iota(I32, shape, axis).astype(dtype)


def dot(a, b):
    return jnp.dot(a, b, preferred_element_type=F32)


def dot_nt(a, b):
    return lax.dot_general(a, b, NT, preferred_element_type=F32)


def ones_where(mask):
    return jnp.where(mask, 1.0, 0.0).astype(BF16)


def hot_rows(rows, index):
    short = jnp.broadcast_to(index, (16, index.shape[1])).astype(jnp.int16)
    at = lax.broadcasted_iota(jnp.int16, (rows, index.shape[1]), 0)
    match = at == jnp.concatenate([short] * (rows // 16), axis=0)
    return jnp.where(match, jnp.ones((), BF16), jnp.zeros((), BF16))


def hot_columns(column, width):
    rows = column.shape[0]
    short = jnp.broadcast_to(column, (rows, LANES)).astype(I32).astype(jnp.int16)
    at = lax.broadcasted_iota(jnp.int16, (rows, width), 1)
    match = at == jnp.concatenate([short] * (width // LANES), axis=1)
    return jnp.where(match, jnp.ones((), BF16), jnp.zeros((), BF16))


def lanes_of(ref, first, count):
    return jnp.concatenate([ref[pl.ds(first + k, 1), :] for k in range(count)], axis=1)


def rank_ids(owner, base, shards, tri, ones):
    width = tri.shape[0]
    chunks = owner.shape[1] // width
    own = jnp.where(iota((shards, owner.shape[1]), 0, F32) == owner, 1.0, 0.0)
    stacked = jnp.concatenate(
        [own[:, k * width : (k + 1) * width] for k in range(chunks)], axis=0
    ).astype(BF16)
    before = dot(stacked, tri)
    totals = dot(stacked, ones)
    ranks = []
    for k in range(chunks):
        rows = slice(k * shards, (k + 1) * shards)
        at = before[rows] + jnp.concatenate([base] * (width // LANES), axis=1)
        ranks.append(jnp.sum(own[:, k * width : (k + 1) * width] * at, axis=0, keepdims=True))
        base = base + totals[rows]
    return own, jnp.concatenate(ranks, axis=1), base


def strict_upper(width):
    return ones_where(iota((width, width), 0) < iota((width, width), 1))


def pack_places(place, shift, block):
    last = place & (block - 1)
    scale = (1 << (last & 15)).astype(F32) * jnp.where(last >= 16, 65536.0, 1.0)
    packed = ((place >> shift) + 64).astype(F32) * scale
    half = place.shape[0] // 2
    return jnp.concatenate([packed[:half].T, packed[half:].T], axis=0).astype(BF16)


def look_up(table, ids):
    count = ids.shape[1]
    lows, lines = table.shape
    line = ids >> 7
    hot = hot_rows(lines, line & (lines - 1))
    low = (ids & 127) + jnp.where(line >= lines, LANES, 0)
    found = jnp.where(iota((lows, count), 0) == low, dot(table, hot), 0.0)
    return jnp.sum(found, axis=0, keepdims=True)


def unpack(value):
    last, scale = jnp.zeros_like(value), jnp.ones_like(value)
    for bits in (16, 8, 4, 2, 1):
        big = value >= 64.0 * 2.0**bits
        value = jnp.where(big, value * 2.0**-bits, value)
        last = last + jnp.where(big, float(bits), 0.0)
        scale = jnp.where(big, scale * 2.0**bits, scale)
    return value - 64.0, last, scale


def send_kernel(
    shards, rows_dev, per_field, groups, group,
    ids_ref, place_ref, req_ref, grads_ref, out_ref, mrow_ref, mcol_ref,
    ids, places, requests, grads, col, off_vmem, off, extra, rows_scr, sems, *scratch,
):
    step = pl.program_id(0)

    @pl.when(step == 0)
    def _():
        loads = [
            pltpu.make_async_copy(source, target, sems.at[at])
            for at, (source, target) in enumerate(
                ((place_ref, places), (ids_ref, ids), (req_ref, requests), (grads_ref, grads))
            )
        ]
        for load in loads:
            load.start()
        for load in loads[:3]:
            load.wait()
        index_ids(
            shards, rows_dev, per_field, groups,
            ids, places, requests, col, off_vmem, extra, mrow_ref, mcol_ref, *scratch,
        )
        copy = pltpu.make_async_copy(off_vmem, off, sems.at[4])
        copy.start()
        loads[3].wait()
        sort_rows(col, grads, rows_scr)
        copy.wait()

    fill_slots(step, group, groups, off, extra, rows_scr, out_ref)


def index_ids(
    shards, rows_dev, per_field, groups,
    ids_ref, place_ref, req_ref, col_ref, off_ref, extra_ref, mrow_ref, mcol_ref,
    table, ex, values, owners, scales, rank_scr, mark, off_scr,
):
    shift = rows_dev.bit_length() - 1
    width = ids_ref.shape[1]
    count = per_field * width
    fields = ids_ref.shape[0] // per_field
    span = fields // groups
    batch = count // req_ref.shape[1]
    batches = req_ref.shape[0] // batch
    table[...] = pack_places(place_ref[...], shift, rows_dev // shards)
    tri = strict_upper(width)
    ones = jnp.ones((width, LANES), BF16)

    def train_look_up(c, unused):
        ids = lanes_of(ids_ref, c * per_field, per_field)
        values[pl.ds(c, 1), :] = look_up(table[...], ids)
        return unused

    def request_look_up(c, unused):
        ids = lanes_of(req_ref, c * batch, batch)
        values[pl.ds(fields + c, 1), :] = look_up(table[...], ids)
        return unused

    values[...] = jnp.zeros_like(values)
    lax.fori_loop(0, fields, train_look_up, 0, unroll=8)
    lax.fori_loop(0, batches, request_look_up, 0, unroll=4)
    owner, unused, scale = unpack(values[...])
    owners[...] = owner
    scales[...] = scale

    def packed(ids, at):
        return ((ids >> shift) + 64).astype(F32) * scales[pl.ds(at, 1), :]

    def field_step(field, carry):
        base, row = carry
        ids = lanes_of(ids_ref, field * per_field, per_field)
        mark[pl.ds(field * shards, shards), :] = base
        own, rank, base = rank_ids(owners[pl.ds(field, 1), :], base, shards, tri, ones)
        rank_scr[pl.ds(field, 1), :] = rank
        at = hot_rows(width, rank.astype(I32))
        digits = (own * packed(ids, field)).astype(BF16)
        return base, row + dot_nt(at, jnp.concatenate([digits, digits], axis=0))

    base, row = lax.fori_loop(
        0,
        fields,
        field_step,
        (jnp.zeros((shards, LANES), F32), jnp.zeros((width, 2 * shards), F32)),
        unroll=8,
    )
    mark[fields * shards :, :] = base
    row = row.T[:shards]

    lane = iota((1, count), 1)

    def request_step(c, carry):
        base, row = carry
        ids = lanes_of(req_ref, c * batch, batch)
        own, rank, base = rank_ids(owners[pl.ds(fields + c, 1), :], base, shards, tri, ones)
        at = hot_rows(LANES, jnp.where(rank < REQ_SLOTS, rank, -1.0).astype(I32))
        field = c * (batch // per_field) + lane // (per_field * LANES)
        digits = [
            own * packed(ids, fields + c),
            own * (lane & (LANES - 1)).astype(F32),
            own * (field + 1).astype(F32),
        ]
        return base, row + dot_nt(jnp.concatenate(digits, axis=0).astype(BF16), at)

    most, asked = lax.fori_loop(
        0,
        batches,
        request_step,
        (jnp.zeros((shards, LANES), F32), jnp.zeros((3 * shards, LANES), F32)),
        unroll=4,
    )
    most = jnp.minimum(jnp.max(most, axis=0, keepdims=True), 255.0)
    parts = [
        row[:, :LANES], row[:, LANES:], asked[:shards], jnp.broadcast_to(most, (shards, LANES))
    ]
    ex[...] = jnp.zeros_like(ex)
    for kind, part in enumerate(parts):
        ex[pl.ds(kind, shards, stride=EXTRA), :] = part
    extra_ref[...] = ex[: shards * EXTRA, :].astype(BF16)
    number = asked[2 * shards :]
    field = number.astype(I32) - 1
    mrow_ref[...] = jnp.where(
        field < 0, -1, (field & 3) * LANES + asked[shards : 2 * shards].astype(I32)
    )
    mcol_ref[...] = jnp.where(jnp.concatenate([number, number], axis=0).T > 4.0, 1.0, 0.0)

    earlier = ones_where(iota((shards, shards), 1) < iota((shards, shards), 0))
    lane = iota((shards, LANES), 1)
    table_off = jnp.zeros((shards, LANES), F32)
    for g in range(groups):
        first = mark[g * span * shards : (g * span + 1) * shards, :]
        after = mark[(g + 1) * span * shards : ((g + 1) * span + 1) * shards, :]
        off = dot(earlier, (after - first).astype(BF16)) - first
        off_scr[g * shards : (g + 1) * shards, :] = off
        table_off = jnp.where(lane == g, off, table_off)
        table_off = jnp.where(lane == groups + g, after, table_off)
    off_ref[...] = table_off.astype(I32)

    total = span * count
    blocks = total // LANES
    at = iota((1, total), 1)
    sample = (at & (width - 1)).astype(F32)
    field = (at // count).astype(F32)

    def group_step(g, unused):
        owner = lanes_of(owners, g * span, span)
        off = off_scr[pl.ds(g * shards, shards), :]
        shifts = jnp.where(
            iota((shards, total), 0, F32) == owner,
            jnp.concatenate([off] * blocks, axis=1),
            0.0,
        )
        pos = lanes_of(rank_scr, g * span, span) + jnp.sum(shifts, axis=0, keepdims=True)
        pos = pos.astype(I32)
        block = iota((blocks, total), 0) == (pos >> 7)
        source = jnp.concatenate(
            [jnp.where(block, sample, 0.0), jnp.where(block, field, 0.0)], axis=0
        ).astype(BF16)
        col_ref[g] = dot_nt(hot_rows(LANES, pos & 127), source)
        return unused

    lax.fori_loop(0, groups, group_step, 0, unroll=4)


def index_scratch(samples, id_columns, per_field, groups, shards, lines):
    fields = id_columns // per_field
    count = per_field * samples
    return [
        pltpu.VMEM((2 * LANES, lines // 2), BF16),
        pltpu.VMEM(((shards + 1) * EXTRA, LANES), F32),
        pltpu.VMEM((2 * fields, count), F32),
        pltpu.VMEM((2 * fields, count), F32),
        pltpu.VMEM((2 * fields, count), F32),
        pltpu.VMEM((fields, count), F32),
        pltpu.VMEM(((fields + 1) * shards, LANES), F32),
        pltpu.VMEM((groups * shards, LANES), F32),
    ]


def sort_rows(col_ref, grads_ref, rows_scr):
    samples = grads_ref.shape[0]
    groups = col_ref.shape[0]
    blocks = col_ref.shape[2] // 2
    total = blocks * LANES
    pad = (rows_scr.shape[1] - total) // 2
    span = grads_ref.shape[1] // groups

    def sort_group(g, unused):
        col = col_ref[g]
        hots = [
            hot_columns(col[:, b : b + 1], samples) for b in range(blocks)
        ]
        part = grads_ref[:, pl.ds(pl.multiple_of(g * span, span), span)]
        rows = dot(jnp.concatenate(hots, axis=0), part)
        field = jnp.concatenate(
            [
                jnp.broadcast_to(col[:, blocks + b : blocks + b + 1], (LANES, LANES))
                for b in range(blocks)
            ],
            axis=0,
        )
        picked = rows[:, :LANES]
        for q in range(1, span // LANES):
            picked = jnp.where(field == float(q), rows[:, q * LANES : (q + 1) * LANES], picked)
        rows_scr[g, pad : pad + total, :] = picked
        return unused

    lax.fori_loop(0, groups, sort_group, 0, unroll=2)


def fill_slots(step, group, groups, off_ref, extra_ref, rows_scr, out_ref):
    slots = out_ref.shape[1] - EXTRA
    at = iota((slots, LANES), 0)

    def one(b, unused):
        owner = step * group + b
        picked = rows_scr[0, pl.ds(slots + off_ref[owner, 0], slots), :]
        for g in range(1, groups):
            start = off_ref[owner, groups + g - 1]
            rows = rows_scr[g, pl.ds(slots + off_ref[owner, g], slots), :]
            picked = jnp.where(at >= start, rows, picked)
        picked = jnp.where(at >= off_ref[owner, 2 * groups - 1], 0.0, picked)
        out_ref[b, 0:slots, :] = picked.astype(BF16)
        out_ref[b, slots : slots + EXTRA, :] = extra_ref[
            pl.ds(pl.multiple_of(owner * EXTRA, EXTRA), EXTRA), :
        ]
        return unused

    lax.fori_loop(0, group, one, 0, unroll=4)


def sum_kernel(group, got_ref, extra_ref, out_ref, picks_ref, scr, hi_scr, lo_scr, total):
    shards = extra_ref.shape[0]
    slots = got_ref.shape[1] - EXTRA
    step = pl.program_id(0)

    @pl.when(step == 0)
    def _():
        scr[: shards * EXTRA, :] = extra_ref[...].astype(F32).reshape(shards * EXTRA, LANES)
        kinds = [scr[pl.ds(kind, shards, stride=EXTRA), :] for kind in range(4)]
        first, last, unused = unpack(jnp.concatenate(kinds[:3], axis=0))
        first = jnp.maximum(first, 0.0).astype(I32)
        high = (first & 15) * 32 + last.astype(I32)
        low = (first >> 4).astype(F32)
        for half in range(2):
            hi_scr[half] = high[half * shards : (half + 1) * shards]
        lo_scr[...] = low[: 2 * shards].T
        total[...] = jnp.zeros_like(total)
        picks_ref[...] = jnp.concatenate(
            [high[2 * shards :].astype(F32), low[2 * shards :]], axis=0
        ).T
        most = jnp.max(kinds[3], axis=0, keepdims=True)
        out_ref[4 * 512 :, :] = jnp.broadcast_to(most, (8, LANES))

    turned = pltpu.roll(lo_scr[...], lax.rem(2 * shards - step * group, 2 * shards), 1)
    highs, values = [], []
    for k in range(group):
        for half in range(2):
            hi = hi_scr[half, pl.ds(step * group + k, 1), :]
            highs.append(hot_rows(512, hi))
            low = turned[:, half * shards + k : half * shards + k + 1]
            low = jnp.broadcast_to(low, (LANES, LANES)).astype(I32).astype(jnp.int16)
            rows = got_ref[k, half * LANES : (half + 1) * LANES, :]
            zero = jnp.zeros((), BF16)
            values.append(
                jnp.concatenate(
                    [jnp.where(low == jnp.int16(q), rows, zero) for q in range(4)], axis=1
                )
            )
    total[...] += dot(jnp.concatenate(highs, axis=1), jnp.concatenate(values, axis=0))

    @pl.when(step == pl.num_programs(0) - 1)
    def _():
        for q in range(4):
            out_ref[q * 512 : (q + 1) * 512, :] = total[:, q * LANES : (q + 1) * LANES]


def pick_rows(count, height, high, low, wide):
    hots = [
        hot_columns(high[:height, b : b + 1], 512) for b in range(count)
    ]
    rows = dot(jnp.concatenate(hots, axis=0), wide)
    lows = jnp.concatenate(
        [jnp.broadcast_to(low[:height, b : b + 1], (height, LANES)) for b in range(count)], axis=0
    )
    picked = rows[:, :LANES]
    for q in range(1, 4):
        picked = jnp.where(lows == float(q), rows[:, q * LANES : (q + 1) * LANES], picked)
    return picked.astype(BF16)


def update_kernel(
    parts, table_ref, accum_ref, one_ref, two_ref, picks_ref, rows_ref, accum_out_ref, sent_ref,
    most_ref, rows, updated, moved, sent, sems,
):
    count = rows.shape[0]
    most_ref[...] = jnp.maximum(one_ref[count:, :], two_ref[count:, :])
    gradient = one_ref[:count, :] + two_ref[:count, :]
    history = accum_ref[...] + gradient * gradient
    updated[...] = history
    rows[...] = table_ref[...] - 0.1 * gradient * lax.rsqrt(history)
    copies = [
        pltpu.make_async_copy(rows, rows_ref, sems.at[0]),
        pltpu.make_async_copy(updated, accum_out_ref, sems.at[1]),
    ]
    for copy in copies:
        copy.start()
    moved[...] = rows[...].astype(BF16)
    wide = jnp.concatenate([moved[q * 512 : (q + 1) * 512, :] for q in range(4)], axis=1)
    shards = sent.shape[0]
    block = count // shards
    sent[:, REQ_SLOTS:, :] = moved[...].reshape(shards, block, LANES)
    group = shards // parts
    for part in range(parts):
        first = part * group
        picked = pick_rows(
            group, REQ_SLOTS, picks_ref[:, first : first + group],
            picks_ref[:, LANES // 2 + first : LANES // 2 + first + group], wide,
        )
        at = slice(first, first + group)
        sent[at, :REQ_SLOTS, :] = picked.reshape(group, REQ_SLOTS, LANES)
        copies.append(pltpu.make_async_copy(sent.at[at], sent_ref.at[at], sems.at[2 + part]))
        copies[-1].start()
    for copy in copies:
        copy.wait()


def rank_kernel(
    group, ret_ref, mrow_ref, mcol_ref, place_ref, w_ref, b_ref, score_ref, out_ref, serving_ref,
    total, wide, weights, sem,
):
    step = pl.program_id(0)
    load = pltpu.make_async_copy(w_ref, weights, sem)

    @pl.when(step == 0)
    def _():
        load.start()
        total[...] = jnp.zeros_like(total)

    turned = pltpu.roll(mcol_ref[...], lax.rem(LANES - step * group, LANES), 1)
    hots, values = [], []
    for b in range(group):
        hots.append(
            hot_rows(512, mrow_ref[pl.ds(step * group + b, 1), :])
        )
        low = jnp.broadcast_to(turned[:, b : b + 1], (LANES, LANES)).astype(I32).astype(jnp.int16)
        rows = ret_ref[b, :LANES, :]
        zero = jnp.zeros((), BF16)
        values.append(
            jnp.concatenate([jnp.where(low == jnp.int16(q), rows, zero) for q in range(2)], axis=1)
        )
    total[...] += dot(jnp.concatenate(hots, axis=1), jnp.concatenate(values, axis=0))
    wide[step] = ret_ref[:, REQ_SLOTS:, :].reshape(wide.shape[1:])

    @pl.when(step == pl.num_programs(0) - 1)
    def _():
        pooled = jnp.concatenate(
            [
                total[(f & 3) * LANES : (f & 3) * LANES + LANES, (f >> 2) * LANES : (f >> 2) * LANES + LANES]
                for f in range(8)
            ],
            axis=1,
        ).astype(BF16)
        load.wait()
        hidden = jnp.maximum(dot(pooled, weights[...]) + b_ref[...], 0.0).astype(BF16)
        out_ref[...] = dot_nt(score_ref[...], hidden)
        place = place_ref[...]
        owner, last = place >> 11, place & 31
        high = ((owner & 15) * 32 + last).astype(F32)
        zero = jnp.zeros((LANES // 2 - place.shape[0], LANES), F32)
        cols = jnp.concatenate([high, zero, (owner >> 4).astype(F32), zero], axis=0).T
        moved = jnp.concatenate([wide[q // 2, (q % 2) * 512 : (q % 2) * 512 + 512] for q in range(4)], axis=1)
        serving_ref[...] = pick_rows(
            place.shape[0], LANES, cols, cols[:, LANES // 2 :], moved
        )


def bucket_slots(targets, target_count, capacity):
    one_hot = (targets[:, None] == jnp.arange(target_count, dtype=I32)[None, :]).astype(I32)
    ranking = jnp.sum(jnp.cumsum(one_hot, axis=0) * one_hot, axis=1) - 1
    return targets * capacity + ranking


def range_scores(serving_rows, req_ids, w_hidden, b_hidden, w_score, shards, fields):
    rows_dev, width = serving_rows.shape
    requests, id_columns = req_ids.shape
    capacity = 2 * requests * id_columns // shards
    flat = req_ids.reshape(-1)
    slot = bucket_slots(flat // rows_dev, shards, capacity)
    keys = jnp.zeros((shards * capacity,), I32).at[slot].set(flat % rows_dev)
    asked = exchange(keys.reshape(shards, capacity))
    found = jnp.take(serving_rows, asked.reshape(-1), axis=0, mode="clip")
    returned = exchange(found.reshape(shards, capacity, width)).reshape(-1, width)
    rows = jnp.take(returned, slot, axis=0, mode="clip").astype(F32)
    pooled = jnp.sum(rows.reshape(requests * fields, id_columns // fields, width), axis=1)
    pooled = pooled.astype(BF16).reshape(requests, fields * width)
    hidden = jnp.dot(pooled, w_hidden, preferred_element_type=F32) + b_hidden
    return jnp.dot(jax.nn.relu(hidden).astype(BF16), w_score, preferred_element_type=F32)


def whole(shape):
    return pl.BlockSpec(shape, lambda *step: (0,) * len(shape))


def call(kernel, name, flops, moved, **kwargs):
    return pl.pallas_call(
        kernel,
        name=name,
        compiler_params=pltpu.CompilerParams(vmem_limit_bytes=VMEM_LIMIT),
        cost_estimate=pl.CostEstimate(flops=flops, bytes_accessed=moved, transcendentals=0),
        **kwargs,
    )


def in_hbm(array):
    return pltpu.with_memory_space_constraint(array, pltpu.HBM)


def exchange(rows):
    return lax.all_to_all(rows, "shard", split_axis=0, concat_axis=0, tiled=True)


def on_device(
    table_rows,
    accum,
    hash_keys,
    hash_place,
    sample_ids,
    sample_grads,
    req_ids,
    w_hidden,
    b_hidden,
    w_score,
):
    rows_dev, width = table_rows.shape
    shards = lax.axis_size("shard")
    samples, id_columns = sample_ids.shape
    requests = req_ids.shape[0]
    slots = 2 * samples * id_columns // shards
    hidden_width = w_hidden.shape[1]
    per_field = id_columns * width // sample_grads.shape[1]
    block = rows_dev // shards
    groups = 2
    sorted_rows = samples * id_columns // groups
    places = hash_place.reshape(-1, LANES)
    shape = jax.ShapeDtypeStruct
    extras = shape((shards * EXTRA, LANES), BF16)
    columns = shape((LANES, 2 * shards), F32)
    ex = pltpu.VMEM(((shards + 1) * EXTRA, LANES), F32)

    group = 16
    sent, mrow, mcol = call(
        functools.partial(send_kernel, shards, rows_dev, per_field, groups, group),
        "send",
        2**34,
        2**23,
        grid=(shards // group,),
        in_specs=[pl.BlockSpec(memory_space=pl.ANY)] * 4,
        out_specs=(
            pl.BlockSpec((group, slots + EXTRA, width), lambda g: (g, 0, 0)),
            whole((shards, LANES)),
            whole(columns.shape),
        ),
        out_shape=(
            shape((shards, slots + EXTRA, width), BF16),
            shape((shards, LANES), I32),
            columns,
        ),
        scratch_shapes=[
            pltpu.VMEM((id_columns, samples), I32),
            pltpu.VMEM(places.shape, I32),
            pltpu.VMEM((id_columns, requests), I32),
            pltpu.VMEM(sample_grads.shape, BF16),
            pltpu.VMEM((groups, LANES, 2 * sorted_rows // LANES), F32),
            pltpu.VMEM((shards, LANES), I32),
            pltpu.SMEM((shards, LANES), I32),
            pltpu.VMEM(extras.shape, BF16),
            pltpu.VMEM((groups, sorted_rows + 2 * slots, width), F32),
            pltpu.SemaphoreType.DMA((5,)),
        ]
        + index_scratch(samples, id_columns, per_field, groups, shards, places.shape[0]),
    )(*[in_hbm(array) for array in (sample_ids.T, places, req_ids.T, sample_grads)])
    got = exchange(sent)

    group = 32
    partial_sum, picks = call(
        functools.partial(sum_kernel, group),
        "gradient_sum",
        2**33,
        2**22,
        grid=(shards // group,),
        in_specs=[
            pl.BlockSpec((group, slots + EXTRA, width), lambda g: (g, 0, 0)),
            pl.BlockSpec((shards, EXTRA, width), lambda g: (0, slots // EXTRA, 0)),
        ],
        out_specs=(whole((rows_dev + 8, width)), whole(columns.shape)),
        out_shape=(shape((rows_dev + 8, width), F32), columns),
        scratch_shapes=[
            ex,
            pltpu.VMEM((2, shards, LANES), I32),
            pltpu.VMEM((LANES, LANES), F32),
            pltpu.VMEM((512, 512), F32),
        ],
    )(got, got)
    other = lax.ppermute(partial_sum, "rep", [(0, 1), (1, 0)])

    parts = 4
    any_space = pl.BlockSpec(memory_space=pl.ANY)
    rows_type = shape((rows_dev, width), F32)
    new_rows, new_accum, sent, most = call(
        functools.partial(update_kernel, parts),
        "update",
        2**32,
        2**23,
        grid=(1,),
        in_specs=[
            whole(table_rows.shape),
            whole(accum.shape),
            whole(partial_sum.shape),
            whole(partial_sum.shape),
            whole(columns.shape),
        ],
        out_specs=(
            any_space,
            any_space,
            any_space,
            whole((8, LANES)),
        ),
        out_shape=(
            rows_type,
            rows_type,
            pltpu.HBM((shards, REQ_SLOTS + block, width), BF16),
            shape((8, LANES), F32),
        ),
        scratch_shapes=[
            pltpu.VMEM(table_rows.shape, F32),
            pltpu.VMEM(table_rows.shape, F32),
            pltpu.VMEM(table_rows.shape, BF16),
            pltpu.VMEM((shards, REQ_SLOTS + block, width), BF16),
            pltpu.SemaphoreType.DMA((2 + parts,)),
        ],
    )(table_rows, accum, partial_sum, other, picks)
    returned = exchange(sent)

    place_rows = rows_dev // LANES
    own_places = lax.dynamic_slice_in_dim(
        places, lax.axis_index("shard") * place_rows, place_rows, axis=0
    )
    group = 32
    scores, serving_rows = call(
        functools.partial(rank_kernel, group),
        "pool_rank",
        2**32,
        2**22,
        grid=(shards // group,),
        in_specs=[
            pl.BlockSpec((group, REQ_SLOTS + block, width), lambda g: (g, 0, 0)),
            whole((shards, LANES)),
            whole(columns.shape),
            whole(own_places.shape),
            pl.BlockSpec(memory_space=pl.ANY),
            whole((1, hidden_width)),
            whole((1, hidden_width)),
        ],
        out_specs=(whole((1, requests)), whole((rows_dev, width))),
        out_shape=(pltpu.HBM((1, requests), F32), shape((rows_dev, width), BF16)),
        scratch_shapes=[
            pltpu.VMEM((512, 256), F32),
            pltpu.VMEM((2, 1024, LANES), BF16),
            pltpu.VMEM(w_hidden.shape, BF16),
            pltpu.SemaphoreType.DMA,
        ],
    )(
        returned, mrow, mcol, own_places, in_hbm(w_hidden),
        b_hidden.reshape(1, -1), w_score.reshape(1, -1),
    )
    scores = lax.cond(
        most[0, 0] <= REQ_SLOTS,
        lambda: scores.reshape(requests),
        lambda: range_scores(
            serving_rows, req_ids, w_hidden, b_hidden, w_score, shards, id_columns // per_field
        ),
    )
    return (new_rows, new_accum, serving_rows, scores)


def solution(mesh):
    return jax.shard_map(
        on_device,
        mesh=mesh,
        in_specs=(
            P("shard", None),
            P("shard", None),
            P("shard"),
            P(),
            P(("rep", "shard"), None),
            P(("rep", "shard"), None),
            P(("rep", "shard"), None),
            P(),
            P(),
            P(),
        ),
        out_specs=(P("shard", None), P("shard", None), P("shard", None), P(("rep", "shard"))),
        check_vma=False,
    )
```

```python
import functools

import jax
import jax.numpy as jnp
from jax import lax
from jax.experimental import pallas as pl
from jax.experimental.pallas import tpu as pltpu
from jax.sharding import PartitionSpec as P

F32, BF16, I32 = jnp.float32, jnp.bfloat16, jnp.int32
NT = (((1,), (1,)), ((), ()))
VMEM_LIMIT = 32 * 2**20
EXTRA = 16
LANES = 128
REQ_SLOTS = 112


def iota(shape, axis, dtype=I32):
    return lax.broadcasted_iota(I32, shape, axis).astype(dtype)


def dot(a, b):
    return jnp.dot(a, b, preferred_element_type=F32)


def dot_nt(a, b):
    return lax.dot_general(a, b, NT, preferred_element_type=F32)


def ones_where(mask):
    return jnp.where(mask, 1.0, 0.0).astype(BF16)


def hot_rows(rows, index):
    short = jnp.broadcast_to(index, (16, index.shape[1])).astype(jnp.int16)
    at = lax.broadcasted_iota(jnp.int16, (rows, index.shape[1]), 0)
    match = at == jnp.concatenate([short] * (rows // 16), axis=0)
    return jnp.where(match, jnp.ones((), BF16), jnp.zeros((), BF16))


def hot_columns(column, width):
    rows = column.shape[0]
    short = jnp.broadcast_to(column, (rows, LANES)).astype(I32).astype(jnp.int16)
    at = lax.broadcasted_iota(jnp.int16, (rows, width), 1)
    match = at == jnp.concatenate([short] * (width // LANES), axis=1)
    return jnp.where(match, jnp.ones((), BF16), jnp.zeros((), BF16))


def lanes_of(ref, first, count):
    return jnp.concatenate([ref[pl.ds(first + k, 1), :] for k in range(count)], axis=1)


def rank_ids(owner, base, shards, tri, ones):
    width = tri.shape[0]
    chunks = owner.shape[1] // width
    own = jnp.where(iota((shards, owner.shape[1]), 0, F32) == owner, 1.0, 0.0)
    stacked = jnp.concatenate(
        [own[:, k * width : (k + 1) * width] for k in range(chunks)], axis=0
    ).astype(BF16)
    before = dot(stacked, tri)
    totals = dot(stacked, ones)
    ranks = []
    for k in range(chunks):
        rows = slice(k * shards, (k + 1) * shards)
        at = before[rows] + jnp.concatenate([base] * (width // LANES), axis=1)
        ranks.append(jnp.sum(own[:, k * width : (k + 1) * width] * at, axis=0, keepdims=True))
        base = base + totals[rows]
    return own, jnp.concatenate(ranks, axis=1), base


def strict_upper(width):
    return ones_where(iota((width, width), 0) < iota((width, width), 1))


def pack_places(place, shift, block):
    last = place & (block - 1)
    scale = (1 << (last & 15)).astype(F32) * jnp.where(last >= 16, 65536.0, 1.0)
    packed = ((place >> shift) + 64).astype(F32) * scale
    half = place.shape[0] // 2
    return jnp.concatenate([packed[:half].T, packed[half:].T], axis=0).astype(BF16)


def look_up(table, ids):
    count = ids.shape[1]
    lows, lines = table.shape
    line = ids >> 7
    hot = hot_rows(lines, line & (lines - 1))
    low = (ids & 127) + jnp.where(line >= lines, LANES, 0)
    found = jnp.where(iota((lows, count), 0) == low, dot(table, hot), 0.0)
    return jnp.sum(found, axis=0, keepdims=True)


def unpack(value):
    last, scale = jnp.zeros_like(value), jnp.ones_like(value)
    for bits in (16, 8, 4, 2, 1):
        big = value >= 64.0 * 2.0**bits
        value = jnp.where(big, value * 2.0**-bits, value)
        last = last + jnp.where(big, float(bits), 0.0)
        scale = jnp.where(big, scale * 2.0**bits, scale)
    return value - 64.0, last, scale


def send_kernel(
    shards, rows_dev, per_field, groups, group,
    ids_ref, place_ref, req_ref, grads_ref, out_ref, mrow_ref, mcol_ref,
    ids, places, requests, grads, col, off_vmem, off, extra, rows_scr, sems, *scratch,
):
    step = pl.program_id(0)

    @pl.when(step == 0)
    def _():
        loads = [
            pltpu.make_async_copy(source, target, sems.at[at])
            for at, (source, target) in enumerate(
                ((place_ref, places), (ids_ref, ids), (req_ref, requests), (grads_ref, grads))
            )
        ]
        for load in loads:
            load.start()
        for load in loads[:3]:
            load.wait()
        index_ids(
            shards, rows_dev, per_field, groups,
            ids, places, requests, col, off_vmem, extra, mrow_ref, mcol_ref, *scratch,
        )
        copy = pltpu.make_async_copy(off_vmem, off, sems.at[4])
        copy.start()
        loads[3].wait()
        sort_rows(col, grads, rows_scr)
        copy.wait()

    fill_slots(step, group, groups, off, extra, rows_scr, out_ref)


def index_ids(
    shards, rows_dev, per_field, groups,
    ids_ref, place_ref, req_ref, col_ref, off_ref, extra_ref, mrow_ref, mcol_ref,
    table, ex, values, owners, scales, rank_scr, mark, off_scr,
):
    shift = rows_dev.bit_length() - 1
    width = ids_ref.shape[1]
    count = per_field * width
    fields = ids_ref.shape[0] // per_field
    span = fields // groups
    batch = count // req_ref.shape[1]
    batches = req_ref.shape[0] // batch
    table[...] = pack_places(place_ref[...], shift, rows_dev // shards)
    tri = strict_upper(width)
    ones = jnp.ones((width, LANES), BF16)

    def train_look_up(c, unused):
        ids = lanes_of(ids_ref, c * per_field, per_field)
        values[pl.ds(c, 1), :] = look_up(table[...], ids)
        return unused

    def request_look_up(c, unused):
        ids = lanes_of(req_ref, c * batch, batch)
        values[pl.ds(fields + c, 1), :] = look_up(table[...], ids)
        return unused

    values[...] = jnp.zeros_like(values)
    lax.fori_loop(0, fields, train_look_up, 0, unroll=8)
    lax.fori_loop(0, batches, request_look_up, 0, unroll=4)
    owner, unused, scale = unpack(values[...])
    owners[...] = owner
    scales[...] = scale

    def packed(ids, at):
        return ((ids >> shift) + 64).astype(F32) * scales[pl.ds(at, 1), :]

    def field_step(field, carry):
        base, row = carry
        ids = lanes_of(ids_ref, field * per_field, per_field)
        mark[pl.ds(field * shards, shards), :] = base
        own, rank, base = rank_ids(owners[pl.ds(field, 1), :], base, shards, tri, ones)
        rank_scr[pl.ds(field, 1), :] = rank
        at = hot_rows(width, rank.astype(I32))
        digits = (own * packed(ids, field)).astype(BF16)
        return base, row + dot_nt(at, jnp.concatenate([digits, digits], axis=0))

    base, row = lax.fori_loop(
        0,
        fields,
        field_step,
        (jnp.zeros((shards, LANES), F32), jnp.zeros((width, 2 * shards), F32)),
        unroll=8,
    )
    mark[fields * shards :, :] = base
    row = row.T[:shards]

    lane = iota((1, count), 1)

    def request_step(c, carry):
        base, row = carry
        ids = lanes_of(req_ref, c * batch, batch)
        own, rank, base = rank_ids(owners[pl.ds(fields + c, 1), :], base, shards, tri, ones)
        at = hot_rows(LANES, jnp.where(rank < REQ_SLOTS, rank, -1.0).astype(I32))
        field = c * (batch // per_field) + lane // (per_field * LANES)
        digits = [
            own * packed(ids, fields + c),
            own * (lane & (LANES - 1)).astype(F32),
            own * (field + 1).astype(F32),
        ]
        return base, row + dot_nt(jnp.concatenate(digits, axis=0).astype(BF16), at)

    most, asked = lax.fori_loop(
        0,
        batches,
        request_step,
        (jnp.zeros((shards, LANES), F32), jnp.zeros((3 * shards, LANES), F32)),
        unroll=4,
    )
    most = jnp.minimum(jnp.max(most, axis=0, keepdims=True), 255.0)
    parts = [
        row[:, :LANES], row[:, LANES:], asked[:shards], jnp.broadcast_to(most, (shards, LANES))
    ]
    ex[...] = jnp.zeros_like(ex)
    for kind, part in enumerate(parts):
        ex[pl.ds(kind, shards, stride=EXTRA), :] = part
    extra_ref[...] = ex[: shards * EXTRA, :].astype(BF16)
    number = asked[2 * shards :]
    field = number.astype(I32) - 1
    mrow_ref[...] = jnp.where(
        field < 0, -1, (field & 3) * LANES + asked[shards : 2 * shards].astype(I32)
    )
    mcol_ref[...] = jnp.where(jnp.concatenate([number, number], axis=0).T > 4.0, 1.0, 0.0)

    earlier = ones_where(iota((shards, shards), 1) < iota((shards, shards), 0))
    lane = iota((shards, LANES), 1)
    table_off = jnp.zeros((shards, LANES), F32)
    for g in range(groups):
        first = mark[g * span * shards : (g * span + 1) * shards, :]
        after = mark[(g + 1) * span * shards : ((g + 1) * span + 1) * shards, :]
        off = dot(earlier, (after - first).astype(BF16)) - first
        off_scr[g * shards : (g + 1) * shards, :] = off
        table_off = jnp.where(lane == g, off, table_off)
        table_off = jnp.where(lane == groups + g, after, table_off)
    off_ref[...] = table_off.astype(I32)

    total = span * count
    blocks = total // LANES
    at = iota((1, total), 1)
    sample = (at & (width - 1)).astype(F32)
    field = (at // count).astype(F32)

    def group_step(g, unused):
        owner = lanes_of(owners, g * span, span)
        off = off_scr[pl.ds(g * shards, shards), :]
        shifts = jnp.where(
            iota((shards, total), 0, F32) == owner,
            jnp.concatenate([off] * blocks, axis=1),
            0.0,
        )
        pos = lanes_of(rank_scr, g * span, span) + jnp.sum(shifts, axis=0, keepdims=True)
        pos = pos.astype(I32)
        block = iota((blocks, total), 0) == (pos >> 7)
        source = jnp.concatenate(
            [jnp.where(block, sample, 0.0), jnp.where(block, field, 0.0)], axis=0
        ).astype(BF16)
        col_ref[g] = dot_nt(hot_rows(LANES, pos & 127), source)
        return unused

    lax.fori_loop(0, groups, group_step, 0, unroll=4)


def index_scratch(samples, id_columns, per_field, groups, shards, lines):
    fields = id_columns // per_field
    count = per_field * samples
    return [
        pltpu.VMEM((2 * LANES, lines // 2), BF16),
        pltpu.VMEM(((shards + 1) * EXTRA, LANES), F32),
        pltpu.VMEM((2 * fields, count), F32),
        pltpu.VMEM((2 * fields, count), F32),
        pltpu.VMEM((2 * fields, count), F32),
        pltpu.VMEM((fields, count), F32),
        pltpu.VMEM(((fields + 1) * shards, LANES), F32),
        pltpu.VMEM((groups * shards, LANES), F32),
    ]


def sort_rows(col_ref, grads_ref, rows_scr):
    samples = grads_ref.shape[0]
    groups = col_ref.shape[0]
    blocks = col_ref.shape[2] // 2
    total = blocks * LANES
    pad = (rows_scr.shape[1] - total) // 2
    span = grads_ref.shape[1] // groups

    def sort_group(g, unused):
        col = col_ref[g]
        hots = [
            hot_columns(col[:, b : b + 1], samples) for b in range(blocks)
        ]
        part = grads_ref[:, pl.ds(pl.multiple_of(g * span, span), span)]
        rows = dot(jnp.concatenate(hots, axis=0), part)
        field = jnp.concatenate(
            [
                jnp.broadcast_to(col[:, blocks + b : blocks + b + 1], (LANES, LANES))
                for b in range(blocks)
            ],
            axis=0,
        )
        picked = rows[:, :LANES]
        for q in range(1, span // LANES):
            picked = jnp.where(field == float(q), rows[:, q * LANES : (q + 1) * LANES], picked)
        rows_scr[g, pad : pad + total, :] = picked
        return unused

    lax.fori_loop(0, groups, sort_group, 0, unroll=2)


def fill_slots(step, group, groups, off_ref, extra_ref, rows_scr, out_ref):
    slots = out_ref.shape[1] - EXTRA
    at = iota((slots, LANES), 0)

    def one(b, unused):
        owner = step * group + b
        picked = rows_scr[0, pl.ds(slots + off_ref[owner, 0], slots), :]
        for g in range(1, groups):
            start = off_ref[owner, groups + g - 1]
            rows = rows_scr[g, pl.ds(slots + off_ref[owner, g], slots), :]
            picked = jnp.where(at >= start, rows, picked)
        picked = jnp.where(at >= off_ref[owner, 2 * groups - 1], 0.0, picked)
        out_ref[b, 0:slots, :] = picked.astype(BF16)
        out_ref[b, slots : slots + EXTRA, :] = extra_ref[
            pl.ds(pl.multiple_of(owner * EXTRA, EXTRA), EXTRA), :
        ]
        return unused

    lax.fori_loop(0, group, one, 0, unroll=4)


def sum_kernel(group, got_ref, extra_ref, out_ref, picks_ref, scr, hi_scr, lo_scr, total):
    shards = extra_ref.shape[0]
    slots = got_ref.shape[1] - EXTRA
    step = pl.program_id(0)

    @pl.when(step == 0)
    def _():
        scr[: shards * EXTRA, :] = extra_ref[...].astype(F32).reshape(shards * EXTRA, LANES)
        kinds = [scr[pl.ds(kind, shards, stride=EXTRA), :] for kind in range(4)]
        first, last, unused = unpack(jnp.concatenate(kinds[:3], axis=0))
        first = jnp.maximum(first, 0.0).astype(I32)
        high = (first & 15) * 32 + last.astype(I32)
        low = (first >> 4).astype(F32)
        for half in range(2):
            hi_scr[half] = high[half * shards : (half + 1) * shards]
        lo_scr[...] = low[: 2 * shards].T
        total[...] = jnp.zeros_like(total)
        picks_ref[...] = jnp.concatenate(
            [high[2 * shards :].astype(F32), low[2 * shards :]], axis=0
        ).T
        most = jnp.max(kinds[3], axis=0, keepdims=True)
        out_ref[4 * 512 :, :] = jnp.broadcast_to(most, (16, LANES)).astype(BF16)

    turned = pltpu.roll(lo_scr[...], lax.rem(2 * shards - step * group, 2 * shards), 1)
    highs, values = [], []
    for k in range(group):
        for half in range(2):
            hi = hi_scr[half, pl.ds(step * group + k, 1), :]
            highs.append(hot_rows(512, hi))
            low = turned[:, half * shards + k : half * shards + k + 1]
            low = jnp.broadcast_to(low, (LANES, LANES)).astype(I32).astype(jnp.int16)
            rows = got_ref[k, half * LANES : (half + 1) * LANES, :]
            zero = jnp.zeros((), BF16)
            values.append(
                jnp.concatenate(
                    [jnp.where(low == jnp.int16(q), rows, zero) for q in range(4)], axis=1
                )
            )
    total[...] += dot(jnp.concatenate(highs, axis=1), jnp.concatenate(values, axis=0))

    @pl.when(step == pl.num_programs(0) - 1)
    def _():
        for q in range(4):
            out_ref[q * 512 : (q + 1) * 512, :] = total[:, q * LANES : (q + 1) * LANES].astype(BF16)


def pick_rows(count, height, high, low, wide):
    hots = [
        hot_columns(high[:height, b : b + 1], 512) for b in range(count)
    ]
    rows = dot(jnp.concatenate(hots, axis=0), wide)
    lows = jnp.concatenate(
        [jnp.broadcast_to(low[:height, b : b + 1], (height, LANES)) for b in range(count)], axis=0
    )
    picked = rows[:, :LANES]
    for q in range(1, 4):
        picked = jnp.where(lows == float(q), rows[:, q * LANES : (q + 1) * LANES], picked)
    return picked.astype(BF16)


def update_kernel(
    parts, table_ref, accum_ref, one_ref, two_ref, picks_ref, rows_ref, accum_out_ref, sent_ref,
    most_ref, rows, updated, moved, sent, sems,
):
    count = rows.shape[0]
    most = jnp.maximum(one_ref[count:, :].astype(F32), two_ref[count:, :].astype(F32))
    most_ref[...] = most[:8]
    gradient = one_ref[:count, :].astype(F32) + two_ref[:count, :].astype(F32)
    history = accum_ref[...] + gradient * gradient
    updated[...] = history
    rows[...] = table_ref[...] - 0.1 * gradient * lax.rsqrt(history)
    copies = [
        pltpu.make_async_copy(rows, rows_ref, sems.at[0]),
        pltpu.make_async_copy(updated, accum_out_ref, sems.at[1]),
    ]
    for copy in copies:
        copy.start()
    moved[...] = rows[...].astype(BF16)
    wide = jnp.concatenate([moved[q * 512 : (q + 1) * 512, :] for q in range(4)], axis=1)
    shards = sent.shape[0]
    block = count // shards
    sent[:, REQ_SLOTS:, :] = moved[...].reshape(shards, block, LANES)
    group = shards // parts
    for part in range(parts):
        first = part * group
        picked = pick_rows(
            group, REQ_SLOTS, picks_ref[:, first : first + group],
            picks_ref[:, LANES // 2 + first : LANES // 2 + first + group], wide,
        )
        at = slice(first, first + group)
        sent[at, :REQ_SLOTS, :] = picked.reshape(group, REQ_SLOTS, LANES)
        copies.append(pltpu.make_async_copy(sent.at[at], sent_ref.at[at], sems.at[2 + part]))
        copies[-1].start()
    for copy in copies:
        copy.wait()


def rank_kernel(
    group, ret_ref, mrow_ref, mcol_ref, place_ref, w_ref, b_ref, score_ref, out_ref, serving_ref,
    total, wide, weights, sem,
):
    step = pl.program_id(0)
    load = pltpu.make_async_copy(w_ref, weights, sem)

    @pl.when(step == 0)
    def _():
        load.start()
        total[...] = jnp.zeros_like(total)

    turned = pltpu.roll(mcol_ref[...], lax.rem(LANES - step * group, LANES), 1)
    hots, values = [], []
    for b in range(group):
        hots.append(
            hot_rows(512, mrow_ref[pl.ds(step * group + b, 1), :])
        )
        low = jnp.broadcast_to(turned[:, b : b + 1], (LANES, LANES)).astype(I32).astype(jnp.int16)
        rows = ret_ref[b, :LANES, :]
        zero = jnp.zeros((), BF16)
        values.append(
            jnp.concatenate([jnp.where(low == jnp.int16(q), rows, zero) for q in range(2)], axis=1)
        )
    total[...] += dot(jnp.concatenate(hots, axis=1), jnp.concatenate(values, axis=0))
    wide[step] = ret_ref[:, REQ_SLOTS:, :].reshape(wide.shape[1:])

    @pl.when(step == pl.num_programs(0) - 1)
    def _():
        pooled = jnp.concatenate(
            [
                total[(f & 3) * LANES : (f & 3) * LANES + LANES, (f >> 2) * LANES : (f >> 2) * LANES + LANES]
                for f in range(8)
            ],
            axis=1,
        ).astype(BF16)
        load.wait()
        hidden = jnp.maximum(dot(pooled, weights[...]) + b_ref[...], 0.0).astype(BF16)
        out_ref[...] = dot_nt(score_ref[...], hidden)
        place = place_ref[...]
        owner, last = place >> 11, place & 31
        high = ((owner & 15) * 32 + last).astype(F32)
        zero = jnp.zeros((LANES // 2 - place.shape[0], LANES), F32)
        cols = jnp.concatenate([high, zero, (owner >> 4).astype(F32), zero], axis=0).T
        moved = jnp.concatenate([wide[q // 2, (q % 2) * 512 : (q % 2) * 512 + 512] for q in range(4)], axis=1)
        serving_ref[...] = pick_rows(
            place.shape[0], LANES, cols, cols[:, LANES // 2 :], moved
        )


def bucket_slots(targets, target_count, capacity):
    one_hot = (targets[:, None] == jnp.arange(target_count, dtype=I32)[None, :]).astype(I32)
    ranking = jnp.sum(jnp.cumsum(one_hot, axis=0) * one_hot, axis=1) - 1
    return targets * capacity + ranking


def range_scores(serving_rows, req_ids, w_hidden, b_hidden, w_score, shards, fields):
    rows_dev, width = serving_rows.shape
    requests, id_columns = req_ids.shape
    capacity = 2 * requests * id_columns // shards
    flat = req_ids.reshape(-1)
    slot = bucket_slots(flat // rows_dev, shards, capacity)
    keys = jnp.zeros((shards * capacity,), I32).at[slot].set(flat % rows_dev)
    asked = exchange(keys.reshape(shards, capacity))
    found = jnp.take(serving_rows, asked.reshape(-1), axis=0, mode="clip")
    returned = exchange(found.reshape(shards, capacity, width)).reshape(-1, width)
    rows = jnp.take(returned, slot, axis=0, mode="clip").astype(F32)
    pooled = jnp.sum(rows.reshape(requests * fields, id_columns // fields, width), axis=1)
    pooled = pooled.astype(BF16).reshape(requests, fields * width)
    hidden = jnp.dot(pooled, w_hidden, preferred_element_type=F32) + b_hidden
    return jnp.dot(jax.nn.relu(hidden).astype(BF16), w_score, preferred_element_type=F32)


def whole(shape):
    return pl.BlockSpec(shape, lambda *step: (0,) * len(shape))


def call(kernel, name, flops, moved, **kwargs):
    return pl.pallas_call(
        kernel,
        name=name,
        compiler_params=pltpu.CompilerParams(vmem_limit_bytes=VMEM_LIMIT),
        cost_estimate=pl.CostEstimate(flops=flops, bytes_accessed=moved, transcendentals=0),
        **kwargs,
    )


def in_hbm(array):
    return pltpu.with_memory_space_constraint(array, pltpu.HBM)


def exchange(rows):
    return lax.all_to_all(rows, "shard", split_axis=0, concat_axis=0, tiled=True)


def on_device(
    table_rows,
    accum,
    hash_keys,
    hash_place,
    sample_ids,
    sample_grads,
    req_ids,
    w_hidden,
    b_hidden,
    w_score,
):
    rows_dev, width = table_rows.shape
    shards = lax.axis_size("shard")
    samples, id_columns = sample_ids.shape
    requests = req_ids.shape[0]
    slots = 2 * samples * id_columns // shards
    hidden_width = w_hidden.shape[1]
    per_field = id_columns * width // sample_grads.shape[1]
    block = rows_dev // shards
    groups = 2
    sorted_rows = samples * id_columns // groups
    places = hash_place.reshape(-1, LANES)
    shape = jax.ShapeDtypeStruct
    extras = shape((shards * EXTRA, LANES), BF16)
    columns = shape((LANES, 2 * shards), F32)
    ex = pltpu.VMEM(((shards + 1) * EXTRA, LANES), F32)

    group = 16
    sent, mrow, mcol = call(
        functools.partial(send_kernel, shards, rows_dev, per_field, groups, group),
        "send",
        2**34,
        2**23,
        grid=(shards // group,),
        in_specs=[pl.BlockSpec(memory_space=pl.ANY)] * 4,
        out_specs=(
            pl.BlockSpec((group, slots + EXTRA, width), lambda g: (g, 0, 0)),
            whole((shards, LANES)),
            whole(columns.shape),
        ),
        out_shape=(
            shape((shards, slots + EXTRA, width), BF16),
            shape((shards, LANES), I32),
            columns,
        ),
        scratch_shapes=[
            pltpu.VMEM((id_columns, samples), I32),
            pltpu.VMEM(places.shape, I32),
            pltpu.VMEM((id_columns, requests), I32),
            pltpu.VMEM(sample_grads.shape, BF16),
            pltpu.VMEM((groups, LANES, 2 * sorted_rows // LANES), F32),
            pltpu.VMEM((shards, LANES), I32),
            pltpu.SMEM((shards, LANES), I32),
            pltpu.VMEM(extras.shape, BF16),
            pltpu.VMEM((groups, sorted_rows + 2 * slots, width), F32),
            pltpu.SemaphoreType.DMA((5,)),
        ]
        + index_scratch(samples, id_columns, per_field, groups, shards, places.shape[0]),
    )(*[in_hbm(array) for array in (sample_ids.T, places, req_ids.T, sample_grads)])
    got = exchange(sent)

    group = 32
    partial_sum, picks = call(
        functools.partial(sum_kernel, group),
        "gradient_sum",
        2**33,
        2**22,
        grid=(shards // group,),
        in_specs=[
            pl.BlockSpec((group, slots + EXTRA, width), lambda g: (g, 0, 0)),
            pl.BlockSpec((shards, EXTRA, width), lambda g: (0, slots // EXTRA, 0)),
        ],
        out_specs=(whole((rows_dev + 16, width)), whole(columns.shape)),
        out_shape=(shape((rows_dev + 16, width), BF16), columns),
        scratch_shapes=[
            ex,
            pltpu.VMEM((2, shards, LANES), I32),
            pltpu.VMEM((LANES, LANES), F32),
            pltpu.VMEM((512, 512), F32),
        ],
    )(got, got)
    other = lax.ppermute(partial_sum, "rep", [(0, 1), (1, 0)])

    parts = 4
    any_space = pl.BlockSpec(memory_space=pl.ANY)
    rows_type = shape((rows_dev, width), F32)
    new_rows, new_accum, sent, most = call(
        functools.partial(update_kernel, parts),
        "update",
        2**32,
        2**23,
        grid=(1,),
        in_specs=[
            whole(table_rows.shape),
            whole(accum.shape),
            whole(partial_sum.shape),
            whole(partial_sum.shape),
            whole(columns.shape),
        ],
        out_specs=(
            any_space,
            any_space,
            any_space,
            whole((8, LANES)),
        ),
        out_shape=(
            rows_type,
            rows_type,
            pltpu.HBM((shards, REQ_SLOTS + block, width), BF16),
            shape((8, LANES), F32),
        ),
        scratch_shapes=[
            pltpu.VMEM(table_rows.shape, F32),
            pltpu.VMEM(table_rows.shape, F32),
            pltpu.VMEM(table_rows.shape, BF16),
            pltpu.VMEM((shards, REQ_SLOTS + block, width), BF16),
            pltpu.SemaphoreType.DMA((2 + parts,)),
        ],
    )(table_rows, accum, partial_sum, other, picks)
    returned = exchange(sent)

    place_rows = rows_dev // LANES
    own_places = lax.dynamic_slice_in_dim(
        places, lax.axis_index("shard") * place_rows, place_rows, axis=0
    )
    group = 32
    scores, serving_rows = call(
        functools.partial(rank_kernel, group),
        "pool_rank",
        2**32,
        2**22,
        grid=(shards // group,),
        in_specs=[
            pl.BlockSpec((group, REQ_SLOTS + block, width), lambda g: (g, 0, 0)),
            whole((shards, LANES)),
            whole(columns.shape),
            whole(own_places.shape),
            pl.BlockSpec(memory_space=pl.ANY),
            whole((1, hidden_width)),
            whole((1, hidden_width)),
        ],
        out_specs=(whole((1, requests)), whole((rows_dev, width))),
        out_shape=(pltpu.HBM((1, requests), F32), shape((rows_dev, width), BF16)),
        scratch_shapes=[
            pltpu.VMEM((512, 256), F32),
            pltpu.VMEM((2, 1024, LANES), BF16),
            pltpu.VMEM(w_hidden.shape, BF16),
            pltpu.SemaphoreType.DMA,
        ],
    )(
        returned, mrow, mcol, own_places, in_hbm(w_hidden),
        b_hidden.reshape(1, -1), w_score.reshape(1, -1),
    )
    scores = lax.cond(
        most[0, 0] <= REQ_SLOTS,
        lambda: scores.reshape(requests),
        lambda: range_scores(
            serving_rows, req_ids, w_hidden, b_hidden, w_score, shards, id_columns // per_field
        ),
    )
    return (new_rows, new_accum, serving_rows, scores)


def solution(mesh):
    return jax.shard_map(
        on_device,
        mesh=mesh,
        in_specs=(
            P("shard", None),
            P("shard", None),
            P("shard"),
            P(),
            P(("rep", "shard"), None),
            P(("rep", "shard"), None),
            P(("rep", "shard"), None),
            P(),
            P(),
            P(),
        ),
        out_specs=(P("shard", None), P("shard", None), P("shard", None), P(("rep", "shard"))),
        check_vma=False,
    )
```
